512 devices in a mesh: slab: 64 (over z, y), head: 8 (over x, core).
Axes of the slice: x: 4, y: 4, z: 16, core: 2. Of those that a mesh axis runs over, the one named last changes fastest.
Arguments:
- video_token_state: bfloat16 [24576, 3072], P('slab'), may hold values from -6 to 6
- text_tokens: bfloat16 [128, 3072], replicated, may hold values from -6 to 6
- text_mask: int32 [128], replicated, may hold values from 0 to 1, as said below
- head_window: int32 [16, 2], replicated, may hold values from 0 to 1, as said below
- video_query_weight: bfloat16 [3072, 2048], P('slab', 'head'), may hold values from -0.109375 to 0.109375
- video_key_weight: bfloat16 [3072, 2048], P('slab', 'head'), may hold values from -0.109375 to 0.109375
- video_value_weight: bfloat16 [3072, 2048], P('slab', 'head'), may hold values from -0.109375 to 0.109375
- wout_video: bfloat16 [2048, 3072], P('head', 'slab'), may hold values from -0.125 to 0.125
- wquery_text: bfloat16 [3072, 2048], P('slab', 'head'), may hold values from -0.109375 to 0.109375
- wkey_text: bfloat16 [3072, 2048], P('slab', 'head'), may hold values from -0.109375 to 0.109375
- wvalue_text: bfloat16 [3072, 2048], P('slab', 'head'), may hold values from -0.109375 to 0.109375
- video_query_gain: float32 [128], replicated, may hold values from 1.25 to 2.5
- video_key_gain: float32 [128], replicated, may hold values from 1.25 to 2.5
- qgain_text: float32 [128], replicated, may hold values from 1.25 to 2.5
- kgain_text: float32 [128], replicated, may hold values from 1.25 to 2.5
Outputs:
- video_out: bfloat16 [24576, 3072], P(('slab', 'head'))
- text_attn: bfloat16 [128, 2048], P(None, 'head')
The draws below stay inside these ranges and needn't reach their ends.
Inputs may be any that keep to these rules, and one draw needn't show every extreme that they name: `text_mask`: the ones form a prefix: the first 16 text tokens are always real and the last one never is. `head_window`: each of the values 0 and 1 is taken by some head in each of the two columns.
All inputs are finite; a program needn't handle non-finite values.
Results may differ from the reference program's by a relative error of at most 0.019.
Values may be sent and summed in bfloat16 or wider, within the bound.
A program may use at most 64 MiB of HBM per device.

```python
import math
import jax
import jax.numpy as jnp
from jax import lax

D = 3072
HEAD_SIZE = 128
SHARD_HEADS = 16
COLUMN_TILES = 8
TXT = 128
TILE_TOKENS = 384
NVID = 24576
N_HEAD = 8


def draw_text_mask(key, part):
    key = jax.random.fold_in(key, 11)
    live_count = jax.random.randint(key, (), TXT // 8, TXT)
    return (jnp.arange(TXT, dtype=jnp.int32) < live_count).astype(jnp.int32)


def draw_head_window(key, part):
    key = jax.random.fold_in(key, 23)
    subkeys = jax.random.split(key, 2)
    row_reach = jax.random.permutation(subkeys[0], SHARD_HEADS) % 2
    column_reach = jax.random.permutation(subkeys[1], SHARD_HEADS) % 2
    return jnp.stack([row_reach, column_reach], axis=1).astype(jnp.int32)


def level_of(stream_key, dims, shards, smallest, largest):
    def one(axis_at, blocks):
        steps = jax.random.uniform(jax.random.fold_in(jax.random.fold_in(stream_key, 6), axis_at), (blocks,), jnp.float32, smallest / len(shards), largest / len(shards))
        return jnp.repeat(jnp.exp(steps), dims[axis_at] // blocks).reshape((-1,) + (1,) * (len(dims) - axis_at - 1))

    level = one(*shards[0])
    for cut in shards[1:]:
        level = level * one(*cut)
    return level


def scatter_about(own_key, extent, width, bound, cuts=(), held_as=jnp.bfloat16):
    entries = width * jax.random.normal(own_key, extent, jnp.float32)
    if cuts:
        entries = entries * level_of(own_key, extent, cuts, -0.22, 0.18)
    return jnp.clip(entries, -bound, bound).astype(held_as)


def setup_inputs(seed: int = 0) -> dict:
    key_list = jax.random.split(jax.random.key(seed), 16)
    video_token_state = scatter_about(key_list[0], (NVID, D), 1.0, 6.0, ((0, 64),))
    text_tokens = scatter_about(key_list[1], (TXT, D), 1.0, 6.0)
    text_mask = draw_text_mask(jax.random.fold_in(key_list[15], 71), 0)
    head_window = draw_head_window(jax.random.fold_in(key_list[15], 71), 0)
    video_query_weight = scatter_about(key_list[4], (D, SHARD_HEADS * HEAD_SIZE), D ** -0.5, 0.109375, ((0, 64), (1, 8)))
    video_key_weight = scatter_about(key_list[5], (D, SHARD_HEADS * HEAD_SIZE), D ** -0.5, 0.109375, ((0, 64), (1, 8)))
    video_value_weight = scatter_about(key_list[6], (D, SHARD_HEADS * HEAD_SIZE), D ** -0.5, 0.109375, ((0, 64), (1, 8)))
    wout_video = scatter_about(key_list[7], (SHARD_HEADS * HEAD_SIZE, D), (SHARD_HEADS * HEAD_SIZE) ** -0.5, 0.125, ((0, 8), (1, 64)))
    wquery_text = scatter_about(key_list[8], (D, SHARD_HEADS * HEAD_SIZE), D ** -0.5, 0.109375, ((0, 64), (1, 8)))
    wkey_text = scatter_about(key_list[9], (D, SHARD_HEADS * HEAD_SIZE), D ** -0.5, 0.109375, ((0, 64), (1, 8)))
    wvalue_text = scatter_about(key_list[10], (D, SHARD_HEADS * HEAD_SIZE), D ** -0.5, 0.109375, ((0, 64), (1, 8)))
    video_query_gain = jnp.clip(jnp.exp(jax.random.uniform(key_list[11], (HEAD_SIZE,), jnp.float32, math.log(1.25), math.log(2.5))), 1.25, 2.5)
    video_key_gain = jnp.clip(jnp.exp(jax.random.uniform(key_list[12], (HEAD_SIZE,), jnp.float32, math.log(1.25), math.log(2.5))), 1.25, 2.5)
    qgain_text = jnp.clip(jnp.exp(jax.random.uniform(key_list[13], (HEAD_SIZE,), jnp.float32, math.log(1.25), math.log(2.5))), 1.25, 2.5)
    kgain_text = jnp.clip(jnp.exp(jax.random.uniform(key_list[14], (HEAD_SIZE,), jnp.float32, math.log(1.25), math.log(2.5))), 1.25, 2.5)
    return dict(video_token_state=video_token_state, text_tokens=text_tokens, text_mask=text_mask, head_window=head_window, video_query_weight=video_query_weight, video_key_weight=video_key_weight, video_value_weight=video_value_weight, wout_video=wout_video, wquery_text=wquery_text, wkey_text=wkey_text, wvalue_text=wvalue_text, video_query_gain=video_query_gain, video_key_gain=video_key_gain, qgain_text=qgain_text, kgain_text=kgain_text)


norm_eps = 1e-06

def layer_normalize(token_rows):
    values = token_rows.astype(jnp.float32)
    center = values - lax.optimization_barrier(jnp.mean(values, axis=-1, keepdims=True))
    spread = lax.optimization_barrier(jnp.mean(center * center, axis=-1, keepdims=True))
    return (center * lax.rsqrt(spread + norm_eps)).astype(jnp.bfloat16)

def per_head_norm(projected, gain):
    row_count = projected.shape[0]
    per_head = projected.reshape(row_count, -1, gain.shape[0])
    mean_square = lax.optimization_barrier(jnp.mean(per_head * per_head, axis=-1, keepdims=True))
    return (per_head * lax.rsqrt(mean_square + norm_eps) * gain).reshape(row_count, -1).astype(jnp.bfloat16)

def apply_projection(normed, wquery, wkey, wvalue, qgain, kgain):
    queries = per_head_norm(jnp.dot(normed, wquery, preferred_element_type=jnp.float32), qgain)
    key_rows = per_head_norm(jnp.dot(normed, wkey, preferred_element_type=jnp.float32), kgain)
    value_rows = jnp.dot(normed, wvalue, preferred_element_type=jnp.float32).astype(jnp.bfloat16)
    return (queries, key_rows, value_rows)

def rounded(weights):
    return lax.optimization_barrier(weights.astype(jnp.bfloat16)).astype(jnp.float32)

def reference(video_token_state, text_tokens, text_mask, head_window, video_query_weight, video_key_weight, video_value_weight, wout_video, wquery_text, wkey_text, wvalue_text, video_query_gain, video_key_gain, qgain_text, kgain_text):
    score_scale = 1.0 / math.sqrt(HEAD_SIZE)
    slab_count = NVID // TILE_TOKENS
    tile_row_span = slab_count // COLUMN_TILES
    model_width = SHARD_HEADS * HEAD_SIZE
    video_query, video_keys, video_values = apply_projection(layer_normalize(video_token_state), video_query_weight, video_key_weight, video_value_weight, video_query_gain, video_key_gain)
    text_query, text_keys, text_values = apply_projection(layer_normalize(text_tokens), wquery_text, wkey_text, wvalue_text, qgain_text, kgain_text)
    text_live = text_mask > 0
    text_key_heads = text_keys.astype(jnp.float32).reshape(TXT, SHARD_HEADS, HEAD_SIZE)
    text_value_heads = text_values.astype(jnp.float32).reshape(TXT, SHARD_HEADS, HEAD_SIZE)
    tile_grid_keys = jnp.pad(video_keys.reshape(tile_row_span, COLUMN_TILES, TILE_TOKENS, model_width), ((1, 1), (1, 1), (0, 0), (0, 0)))
    grid_values = jnp.pad(video_values.reshape(tile_row_span, COLUMN_TILES, TILE_TOKENS, model_width), ((1, 1), (1, 1), (0, 0), (0, 0)))
    row_step = jnp.repeat(jnp.arange(-1, 2, dtype=jnp.int32), 3)
    col_step = jnp.tile(jnp.arange(-1, 2, dtype=jnp.int32), 3)
    reach = (jnp.abs(row_step)[None, :] <= head_window[:, 0, None]) & (jnp.abs(col_step)[None, :] <= head_window[:, 1, None])
    zero = jnp.zeros((), jnp.int32)

    def slab_attention(slab_index):
        band_row = (slab_index // COLUMN_TILES).astype(jnp.int32)
        band_col = (slab_index % COLUMN_TILES).astype(jnp.int32)
        starting_row = (slab_index * TILE_TOKENS).astype(jnp.int32)
        queries = lax.dynamic_slice_in_dim(video_query, starting_row, TILE_TOKENS, 0).astype(jnp.float32).reshape(TILE_TOKENS, SHARD_HEADS, HEAD_SIZE)
        near_keys = lax.dynamic_slice(tile_grid_keys, (band_row, band_col, zero, zero), (3, 3, TILE_TOKENS, model_width)).astype(jnp.float32).reshape(9 * TILE_TOKENS, SHARD_HEADS, HEAD_SIZE)
        near_values = lax.dynamic_slice(grid_values, (band_row, band_col, zero, zero), (3, 3, TILE_TOKENS, model_width)).astype(jnp.float32).reshape(9 * TILE_TOKENS, SHARD_HEADS, HEAD_SIZE)
        inside = (band_row + row_step >= 0) & (band_row + row_step < tile_row_span) & (band_col + col_step >= 0) & (band_col + col_step < COLUMN_TILES)
        allowed = jnp.repeat(reach & inside[None, :], TILE_TOKENS, axis=1)
        weights = jnp.where(allowed[:, None, :], jnp.exp(jnp.einsum('qhd,khd->hqk', queries, near_keys) * score_scale), 0.0)
        text_weights = jnp.where(text_live[None, None, :], jnp.exp(jnp.einsum('qhd,khd->hqk', queries, text_key_heads) * score_scale), 0.0)
        denominator = lax.optimization_barrier(jnp.sum(weights, axis=2)) + lax.optimization_barrier(jnp.sum(text_weights, axis=2))
        numerator = jnp.einsum('hqk,khd->qhd', rounded(weights), near_values) + jnp.einsum('hqk,khd->qhd', rounded(text_weights), text_value_heads)
        return (numerator / jnp.transpose(denominator)[:, :, None]).reshape(TILE_TOKENS, model_width).astype(jnp.bfloat16)
    video_attn = lax.map(slab_attention, jnp.arange(slab_count, dtype=jnp.int32)).reshape(NVID, model_width)
    text_queries = text_query.astype(jnp.float32).reshape(TXT, SHARD_HEADS, HEAD_SIZE)

    def add_slab(carry, slab_index):
        numerator, denominator = carry
        starting_row = (slab_index * TILE_TOKENS).astype(jnp.int32)
        tile_keys = lax.dynamic_slice_in_dim(video_keys, starting_row, TILE_TOKENS, 0).astype(jnp.float32).reshape(TILE_TOKENS, SHARD_HEADS, HEAD_SIZE)
        slab_values = lax.dynamic_slice_in_dim(video_values, starting_row, TILE_TOKENS, 0).astype(jnp.float32).reshape(TILE_TOKENS, SHARD_HEADS, HEAD_SIZE)
        weights = jnp.exp(jnp.einsum('qhd,khd->hqk', text_queries, tile_keys) * score_scale)
        numerator = numerator + jnp.einsum('hqk,khd->qhd', rounded(weights), slab_values)
        denominator = denominator + lax.optimization_barrier(jnp.sum(weights, axis=2))
        return ((numerator, denominator), None)
    initial = (jnp.zeros((TXT, SHARD_HEADS, HEAD_SIZE), jnp.float32), jnp.zeros((SHARD_HEADS, TXT), jnp.float32))
    (numerator, denominator), unused = lax.scan(add_slab, initial, jnp.arange(slab_count, dtype=jnp.int32))
    self_weights = jnp.where(text_live[None, None, :], jnp.exp(jnp.einsum('qhd,khd->hqk', text_queries, text_key_heads) * score_scale), 0.0)
    numerator = numerator + jnp.einsum('hqk,khd->qhd', rounded(self_weights), text_value_heads)
    denominator = denominator + lax.optimization_barrier(jnp.sum(self_weights, axis=2))
    text_attn = (numerator / jnp.transpose(denominator)[:, :, None]).reshape(TXT, model_width).astype(jnp.bfloat16)
    group_width = model_width // N_HEAD
    summed = jnp.zeros((NVID, D), jnp.float32)
    for group_index in range(N_HEAD):
        columns = video_attn[:, group_index * group_width:(group_index + 1) * group_width]
        weight_rows = wout_video[group_index * group_width:(group_index + 1) * group_width]
        summed = summed + rounded(jnp.dot(columns, weight_rows, preferred_element_type=jnp.float32))
    return (summed.astype(jnp.bfloat16), text_attn)
```

```python
import functools
import math

import jax
import jax.numpy as jnp
from jax import lax
from jax.experimental import pallas as pl
from jax.experimental.pallas import tpu as pltpu
from jax.sharding import PartitionSpec as P

HEAD_SIZE = 128
COLUMN_TILES = 8
Y = 4
MIB = 1 << 20
LANES = 128
VMEM = pltpu.VMEM
DMA = pltpu.SemaphoreType.DMA

norm_eps = 1e-06


def mod(a, n):
    return lax.rem(a, jnp.int32(n))


def remote(src, dst, send, recv, **device):
    return pltpu.make_async_remote_copy(
        src_ref=src, dst_ref=dst, send_sem=send, recv_sem=recv,
        device_id=device, device_id_type=pl.DeviceIdType.MESH,
    )


def greet(slabs=(), heads=()):
    barrier = pltpu.get_barrier_semaphore()
    for slab in slabs:
        pl.semaphore_signal(barrier, 1, device_id={"slab": slab}, device_id_type=pl.DeviceIdType.MESH)
    for head in heads:
        pl.semaphore_signal(barrier, 1, device_id={"head": head}, device_id_type=pl.DeviceIdType.MESH)
    return barrier


def when(condition, step):
    if isinstance(condition, bool):
        if condition:
            step()
    else:
        pl.when(condition)(step)


def hello_slab(z, y, nz):
    barrier = pltpu.get_barrier_semaphore()

    def greet_one(slab):
        pl.semaphore_signal(barrier, 1, device_id={"slab": slab}, device_id_type=pl.DeviceIdType.MESH)

    for d in range(1, Y):
        greet_one(z * Y + mod(y + d, Y))

    def body(d, carry):
        greet_one(mod(z + d, nz) * Y + y)
        return carry

    lax.fori_loop(1, nz, body, 0)
    return barrier, Y - 1 + nz - 1


class SlabSum:
    @staticmethod
    def scratch(block):
        owners, nz, rows, lanes = block.shape
        return [
            VMEM((Y, nz, rows, lanes), block.dtype),
            VMEM((nz, rows, lanes), block.dtype),
            VMEM((nz, rows, lanes), block.dtype),
            DMA((2, 2, Y)),
            DMA((2, 2, nz)),
        ]

    def __init__(self, part, out, scratch):
        self.part, self.out = part, out
        self.from_y, self.sum_y, self.from_z, self.ysem, self.zsem = scratch
        self.owners, self.nz = part.shape[:2]
        slab = lax.axis_index("slab")
        self.z, self.y = slab // Y, mod(slab, Y)

    def _owns(self, y):
        return True if self.owners == Y else y < self.owners

    def _y(self, d, give):
        y, to = self.y, mod(self.y + d, Y)
        src = self.out.at[y] if give else self.part.at[to]
        dst = self.out.at[y] if give else self.from_y.at[y]
        return remote(src, dst, self.ysem.at[give, 0, to], self.ysem.at[give, 1, y], slab=self.z * Y + to)

    def _y_in(self, d, give):
        of = mod(self.y + d, Y)
        dst = self.out.at[of] if give else self.from_y.at[of]
        return remote(dst, dst, self.ysem.at[give, 0, of], self.ysem.at[give, 1, of], slab=self.z * Y + of)

    def _z(self, d, give):
        z, to = self.z, mod(self.z + d, self.nz)
        src = self.out.at[self.y, z] if give else self.sum_y.at[to]
        dst = self.out.at[self.y, z] if give else self.from_z.at[z]
        return remote(src, dst, self.zsem.at[give, 0, to], self.zsem.at[give, 1, z], slab=to * Y + self.y)

    def _z_in(self, d, give):
        of = mod(self.z + d, self.nz)
        dst = self.out.at[self.y, of] if give else self.from_z.at[of]
        return remote(dst, dst, self.zsem.at[give, 0, of], self.zsem.at[give, 1, of], slab=of * Y + self.y)

    def _each_z(self, step):
        def body(d, carry):
            step(d)
            return carry

        lax.fori_loop(1, self.nz, body, 0)

    def start(self):
        for d in range(1, Y):
            when(self._owns(mod(self.y + d, Y)), lambda: self._y(d, 0).start())

    def along_z(self):
        def step():
            for d in range(1, Y):
                self._y_in(d, 0).wait_recv()
            total = self.part[self.y].astype(jnp.float32)
            for d in range(1, Y):
                total = total + self.from_y[mod(self.y + d, Y)].astype(jnp.float32)
            self.sum_y[...] = total.astype(self.sum_y.dtype)
            self._each_z(lambda d: self._z(d, 0).start())

        when(self._owns(self.y), step)

    def hand_out_z(self, finish):
        def step():
            self._each_z(lambda d: self._z_in(d, 0).wait_recv())
            total = self.sum_y[self.z].astype(jnp.float32)
            for d in range(1, self.nz):
                total = total + self.from_z[mod(self.z + d, self.nz)].astype(jnp.float32)
            self.out[self.y, self.z] = finish(total).astype(self.out.dtype)
            self._each_z(lambda d: self._z(d, 1).start())

        when(self._owns(self.y), step)

    def hand_out_y(self):
        def step():
            self._each_z(lambda d: self._z_in(d, 1).wait_recv())
            for d in range(1, Y):
                self._y(d, 1).start()

        when(self._owns(self.y), step)

    def end(self):
        for d in range(1, Y):
            when(self._owns(mod(self.y + d, Y)), lambda: self._y_in(d, 1).wait_recv())

    def settle(self):
        for d in range(1, Y):
            when(self._owns(mod(self.y + d, Y)), lambda: self._y(d, 0).wait_send())

        def mine():
            for d in range(1, Y):
                self._y(d, 1).wait_send()

            def done(d):
                self._z(d, 0).wait_send()
                self._z(d, 1).wait_send()

            self._each_z(done)

        when(self._owns(self.y), mine)


class TorusGather:
    @staticmethod
    def scratch(nz):
        return [
            DMA((2, nz, 2)), DMA((nz, 2)), DMA((3,)), DMA((3,)),
            DMA((2, nz)), DMA((nz,)), DMA((2, nz)), DMA((2, nz)), DMA((nz,)), DMA((nz,)), DMA((3,)),
            DMA((2, 2)), DMA((2, 2)), DMA((2,)), DMA((2,)),
        ]

    def __init__(self, wa, wb, ga, gb, sems):
        self.wa, self.wb, self.ga, self.gb = wa, wb, ga, gb
        (self.az_s, self.az_r, self.ay_s, self.ay_r, self.bz_s, self.bz_r,
         self.by_s, self.by_r, self.bo_s, self.bo_r, self.own_sem,
         self.ly_s, self.ly_r, self.lo_s, self.lo_r) = sems
        self.nz = nz = gb.shape[0]
        self.half = nz // 2
        slab = lax.axis_index("slab")
        self.z, self.y = z, y = slab // Y, mod(slab, Y)
        self.next = mod(z + 1, nz), mod(z + nz - 1, nz)
        self.right, self.left, self.across = mod(y + 1, Y), mod(y + Y - 1, Y), mod(y + 2, Y)
        self.sides = self.right, self.left
        self.parts = (pl.ds(0, self.half), pl.ds(self.half, self.half))
        self.sent = []

    def _go(self, copy):
        copy.start()
        self.sent.append(copy)

    def _landed(self, dst, sem):
        remote(dst, dst, self.own_sem.at[2], sem, slab=self.z * Y + self.right).wait_recv()

    def _pair(self, origin, p):
        return self.ga.at[origin, pl.ds(2 * p, 2)]

    def _a_z(self, origin, p, way):
        block = self._pair(origin, p)
        self._go(remote(block, block, self.az_s.at[way, origin, p], self.az_r.at[origin, p],
                        slab=self.next[way] * Y + self.y))

    def _b_z(self, origin, src, way):
        self._go(remote(src, self.gb.at[origin, self.y], self.bz_s.at[way, origin], self.bz_r.at[origin],
                        slab=self.next[way] * Y + self.y))

    def _two(self, origin, j):
        return self.gb.at[origin, j, pl.ds(0, 2)]

    def _b_y(self, origin, src):
        for way, to in enumerate(self.sides):
            self._go(remote(src, self._two(origin, self.y), self.by_s.at[way, origin], self.by_r.at[way, origin],
                            slab=self.z * Y + to))

    def _b_relay(self, origin):
        self._landed(self._two(origin, self.left), self.by_r.at[0, origin])
        self._landed(self._two(origin, self.right), self.by_r.at[1, origin])
        turn = 1 - 2 * mod(origin, 2)
        block = self._two(origin, mod(self.y - turn + Y, Y))
        self._go(remote(block, block, self.bo_s.at[origin], self.bo_r.at[origin],
                        slab=self.z * Y + mod(self.y + turn + Y, Y)))

    def start(self, meanwhile):
        z, y, wa, wb = self.z, self.y, self.wa, self.wb
        self._b_z(z, wb, 0)
        self._b_z(z, wb, 1)
        for i, to in enumerate((self.right, self.left, self.across)):
            self._go(remote(wa, self.ga.at[z, y], self.ay_s.at[i], self.ay_r.at[i], slab=z * Y + to))
        self.own_a = pltpu.make_async_copy(wa, self.ga.at[z, y], self.own_sem.at[0])
        self.own_a.start()
        self._b_y(z, wb.at[pl.ds(0, 2)])
        self.own_b = pltpu.make_async_copy(wb, self.gb.at[z, y], self.own_sem.at[1])
        self.own_b.start()
        meanwhile()
        odd = mod(y, 2)
        self._landed(self.ga.at[z, y + 1 - 2 * odd], self.ay_r.at[1 - odd])
        self.own_a.wait()
        self._a_z(z, y // 2, 0)
        self._a_z(z, y // 2, 1)
        self._landed(self.ga.at[z, mod(y + Y - 1 + 2 * odd, Y)], self.ay_r.at[odd])
        self._landed(self.ga.at[z, self.across], self.ay_r.at[2])
        self._a_z(z, 1 - y // 2, 0)
        self._a_z(z, 1 - y // 2, 1)

    def step(self, t):
        nz, half, y = self.nz, self.half, self.y
        ways = [(mod(self.z - t + nz, nz), 0, half)]
        if t < half:
            ways.append((mod(self.z + t, nz), 1, half - 1))
        for origin, way, last in ways:
            block = self.gb.at[origin, y]
            self._landed(block, self.bz_r.at[origin])
            if t < last:
                self._b_z(origin, block, way)
            two = self._two(origin, y)
            self._b_y(origin, two)
            if t == half:
                self._go(remote(two, two, self.bo_s.at[origin], self.bo_r.at[origin],
                                slab=self.z * Y + self.across))
        for p in (y // 2, 1 - y // 2):
            for origin, way, last in ways:
                self._landed(self._pair(origin, p), self.az_r.at[origin, p])
                if t < last:
                    self._a_z(origin, p, way)
        self._b_relay(mod(self.z - t + 1 + nz, nz))
        if t > 1:
            self._b_relay(mod(self.z + t - 1, nz))

    def across_landed(self, t):
        origins = [mod(self.z - t + self.nz, self.nz)]
        if 0 < t < self.half:
            origins.append(mod(self.z + t, self.nz))
        for origin in origins:
            if t == self.half:
                self._landed(self._two(origin, self.left), self.by_r.at[0, origin])
                self._landed(self._two(origin, self.right), self.by_r.at[1, origin])
            self._landed(self._two(origin, self.across), self.bo_r.at[origin])

    def _late(self, part, j):
        return self.gb.at[self.parts[part], j, 2]

    def late_start(self):
        for turn in range(2):
            for way in range(2):
                part = way if turn == 0 else 1 - way
                block = self._late(part, self.y)
                self._go(remote(block, block, self.ly_s.at[way, part], self.ly_r.at[way, part],
                                slab=self.z * Y + self.sides[way]))

    def late_relay(self):
        for way in range(2):
            block = self._late(way, self.sides[1 - way])
            self._landed(block, self.ly_r.at[way, way])
            self._go(remote(block, block, self.lo_s.at[way], self.lo_r.at[way], slab=self.z * Y + self.sides[way]))

    def late_end(self):
        for way in range(2):
            self._landed(self._late(1 - way, self.sides[1 - way]), self.ly_r.at[way, 1 - way])
        for way in range(2):
            self._landed(self._late(way, self.across), self.lo_r.at[way])

    def settle(self):
        for copy in self.sent:
            copy.wait_send()


def row_scale(values):
    return lax.rsqrt(jnp.mean(values * values, axis=-1, keepdims=True) + norm_eps)


OPERANDS = 15
FETCH_ORDER = (2, 3, 4, 5, 0, 1, 6, 7, 8, 9, 10, 11, 12, 13, 14)
QKV_SEMS = 15


def whole_kernel(*refs):
    f32, bf16 = jnp.float32, jnp.bfloat16

    def take(count):
        nonlocal refs
        some, refs = refs[:count], refs[count:]
        return some

    fetched = take(OPERANDS)
    out, text_final = take(2)
    held = take(OPERANDS)
    video, text, wq, wk, wv, wo, twq, twk, twv, qg, kg, tqg, tkg, mask, window = held
    (fetch_sem, wb, ga, gb, normed, tnormed, tweight, text_part, text_rows, acc) = take(10)
    (q, k, v, num, den, num_out, num_in, den_in, attn, live, tsum_part, text_out) = take(12)
    (part, pair, far, near) = take(4)
    qkv = TorusGather(wq, wb, ga, gb, take(QKV_SEMS))
    text_sum = SlabSum(text_part, text_rows, take(5))
    attn_sum = SlabSum(tsum_part, text_out, take(5))
    q_s, q_r, k_s, k_r, v_s, v_r, n_s, n_r, d_s, d_r = take(10)
    pair_s, pair_r, far_s, far_r, near_s, near_r = take(6)

    nz = gb.shape[0]
    nx = part.shape[0]
    slab, head = lax.axis_index("slab"), lax.axis_index("head")
    slab_count = lax.axis_size("slab")
    z, y = slab // Y, mod(slab, Y)
    row, column = slab // COLUMN_TILES, mod(slab, COLUMN_TILES)
    above, below = mod(slab + slab_count - COLUMN_TILES, slab_count), mod(slab + COLUMN_TILES, slab_count)
    has_left, has_right = column > 0, column < COLUMN_TILES - 1
    has_above, has_below = row > 0, row < slab_count // COLUMN_TILES - 1
    jump_left, jump_right = has_left & (y == 0), has_right & (y == Y - 1)
    x, core = head // 2, mod(head, 2)
    x_right, x_left, x_far = mod(x + 1, nx), mod(x + nx - 1, nx), mod(x + 2, nx)
    other, right, left = x * 2 + 1 - core, x_right * 2 + core, x_left * 2 + core
    depth, width = wq.shape
    heads = width // HEAD_SIZE
    tokens, model = video.shape
    txt = text.shape[0]
    score_scale = 1.0 / math.sqrt(HEAD_SIZE)
    steps = nz // 2
    nt = (((1,), (1,)), ((), ()))

    fetches = [
        pltpu.make_async_copy(src, dst, fetch_sem.at[i]) for i, (src, dst) in enumerate(zip(fetched, held))
    ]
    for i in FETCH_ORDER:
        fetches[i].start()

    barrier, peers = hello_slab(z, y, nz)
    greet((), (other, right, left))

    @pl.when(jump_left)
    def _():
        greet((slab - 1,))

    @pl.when(jump_right)
    def _():
        greet((slab + 1,))

    for i in FETCH_ORDER[:4]:
        fetches[i].wait()
    for i, weight in enumerate((wk, wv, wo)):
        wb[i] = weight[...]
    pl.semaphore_wait(barrier, peers + 3 + jump_left.astype(jnp.int32) + jump_right.astype(jnp.int32))
    def normalize_video(i, carry):
        at = pl.ds(pl.multiple_of(i * 16, 16), 16)
        values = video[at, :].astype(f32)
        center = values - jnp.mean(values, axis=-1, keepdims=True)
        normed[at, :] = (center * row_scale(center)).astype(bf16)
        return carry

    blocks = tokens // 16
    early = blocks // 4

    def first_rows():
        fetches[0].wait()
        lax.fori_loop(0, early, normalize_video, 0)

    qkv.start(first_rows)

    span = tweight.shape[0]
    aligned = jnp.minimum(slab * depth // LANES * LANES, model - span)
    aligned = pl.multiple_of(aligned, LANES)
    offset = pl.multiple_of(slab * depth - aligned, 16)
    share = nz // heads

    def fill_text_weights():
        tweight[...] = jnp.zeros_like(tweight)
        for i, weight in enumerate((twq, twk, twv)):
            tweight[pl.ds(offset, depth), i * width : (i + 1) * width] = weight[...]

    def normalize_text(i, carry):
        at = pl.ds(pl.multiple_of(i * 16, 16), 16)
        values = text[at, :].astype(f32)
        mean = jnp.mean(values, axis=-1, keepdims=True)
        scale = row_scale(values - mean)
        columns = text[at, pl.ds(aligned, span)].astype(f32)
        tnormed[at, :] = ((columns - mean) * scale).astype(bf16)
        return carry

    def multiply_text():
        for i in range(3):
            product = jnp.dot(
                tnormed[...], tweight[:, i * width : (i + 1) * width], preferred_element_type=f32
            ).astype(bf16)
            for h in range(heads):
                block = product[:, h * HEAD_SIZE : (h + 1) * HEAD_SIZE]
                text_part[i, h * share : (h + 1) * share] = block.reshape(share, txt // share, HEAD_SIZE)

    def finish_text(total):
        gain = jnp.where(y == 0, tqg[...], tkg[...])
        return jnp.where(y == 2, total, total * row_scale(total) * gain)

    for t in range(1, steps + 1):
        qkv.step(t)
        if t == 1:
            for i in FETCH_ORDER[5:]:
                fetches[i].wait()
            fill_text_weights()
            lax.fori_loop(0, txt // 32, normalize_text, 0)
        if t == 2:
            lax.fori_loop(txt // 32, txt // 16, normalize_text, 0)
            multiply_text()
            text_sum.start()
        if t == 4:
            text_sum.along_z()
        if t == 7:
            text_sum.hand_out_z(finish_text)
        rest = blocks - early
        lax.fori_loop(early + (t - 1) * rest // steps, early + t * rest // steps, normalize_video, 0)

    qkv.own_b.wait()
    qkv.late_start()

    acc[...] = jnp.zeros_like(acc)
    group = 4 if nz % 4 == 0 else nz
    span = group * Y * depth

    def multiply_query(c, carry):
        rows = normed[:, pl.ds(pl.multiple_of(c * span, span), span)]
        acc[:, :width] += jnp.dot(
            rows, ga[pl.ds(c * group, group)].reshape(span, width), preferred_element_type=f32
        )
        return carry

    lax.fori_loop(0, nz // group, multiply_query, 0)
    rows_out = []
    for h in range(heads):
        values = acc[:, h * HEAD_SIZE : (h + 1) * HEAD_SIZE]
        q[0, h] = (values * row_scale(values) * qg[...]).astype(bf16)
        to_below = remote(q.at[0, h], q.at[1, h], q_s.at[0, h], q_r.at[0, h], slab=below)
        to_above = remote(q.at[0, h], q.at[2, h], q_s.at[1, h], q_r.at[1, h], slab=above)
        to_below.start()
        to_above.start()
        rows_out.append((to_below, to_above))
    text_sum.hand_out_y()

    pair_depth = 2 * Y * depth

    def multiply_rest(i, carry):
        at = mod(z // 2 + i + nz // 2 - 2, nz // 2)
        rows = normed[:, pl.ds(pl.multiple_of(at * pair_depth, pair_depth), pair_depth)]
        for j in range(2):
            acc[:, (j + 1) * width : (j + 2) * width] += jnp.dot(
                rows, gb[pl.ds(at * 2, 2), :, j].reshape(pair_depth, width), preferred_element_type=f32
            )
        return carry

    near_steps = 5
    for t in range(near_steps + 1):
        qkv.across_landed(t)
    lax.fori_loop(0, 5, multiply_rest, 0)
    for t in range(near_steps + 1, steps + 1):
        qkv.across_landed(t)
    lax.fori_loop(5, nz // 2, multiply_rest, 0)

    to_right, to_left = [], []
    for h in range(heads):
        values = acc[:, width + h * HEAD_SIZE : width + (h + 1) * HEAD_SIZE]
        k[0, h] = (values * row_scale(values) * kg[...]).astype(bf16)
        v[0, h] = acc[:, 2 * width + h * HEAD_SIZE : 2 * width + (h + 1) * HEAD_SIZE].T.astype(bf16)
        right_now = [
            remote(k.at[0, h], k.at[1, h], k_s.at[0, h], k_r.at[0, h], slab=slab + 1),
            remote(v.at[0, h], v.at[1, h], v_s.at[0, h], v_r.at[0, h], slab=slab + 1),
        ]
        left_now = [
            remote(k.at[0, h], k.at[2, h], k_s.at[1, h], k_r.at[1, h], slab=slab - 1),
            remote(v.at[0, h], v.at[2, h], v_s.at[1, h], v_r.at[1, h], slab=slab - 1),
        ]
        to_right += right_now
        to_left += left_now

        def start_all(copies):
            for copy in copies:
                copy.start()

        pl.when(has_right)(functools.partial(start_all, right_now))
        pl.when(has_left)(functools.partial(start_all, left_now))

    @pl.when(jnp.logical_not(has_left))
    def _():
        k[1] = jnp.zeros_like(k[1])
        v[1] = jnp.zeros_like(v[1])

    @pl.when(jnp.logical_not(has_right))
    def _():
        k[2] = jnp.zeros_like(k[2])
        v[2] = jnp.zeros_like(v[2])

    def scores(keys, queries):
        return jnp.exp(lax.dot_general(keys, queries, nt, preferred_element_type=f32) * score_scale)

    def weigh(values, e):
        return jnp.dot(values, e.astype(bf16), preferred_element_type=f32)

    def column_sum(e):
        return jnp.sum(e, axis=0, keepdims=True)

    tsum_part[heads] = jnp.zeros_like(tsum_part[heads])
    for h in range(heads):
        e = scores(k[0, h], q[0, h])
        num[0, h] = weigh(v[0, h], e)
        den[0, h, 0:1] = column_sum(e)

    qkv.late_relay()

    for h in range(heads):
        for copy in rows_out[h]:
            copy.wait_recv()

        def neighbour(tile, carry, h=h):
            e = scores(k[0, h], q[tile, h])
            num[tile, h] = weigh(v[0, h], e)
            den[tile, h] = jnp.broadcast_to(column_sum(e), den.shape[2:])
            return carry

        lax.fori_loop(1, 3, neighbour, 0)
    live[...] = jnp.broadcast_to(mask[...].astype(f32), live.shape).T
    is_first = jnp.where(slab == 0, 1.0, 0.0)
    text_sum.end()

    def text_head(i, h):
        return text_rows[i, h * share : (h + 1) * share].reshape(txt, HEAD_SIZE)

    text_values = []
    for h in range(heads):
        tq = text_head(0, h)
        text_values.append(text_head(2, h).astype(f32).T.astype(bf16))
        e = scores(k[0, h], tq)
        own = scores(text_head(1, h), tq) * live[...] * is_first
        total = weigh(v[0, h], e) + weigh(text_values[h], own)
        tsum_part[h] = total.reshape(tsum_part.shape[1:])
        tsum_part[heads, 0, h : h + 1] = column_sum(e) + column_sum(own)
    attn_sum.start()

    live_wide = jnp.concatenate([live[...]] * (tokens // txt), axis=1)
    for h in range(heads):
        e = scores(text_head(1, h), q[0, h]) * live_wide
        num[0, h] += weigh(text_values[h], e)
        den[0, h, 0:1] += column_sum(e)

    text_sum.settle()
    attn_sum.along_z()

    def add_side(slot, tile, h):
        reach = jnp.where(jnp.where(slot == 1, has_left, has_right), 1.0, 0.0)
        e = scores(k[slot, h], q[tile, h])
        e = e * (reach * window[1, head * heads + h].astype(f32))
        num[tile, h] += weigh(v[slot, h], e)
        den[tile, h, 0:1] += column_sum(e)

    back = []
    for h in range(heads):

        @pl.when(has_left)
        def _():
            for sem, dst in ((k_r, k), (v_r, v)):
                remote(dst.at[1, h], dst.at[1, h], sem.at[0, h], sem.at[0, h], slab=slab - 1).wait_recv()

        @pl.when(has_right)
        def _():
            for sem, dst in ((k_r, k), (v_r, v)):
                remote(dst.at[2, h], dst.at[2, h], sem.at[1, h], sem.at[1, h], slab=slab + 1).wait_recv()

        def side(i, carry, h=h):
            add_side(1 + i % 2, 1 + i // 2, h)
            return carry

        lax.fori_loop(0, 4, side, 0)
        for tile in (1, 2):
            num_out[tile - 1, h] = num[tile, h].astype(bf16)
        now = [
            remote(num_out.at[0, h], num_in.at[1, h], n_s.at[1, h], n_r.at[1, h], slab=above),
            remote(num_out.at[1, h], num_in.at[0, h], n_s.at[0, h], n_r.at[0, h], slab=below),
            remote(den.at[1, h], den_in.at[1, h], d_s.at[1, h], d_r.at[1, h], slab=above),
            remote(den.at[2, h], den_in.at[0, h], d_s.at[0, h], d_r.at[0, h], slab=below),
        ]
        for copy in now:
            copy.start()
        back.append(now)

    def own_side(i, carry):
        add_side(1 + i % 2, 0, i // 2)
        return carry

    lax.fori_loop(0, 2 * heads, own_side, 0)
    attn_sum.hand_out_z(lambda total: total)
    for h in range(heads):
        for copy in back[h]:
            copy.wait_recv()
        total, under = num[0, h], den[0, h, 0:1]
        for side_row, exists in ((0, has_above), (1, has_below)):
            reach = jnp.where(exists, 1.0, 0.0) * window[0, head * heads + h].astype(f32)
            total = total + num_in[side_row, h].astype(f32) * reach
            under = under + den_in[side_row, h, 0:1] * reach
        attn[:, h * HEAD_SIZE : (h + 1) * HEAD_SIZE] = (total / under).T.astype(bf16)

    qkv.late_end()
    order = (x_far, x_right, x_left, x)
    rows = tokens // nx
    halves = part.shape[2]
    pairs = []

    def send_pair(xx):
        mine = attn[pl.ds(pl.multiple_of(xx * rows, 16), rows), :]
        for half in range(halves):
            weight = gb[half * nz // halves : (half + 1) * nz // halves, :, 2].reshape(model // halves, width)
            product = lax.dot_general(mine, weight, nt, preferred_element_type=f32).astype(bf16)
            for c in range(2):
                part[xx, c, half] = product[c * rows // 2 : (c + 1) * rows // 2]
        pairs.append(remote(part.at[xx, 1 - core], pair.at[xx], pair_s.at[xx], pair_r.at[xx], head=other))
        pairs[-1].start()

    def pair_sum(xx):
        remote(pair.at[xx], pair.at[xx], pair_s.at[xx], pair_r.at[xx], head=other).wait_recv()
        pair[xx] = (pair[xx].astype(f32) + part[xx, core].astype(f32)).astype(bf16)

    send_pair(x_far)
    send_pair(x_right)
    send_pair(x_left)
    pair_sum(x_far)
    fars = [
        remote(pair.at[x_far, 0], far.at[0], far_s.at[0], far_r.at[0], head=right),
        remote(pair.at[x_far, 1], far.at[1], far_s.at[1], far_r.at[1], head=left),
    ]
    for copy in fars:
        copy.start()
    pair_sum(x_right)
    pair_sum(x_left)
    nears = [
        remote(pair.at[x_right, 1], near.at[0, 1], near_s.at[0, 1], near_r.at[0, 1], head=right),
        remote(pair.at[x_left, 0], near.at[1, 0], near_s.at[1, 0], near_r.at[1, 0], head=left),
        remote(pair.at[x_right, 0], near.at[0, 0], near_s.at[0, 0], near_r.at[0, 0], head=right),
        remote(pair.at[x_left, 1], near.at[1, 1], near_s.at[1, 1], near_r.at[1, 1], head=left),
    ]
    nears[0].start()
    nears[1].start()
    send_pair(x)
    attn_sum.hand_out_y()
    pair_sum(x)
    fars[0].wait_recv()
    pair[x_right, 0] = (pair[x_right, 0].astype(f32) + far[0].astype(f32)).astype(bf16)
    nears[2].start()
    fars[1].wait_recv()
    pair[x_left, 1] = (pair[x_left, 1].astype(f32) + far[1].astype(f32)).astype(bf16)
    nears[3].start()
    qkv.settle()
    for copy in (*sum(rows_out, ()), *sum(back, []), *pairs):
        copy.wait_send()

    @pl.when(has_right)
    def _():
        for copy in to_right:
            copy.wait_send()

    @pl.when(has_left)
    def _():
        for copy in to_left:
            copy.wait_send()

    for copy in nears:
        copy.wait_recv()
    for half in range(halves):
        at = half * model // halves
        out[:, at : at + model // halves] = (
            pair[x, half].astype(f32) + near[0, half].astype(f32) + near[1, half].astype(f32)
        ).astype(bf16)

    attn_sum.end()
    for h in range(heads):
        total = text_out[h].reshape(HEAD_SIZE, txt) / text_out[heads, 0, h : h + 1]
        text_final[:, h * HEAD_SIZE : (h + 1) * HEAD_SIZE] = total.T.astype(bf16)
    attn_sum.settle()
    for copy in (*fars, *nears):
        copy.wait_send()


def run_whole(slab_count, head_count, operands):
    video, text, wq = operands[0], operands[1], operands[2]
    depth, width = wq.shape
    tokens, model = video.shape
    txt = text.shape[0]
    heads = width // HEAD_SIZE
    nz, nx = slab_count // Y, head_count // 2
    rows = tokens // head_count
    bf16, f32 = jnp.bfloat16, jnp.float32
    text_block = jax.ShapeDtypeStruct((3, nz, txt * heads // nz, HEAD_SIZE), bf16)
    sum_block = jax.ShapeDtypeStruct((heads + 1, nz, HEAD_SIZE // nz, txt), f32)
    half = model // 2
    vmem = pl.BlockSpec(memory_space=VMEM)
    return pl.pallas_call(
        whole_kernel,
        out_shape=(
            jax.ShapeDtypeStruct((rows, model), bf16),
            jax.ShapeDtypeStruct((txt, width), bf16),
        ),
        in_specs=[pl.BlockSpec(memory_space=pltpu.HBM)] * OPERANDS,
        out_specs=(vmem, vmem),
        scratch_shapes=[
            *(VMEM(a.shape, a.dtype) for a in operands[:-1]),
            pltpu.SMEM(operands[-1].shape, operands[-1].dtype),
            DMA((OPERANDS,)),
            VMEM((3, depth, width), bf16),
            VMEM((nz, Y, depth, width), bf16),
            VMEM((nz, Y, 3, depth, width), bf16),
            VMEM((tokens, model), bf16),
            VMEM((txt, 2 * LANES), bf16),
            VMEM((2 * LANES, 3 * width), bf16),
            VMEM(text_block.shape, bf16),
            VMEM(text_block.shape, bf16),
            VMEM((tokens, 3 * width), f32),
            VMEM((3, heads, tokens, HEAD_SIZE), bf16),
            VMEM((3, heads, tokens, HEAD_SIZE), bf16),
            VMEM((3, heads, HEAD_SIZE, tokens), bf16),
            VMEM((3, heads, HEAD_SIZE, tokens), f32),
            VMEM((3, heads, 8, tokens), f32),
            VMEM((2, heads, HEAD_SIZE, tokens), bf16),
            VMEM((2, heads, HEAD_SIZE, tokens), bf16),
            VMEM((2, heads, 8, tokens), f32),
            VMEM((tokens, width), bf16),
            VMEM((txt, txt), f32),
            VMEM(sum_block.shape, f32),
            VMEM(sum_block.shape, f32),
            VMEM((nx, 2, 2, rows, half), bf16),
            VMEM((nx, 2, rows, half), bf16),
            VMEM((2, rows, half), bf16),
            VMEM((2, 2, rows, half), bf16),
            *TorusGather.scratch(nz),
            *SlabSum.scratch(text_block),
            *SlabSum.scratch(sum_block),
            *[DMA((2, heads))] * 10,
            DMA((nx,)), DMA((nx,)), DMA((2,)), DMA((2,)), DMA((2, 2)), DMA((2, 2)),
        ],
        compiler_params=pltpu.CompilerParams(
            collective_id=0, has_side_effects=True, vmem_limit_bytes=32 * MIB
        ),
        name="whole",
    )(*(pltpu.with_memory_space_constraint(a, pltpu.HBM) for a in operands))


def on_device(
    video_token_state,
    text_tokens,
    text_mask,
    head_window,
    video_query_weight,
    video_key_weight,
    video_value_weight,
    wout_video,
    wquery_text,
    wkey_text,
    wvalue_text,
    video_query_gain,
    video_key_gain,
    qgain_text,
    kgain_text,
):
    operands = (
        video_token_state, text_tokens,
        video_query_weight, video_key_weight, video_value_weight, wout_video.T,
        wquery_text, wkey_text, wvalue_text,
        *(row.reshape(1, -1) for row in (video_query_gain, video_key_gain, qgain_text, kgain_text, text_mask)),
        head_window.T,
    )
    return run_whole(lax.axis_size("slab"), lax.axis_size("head"), operands)


def solution(mesh):
    return jax.shard_map(
        on_device,
        mesh=mesh,
        in_specs=(
            P("slab", None),
            P(),
            P(),
            P(),
            P("slab", "head"),
            P("slab", "head"),
            P("slab", "head"),
            P("head", "slab"),
            P("slab", "head"),
            P("slab", "head"),
            P("slab", "head"),
            P(),
            P(),
            P(),
            P(),
        ),
        out_specs=(P(("slab", "head"), None), P(None, "head")),
        check_vma=False,
    )
```

```python
import functools
import math

import jax
import jax.numpy as jnp
from jax import lax
from jax.experimental import pallas as pl
from jax.experimental.pallas import tpu as pltpu
from jax.sharding import PartitionSpec as P

HEAD_SIZE = 128
COLUMN_TILES = 8
Y = 4
NB = 4
MIB = 1 << 20
LANES = 128
VMEM = pltpu.VMEM
DMA = pltpu.SemaphoreType.DMA

norm_eps = 1e-06


def mod(a, n):
    return lax.rem(a, jnp.int32(n))


def remote(src, dst, send, recv, **device):
    return pltpu.make_async_remote_copy(
        src_ref=src, dst_ref=dst, send_sem=send, recv_sem=recv,
        device_id=device, device_id_type=pl.DeviceIdType.MESH,
    )


def greet(slabs=(), heads=()):
    barrier = pltpu.get_barrier_semaphore()
    for slab in slabs:
        pl.semaphore_signal(barrier, 1, device_id={"slab": slab}, device_id_type=pl.DeviceIdType.MESH)
    for head in heads:
        pl.semaphore_signal(barrier, 1, device_id={"head": head}, device_id_type=pl.DeviceIdType.MESH)
    return barrier


def hello_slab(z, y, nz):
    barrier = pltpu.get_barrier_semaphore()

    def greet_one(slab):
        pl.semaphore_signal(barrier, 1, device_id={"slab": slab}, device_id_type=pl.DeviceIdType.MESH)

    for d in range(1, Y):
        greet_one(z * Y + mod(y + d, Y))

    def body(d, carry):
        greet_one(mod(z + d, nz) * Y + y)
        return carry

    lax.fori_loop(1, nz, body, 0)
    return barrier, Y - 1 + nz - 1


class SlabSum:
    @staticmethod
    def scratch(block):
        owners, na, nb, rows, lanes = block.shape
        return [
            VMEM((Y, na, nb, rows, lanes), block.dtype),
            VMEM((na, nb, rows, lanes), block.dtype),
            VMEM((nb, na, rows, lanes), block.dtype),
            VMEM((na, rows, lanes), block.dtype),
            VMEM((na, rows, lanes), block.dtype),
            DMA((2, 2, Y)),
            DMA((2, 2, nb)),
            DMA((2, 2, na)),
        ]

    def __init__(self, part, out, scratch):
        self.part, self.out = part, out
        (self.from_y, self.sum_y, self.from_b, self.sum_b, self.from_a, self.ysem, self.bsem, self.asem) = scratch
        self.owners, self.na, self.nb = part.shape[:3]
        slab = lax.axis_index("slab")
        self.z, self.y = slab // Y, mod(slab, Y)
        self.a, self.b = self.z // self.nb, mod(self.z, self.nb)

    def _owns(self, y):
        return y < self.owners

    def _slab(self, a, b, y):
        return (a * self.nb + b) * Y + y

    def _y(self, d, give):
        y, to = self.y, mod(self.y + d, Y)
        src = self.out.at[y] if give else self.part.at[to]
        dst = self.out.at[y] if give else self.from_y.at[y]
        return remote(src, dst, self.ysem.at[give, 0, to], self.ysem.at[give, 1, y], slab=self.z * Y + to)

    def _y_in(self, d, give):
        of = mod(self.y + d, Y)
        dst = self.out.at[of] if give else self.from_y.at[of]
        return remote(dst, dst, self.ysem.at[give, 0, of], self.ysem.at[give, 1, of], slab=self.z * Y + of)

    def _b(self, d, give, coming=False):
        b, other = self.b, mod(self.b + d, self.nb)
        sent, kept = (other, b) if coming else (b, other)
        src = self.out.at[self.y, :, sent] if give else self.sum_y.at[:, kept]
        dst = self.out.at[self.y, :, sent] if give else self.from_b.at[sent]
        if coming:
            src = dst
        return remote(src, dst, self.bsem.at[give, 0, other], self.bsem.at[give, 1, sent],
                      slab=self._slab(self.a, other, self.y))

    def _a(self, d, give, coming=False):
        a, other = self.a, mod(self.a + d, self.na)
        sent = other if coming else a
        src = self.out.at[self.y, sent, self.b] if give else self.sum_b.at[other]
        dst = self.out.at[self.y, sent, self.b] if give else self.from_a.at[sent]
        if coming:
            src = dst
        return remote(src, dst, self.asem.at[give, 0, other], self.asem.at[give, 1, sent],
                      slab=self._slab(other, self.b, self.y))

    def start(self):
        for d in range(1, Y):
            pl.when(self._owns(mod(self.y + d, Y)))(lambda d=d: self._y(d, 0).start())

    def along_b(self):
        @pl.when(self._owns(self.y))
        def _():
            total = self.part[self.y].astype(jnp.float32)
            for d in range(1, Y):
                self._y_in(d, 0).wait_recv()
                total = total + self.from_y[mod(self.y + d, Y)].astype(jnp.float32)
            self.sum_y[...] = total.astype(self.sum_y.dtype)
            for d in range(1, self.nb):
                self._b(d, 0).start()

    def along_a(self):
        @pl.when(self._owns(self.y))
        def _():
            total = self.sum_y[:, self.b].astype(jnp.float32)
            for d in range(1, self.nb):
                self._b(d, 0, True).wait_recv()
                total = total + self.from_b[mod(self.b + d, self.nb)].astype(jnp.float32)
            self.sum_b[...] = total.astype(self.sum_b.dtype)
            for d in range(1, self.na):
                self._a(d, 0).start()

    def hand_out_a(self, finish):
        @pl.when(self._owns(self.y))
        def _():
            total = self.sum_b[self.a].astype(jnp.float32)
            for d in range(1, self.na):
                self._a(d, 0, True).wait_recv()
                total = total + self.from_a[mod(self.a + d, self.na)].astype(jnp.float32)
            self.out[self.y, self.a, self.b] = finish(total).astype(self.out.dtype)
            for d in range(1, self.na):
                self._a(d, 1).start()

    def hand_out_b(self):
        @pl.when(self._owns(self.y))
        def _():
            for d in range(1, self.na):
                self._a(d, 1, True).wait_recv()
            for d in range(1, self.nb):
                self._b(d, 1).start()

    def hand_out_y(self):
        @pl.when(self._owns(self.y))
        def _():
            for d in range(1, self.nb):
                self._b(d, 1, True).wait_recv()
            for d in range(1, Y):
                self._y(d, 1).start()

    def end(self):
        for d in range(1, Y):
            pl.when(self._owns(mod(self.y + d, Y)))(lambda d=d: self._y_in(d, 1).wait_recv())

    def settle(self):
        for d in range(1, Y):
            pl.when(self._owns(mod(self.y + d, Y)))(lambda d=d: self._y(d, 0).wait_send())

        @pl.when(self._owns(self.y))
        def _():
            for d in range(1, Y):
                self._y(d, 1).wait_send()
            for give in range(2):
                for d in range(1, self.nb):
                    self._b(d, give).wait_send()
                for d in range(1, self.na):
                    self._a(d, give).wait_send()


class TorusGather:
    NEAR = 5

    @staticmethod
    def scratch(nz):
        return [
            DMA((1,)), DMA((nz, 2)), DMA((3,)), DMA((3,)),
            DMA((1,)), DMA((nz,)), DMA((1,)), DMA((2, nz)), DMA((1,)), DMA((2,)), DMA((3,)),
            DMA((2, 2)), DMA((2, 2)), DMA((2,)), DMA((2,)),
        ]

    def __init__(self, wa, wb, ga, gb, sems):
        self.wa, self.wb, self.ga, self.gb = wa, wb, ga, gb
        (self.az_s, self.az_r, self.ay_s, self.ay_r, self.bz_s, self.bz_r,
         self.by_s, self.by_r, self.bo_s, self.bo_r, self.own_sem,
         self.ly_s, self.ly_r, self.lo_s, self.lo_r) = sems
        self.nz = nz = gb.shape[0]
        self.half = nz // 2
        slab = lax.axis_index("slab")
        self.z, self.y = z, y = slab // Y, mod(slab, Y)
        self.next = mod(z + 1, nz), mod(z + nz - 1, nz)
        self.right, self.left, self.across = mod(y + 1, Y), mod(y + Y - 1, Y), mod(y + 2, Y)
        self.sides = self.right, self.left
        self.parts = (pl.ds(0, self.half), pl.ds(self.half, self.half))
        self.sent = []

    def _go(self, copy):
        copy.start()
        self.sent.append(copy)

    def _landed(self, dst, sem):
        remote(dst, dst, self.own_sem.at[2], sem, slab=self.z * Y + self.right).wait_recv()

    def _pair(self, origin, p):
        return self.ga.at[origin, pl.ds(2 * p, 2)]

    def _a_z(self, origin, p, way):
        block = self._pair(origin, p)
        remote(block, block, self.az_s.at[0], self.az_r.at[origin, p],
               slab=self.next[way] * Y + self.y).start()

    def _b_z(self, origin, src, way):
        remote(src, self.gb.at[origin, self.y], self.bz_s.at[0], self.bz_r.at[origin],
               slab=self.next[way] * Y + self.y).start()

    def _two(self, origin, j):
        return self.gb.at[origin, j, pl.ds(0, 2)]

    def _b_y(self, origin, src):
        for way, to in enumerate(self.sides):
            remote(src, self._two(origin, self.y), self.by_s.at[0], self.by_r.at[way, origin],
                   slab=self.z * Y + to).start()

    def _b_relay(self, origin, t):
        self._landed(self._two(origin, self.left), self.by_r.at[0, origin])
        self._landed(self._two(origin, self.right), self.by_r.at[1, origin])
        turn = 1 - 2 * mod(origin, 2)
        block = self._two(origin, mod(self.y - turn + Y, Y))
        remote(block, block, self.bo_s.at[0], self.bo_r.at[int(t > self.NEAR)],
               slab=self.z * Y + mod(self.y + turn + Y, Y)).start()

    def start(self, meanwhile):
        z, y, wa, wb = self.z, self.y, self.wa, self.wb
        self._b_z(z, wb, 0)
        self._b_z(z, wb, 1)
        for i, to in enumerate((self.right, self.left, self.across)):
            self._go(remote(wa, self.ga.at[z, y], self.ay_s.at[i], self.ay_r.at[i], slab=z * Y + to))
        self.own_a = pltpu.make_async_copy(wa, self.ga.at[z, y], self.own_sem.at[0])
        self.own_a.start()
        self._b_y(z, wb.at[pl.ds(0, 2)])
        self.own_b = pltpu.make_async_copy(wb, self.gb.at[z, y], self.own_sem.at[1])
        self.own_b.start()
        meanwhile()
        odd = mod(y, 2)
        self._landed(self.ga.at[z, y + 1 - 2 * odd], self.ay_r.at[1 - odd])
        self.own_a.wait()
        self._a_z(z, y // 2, 0)
        self._a_z(z, y // 2, 1)
        self._landed(self.ga.at[z, mod(y + Y - 1 + 2 * odd, Y)], self.ay_r.at[odd])
        self._landed(self.ga.at[z, self.across], self.ay_r.at[2])
        self._a_z(z, 1 - y // 2, 0)
        self._a_z(z, 1 - y // 2, 1)

    def step(self, t):
        nz, half, y = self.nz, self.half, self.y
        ways = [(mod(self.z - t + nz, nz), 0, half)]
        if t < half:
            ways.append((mod(self.z + t, nz), 1, half - 1))
        for origin, way, last in ways:
            block = self.gb.at[origin, y]
            self._landed(block, self.bz_r.at[origin])
            if t < last:
                self._b_z(origin, block, way)
            two = self._two(origin, y)
            self._b_y(origin, two)
            if t == half:
                remote(two, two, self.bo_s.at[0], self.bo_r.at[1],
                       slab=self.z * Y + self.across).start()
        for p in (y // 2, 1 - y // 2):
            for origin, way, last in ways:
                self._landed(self._pair(origin, p), self.az_r.at[origin, p])
                if t < last:
                    self._a_z(origin, p, way)
        self._b_relay(mod(self.z - t + 1 + nz, nz), t - 1)
        if t > 1:
            self._b_relay(mod(self.z + t - 1, nz), t - 1)

    def near_landed(self):
        self._landed(self.gb.at[pl.ds(0, 2 * self.NEAR + 1), 0, pl.ds(0, 2)], self.bo_r.at[0])

    def far_landed(self):
        last = mod(self.z + self.half, self.nz)
        self._landed(self._two(last, self.left), self.by_r.at[0, last])
        self._landed(self._two(last, self.right), self.by_r.at[1, last])
        self._landed(self.gb.at[pl.ds(0, self.nz - 2 * self.NEAR - 1), 0, pl.ds(0, 2)], self.bo_r.at[1])

    def _late(self, part, j):
        return self.gb.at[self.parts[part], j, 2]

    def late_start(self):
        for turn in range(2):
            for way in range(2):
                part = way if turn == 0 else 1 - way
                block = self._late(part, self.y)
                self._go(remote(block, block, self.ly_s.at[way, part], self.ly_r.at[way, part],
                                slab=self.z * Y + self.sides[way]))

    def late_relay(self):
        for way in range(2):
            block = self._late(way, self.sides[1 - way])
            self._landed(block, self.ly_r.at[way, way])
            self._go(remote(block, block, self.lo_s.at[way], self.lo_r.at[way], slab=self.z * Y + self.sides[way]))

    def late_end(self):
        for way in range(2):
            self._landed(self._late(1 - way, self.sides[1 - way]), self.ly_r.at[way, 1 - way])
        for way in range(2):
            self._landed(self._late(way, self.across), self.lo_r.at[way])

    def settle(self):
        nz, one, two = self.nz, pl.ds(0, 1), pl.ds(0, 2)
        for block, sem in (
            (self.ga.at[pl.ds(0, nz - 1)], self.az_s),
            (self.gb.at[pl.ds(0, nz - 1), one], self.bz_s),
            (self.gb.at[:, two, two], self.by_s),
            (self.gb.at[:, one, two], self.bo_s),
        ):
            remote(block, block, sem.at[0], self.own_sem.at[2], slab=self.z * Y + self.right).wait_send()
        for copy in self.sent:
            copy.wait_send()


def row_scale(values):
    return lax.rsqrt(jnp.mean(values * values, axis=-1, keepdims=True) + norm_eps)


OPERANDS = 15
FETCH_ORDER = (2, 3, 4, 5, 0, 1, 6, 7, 8, 9, 10, 11, 12, 13, 14)
QKV_SEMS = 15


def whole_kernel(*refs):
    f32, bf16 = jnp.float32, jnp.bfloat16

    def take(count):
        nonlocal refs
        some, refs = refs[:count], refs[count:]
        return some

    fetched = take(OPERANDS)
    out, text_final = take(2)
    held = take(OPERANDS)
    video, text, wq, wk, wv, wo, twq, twk, twv, qg, kg, tqg, tkg, mask, window = held
    (fetch_sem, wb, ga, gb, normed, tnormed, tweight, text_part, text_rows, acc) = take(10)
    (q, k, v, num, den, num_out, num_in, den_in, attn, live, tsum_part, text_out) = take(12)
    (part, pair, far, near) = take(4)
    qkv = TorusGather(wq, wb, ga, gb, take(QKV_SEMS))
    text_sum = SlabSum(text_part, text_rows, take(8))
    attn_sum = SlabSum(tsum_part, text_out, take(8))
    q_s, q_r, k_s, k_r, v_s, v_r, n_s, n_r, d_s, d_r = take(10)
    pair_s, pair_r, far_s, far_r, near_s, near_r = take(6)

    nz = gb.shape[0]
    nx = part.shape[0]
    slab, head = lax.axis_index("slab"), lax.axis_index("head")
    slab_count = lax.axis_size("slab")
    z, y = slab // Y, mod(slab, Y)
    row, column = slab // COLUMN_TILES, mod(slab, COLUMN_TILES)
    above, below = mod(slab + slab_count - COLUMN_TILES, slab_count), mod(slab + COLUMN_TILES, slab_count)
    has_left, has_right = column > 0, column < COLUMN_TILES - 1
    has_above, has_below = row > 0, row < slab_count // COLUMN_TILES - 1
    jump_left, jump_right = has_left & (y == 0), has_right & (y == Y - 1)
    x, core = head // 2, mod(head, 2)
    x_right, x_left, x_far = mod(x + 1, nx), mod(x + nx - 1, nx), mod(x + 2, nx)
    other, right, left = x * 2 + 1 - core, x_right * 2 + core, x_left * 2 + core
    depth, width = wq.shape
    heads = width // HEAD_SIZE
    tokens, model = video.shape
    txt = text.shape[0]
    score_scale = 1.0 / math.sqrt(HEAD_SIZE)
    steps = nz // 2
    nt = (((1,), (1,)), ((), ()))

    fetches = [
        pltpu.make_async_copy(src, dst, fetch_sem.at[i]) for i, (src, dst) in enumerate(zip(fetched, held))
    ]
    for i in FETCH_ORDER:
        fetches[i].start()

    barrier, peers = hello_slab(z, y, nz)
    greet((), (other, right, left))

    @pl.when(jump_left)
    def _():
        greet((slab - 1,))

    @pl.when(jump_right)
    def _():
        greet((slab + 1,))

    for i in FETCH_ORDER[:4]:
        fetches[i].wait()
    for i, weight in enumerate((wk, wv, wo)):
        wb[i] = weight[...]
    pl.semaphore_wait(barrier, peers + 3 + jump_left.astype(jnp.int32) + jump_right.astype(jnp.int32))
    def normalize_video(i, carry):
        at = pl.ds(pl.multiple_of(i * 16, 16), 16)
        values = video[at, :].astype(f32)
        center = values - jnp.mean(values, axis=-1, keepdims=True)
        normed[at, :] = (center * row_scale(center)).astype(bf16)
        return carry

    blocks = tokens // 16
    early = blocks // 4

    def first_rows():
        fetches[0].wait()
        lax.fori_loop(0, early, normalize_video, 0)

    qkv.start(first_rows)

    span = tweight.shape[0]
    aligned = jnp.minimum(slab * depth // LANES * LANES, model - span)
    aligned = pl.multiple_of(aligned, LANES)
    offset = pl.multiple_of(slab * depth - aligned, 16)
    na = text_part.shape[1] // heads

    def fill_text_weights():
        tweight[...] = jnp.zeros_like(tweight)
        for i, weight in enumerate((twq, twk, twv)):
            tweight[pl.ds(offset, depth), i * width : (i + 1) * width] = weight[...]

    def normalize_text(i, carry):
        at = pl.ds(pl.multiple_of(i * 16, 16), 16)
        values = text[at, :].astype(f32)
        mean = jnp.mean(values, axis=-1, keepdims=True)
        scale = row_scale(values - mean)
        columns = text[at, pl.ds(aligned, span)].astype(f32)
        tnormed[at, :] = ((columns - mean) * scale).astype(bf16)
        return carry

    def multiply_text():
        for i in range(3):
            product = jnp.dot(
                tnormed[...], tweight[:, i * width : (i + 1) * width], preferred_element_type=f32
            ).astype(bf16)
            for h in range(heads):
                block = product[:, h * HEAD_SIZE : (h + 1) * HEAD_SIZE]
                text_part[i, h * na : (h + 1) * na] = block.reshape(na, *text_part.shape[2:])

    def finish_text(total):
        gain = jnp.where(y == 0, tqg[...], tkg[...])
        return jnp.where(y == 2, total, total * row_scale(total) * gain)

    for t in range(1, steps + 1):
        qkv.step(t)
        if t == 1:
            for i in FETCH_ORDER[5:]:
                fetches[i].wait()
            fill_text_weights()
            lax.fori_loop(0, txt // 32, normalize_text, 0)
        if t == 2:
            lax.fori_loop(txt // 32, txt // 16, normalize_text, 0)
            multiply_text()
            text_sum.start()
        if t == 3:
            text_sum.along_b()
        if t == 4:
            text_sum.along_a()
        if t == 6:
            text_sum.hand_out_a(finish_text)
        if t == 7:
            text_sum.hand_out_b()
        rest = blocks - early
        lax.fori_loop(early + (t - 1) * rest // steps, early + t * rest // steps, normalize_video, 0)

    qkv.own_b.wait()
    qkv.late_start()

    acc[...] = jnp.zeros_like(acc)
    group = 4 if nz % 4 == 0 else nz
    span = group * Y * depth

    def multiply_query(c, carry):
        rows = normed[:, pl.ds(pl.multiple_of(c * span, span), span)]
        acc[:, :width] += jnp.dot(
            rows, ga[pl.ds(c * group, group)].reshape(span, width), preferred_element_type=f32
        )
        return carry

    lax.fori_loop(0, nz // group, multiply_query, 0)
    rows_out = []
    for h in range(heads):
        values = acc[:, h * HEAD_SIZE : (h + 1) * HEAD_SIZE]
        q[0, h] = (values * row_scale(values) * qg[...]).astype(bf16)
        to_below = remote(q.at[0, h], q.at[1, h], q_s.at[0, h], q_r.at[0, h], slab=below)
        to_above = remote(q.at[0, h], q.at[2, h], q_s.at[1, h], q_r.at[1, h], slab=above)
        to_below.start()
        to_above.start()
        rows_out.append((to_below, to_above))
    text_sum.hand_out_y()

    pair_depth = 2 * Y * depth

    def multiply_rest(i, carry):
        at = mod(z // 2 + i + nz // 2 - 2, nz // 2)
        rows = normed[:, pl.ds(pl.multiple_of(at * pair_depth, pair_depth), pair_depth)]
        for j in range(2):
            acc[:, (j + 1) * width : (j + 2) * width] += jnp.dot(
                rows, gb[pl.ds(at * 2, 2), :, j].reshape(pair_depth, width), preferred_element_type=f32
            )
        return carry

    qkv.near_landed()
    lax.fori_loop(0, 5, multiply_rest, 0)
    qkv.far_landed()
    lax.fori_loop(5, nz // 2, multiply_rest, 0)

    to_right, to_left = [], []
    for h in range(heads):
        values = acc[:, width + h * HEAD_SIZE : width + (h + 1) * HEAD_SIZE]
        k[0, h] = (values * row_scale(values) * kg[...]).astype(bf16)
        v[0, h] = acc[:, 2 * width + h * HEAD_SIZE : 2 * width + (h + 1) * HEAD_SIZE].T.astype(bf16)
        right_now = [
            remote(k.at[0, h], k.at[1, h], k_s.at[0, h], k_r.at[0, h], slab=slab + 1),
            remote(v.at[0, h], v.at[1, h], v_s.at[0, h], v_r.at[0, h], slab=slab + 1),
        ]
        left_now = [
            remote(k.at[0, h], k.at[2, h], k_s.at[1, h], k_r.at[1, h], slab=slab - 1),
            remote(v.at[0, h], v.at[2, h], v_s.at[1, h], v_r.at[1, h], slab=slab - 1),
        ]
        to_right += right_now
        to_left += left_now

        def start_all(copies):
            for copy in copies:
                copy.start()

        pl.when(has_right)(functools.partial(start_all, right_now))
        pl.when(has_left)(functools.partial(start_all, left_now))

    @pl.when(jnp.logical_not(has_left))
    def _():
        k[1] = jnp.zeros_like(k[1])
        v[1] = jnp.zeros_like(v[1])

    @pl.when(jnp.logical_not(has_right))
    def _():
        k[2] = jnp.zeros_like(k[2])
        v[2] = jnp.zeros_like(v[2])

    def scores(keys, queries):
        return jnp.exp(lax.dot_general(keys, queries, nt, preferred_element_type=f32) * score_scale)

    def weigh(values, e):
        return jnp.dot(values, e.astype(bf16), preferred_element_type=f32)

    def column_sum(e):
        return jnp.sum(e, axis=0, keepdims=True)

    tsum_part[heads] = jnp.zeros_like(tsum_part[heads])
    for h in range(heads):
        e = scores(k[0, h], q[0, h])
        num[0, h] = weigh(v[0, h], e)
        den[0, h, 0:1] = column_sum(e)

    qkv.late_relay()

    for h in range(heads):
        for copy in rows_out[h]:
            copy.wait_recv()

        def neighbour(tile, carry, h=h):
            e = scores(k[0, h], q[tile, h])
            num[tile, h] = weigh(v[0, h], e)
            den[tile, h] = jnp.broadcast_to(column_sum(e), den.shape[2:])
            return carry

        lax.fori_loop(1, 3, neighbour, 0)
    live[...] = jnp.broadcast_to(mask[...].astype(f32), live.shape).T
    is_first = jnp.where(slab == 0, 1.0, 0.0)
    text_sum.end()

    def text_head(i, h):
        return text_rows[i, h * na : (h + 1) * na].reshape(txt, HEAD_SIZE)

    text_values = []
    for h in range(heads):
        tq = text_head(0, h)
        text_values.append(text_head(2, h).astype(f32).T.astype(bf16))
        e = scores(k[0, h], tq)
        own = scores(text_head(1, h), tq) * live[...] * is_first
        total = weigh(v[0, h], e) + weigh(text_values[h], own)
        tsum_part[h] = total.reshape(tsum_part.shape[1:])
        tsum_part[heads, 0, 0, h : h + 1] = column_sum(e) + column_sum(own)
    attn_sum.start()

    live_wide = jnp.concatenate([live[...]] * (tokens // txt), axis=1)
    for h in range(heads):
        e = scores(text_head(1, h), q[0, h]) * live_wide
        num[0, h] += weigh(text_values[h], e)
        den[0, h, 0:1] += column_sum(e)

    text_sum.settle()
    attn_sum.along_b()

    def add_side(slot, tile, h):
        reach = jnp.where(jnp.where(slot == 1, has_left, has_right), 1.0, 0.0)
        e = scores(k[slot, h], q[tile, h])
        e = e * (reach * window[1, head * heads + h].astype(f32))
        num[tile, h] += weigh(v[slot, h], e)
        den[tile, h, 0:1] += column_sum(e)

    back = []
    for h in range(heads):

        @pl.when(has_left)
        def _():
            for sem, dst in ((k_r, k), (v_r, v)):
                remote(dst.at[1, h], dst.at[1, h], sem.at[0, h], sem.at[0, h], slab=slab - 1).wait_recv()

        @pl.when(has_right)
        def _():
            for sem, dst in ((k_r, k), (v_r, v)):
                remote(dst.at[2, h], dst.at[2, h], sem.at[1, h], sem.at[1, h], slab=slab + 1).wait_recv()

        def side(i, carry, h=h):
            add_side(1 + i % 2, 1 + i // 2, h)
            return carry

        lax.fori_loop(0, 4, side, 0)
        for tile in (1, 2):
            num_out[tile - 1, h] = num[tile, h].astype(bf16)
        now = [
            remote(num_out.at[0, h], num_in.at[1, h], n_s.at[1, h], n_r.at[1, h], slab=above),
            remote(num_out.at[1, h], num_in.at[0, h], n_s.at[0, h], n_r.at[0, h], slab=below),
            remote(den.at[1, h], den_in.at[1, h], d_s.at[1, h], d_r.at[1, h], slab=above),
            remote(den.at[2, h], den_in.at[0, h], d_s.at[0, h], d_r.at[0, h], slab=below),
        ]
        for copy in now:
            copy.start()
        back.append(now)
        if h == 0:
            attn_sum.along_a()
        if h == heads - 1:
            attn_sum.hand_out_a(lambda total: total)

    def own_side(i, carry):
        add_side(1 + i % 2, 0, i // 2)
        return carry

    lax.fori_loop(0, 2 * heads, own_side, 0)
    attn_sum.hand_out_b()
    for h in range(heads):
        for copy in back[h]:
            copy.wait_recv()
        total, under = num[0, h], den[0, h, 0:1]
        for side_row, exists in ((0, has_above), (1, has_below)):
            reach = jnp.where(exists, 1.0, 0.0) * window[0, head * heads + h].astype(f32)
            total = total + num_in[side_row, h].astype(f32) * reach
            under = under + den_in[side_row, h, 0:1] * reach
        attn[:, h * HEAD_SIZE : (h + 1) * HEAD_SIZE] = (total / under).T.astype(bf16)

    qkv.late_end()
    order = (x_far, x_right, x_left, x)
    rows = tokens // nx
    halves = part.shape[2]
    pairs = []

    def send_pair(xx):
        mine = attn[pl.ds(pl.multiple_of(xx * rows, 16), rows), :]
        for half in range(halves):
            weight = gb[half * nz // halves : (half + 1) * nz // halves, :, 2].reshape(model // halves, width)
            product = lax.dot_general(mine, weight, nt, preferred_element_type=f32).astype(bf16)
            for c in range(2):
                part[xx, c, half] = product[c * rows // 2 : (c + 1) * rows // 2]
        pairs.append(remote(part.at[xx, 1 - core], pair.at[xx], pair_s.at[xx], pair_r.at[xx], head=other))
        pairs[-1].start()

    def pair_sum(xx):
        remote(pair.at[xx], pair.at[xx], pair_s.at[xx], pair_r.at[xx], head=other).wait_recv()
        pair[xx] = (pair[xx].astype(f32) + part[xx, core].astype(f32)).astype(bf16)

    send_pair(x_far)
    send_pair(x_right)
    send_pair(x_left)
    pair_sum(x_far)
    fars = [
        remote(pair.at[x_far, 0], far.at[0], far_s.at[0], far_r.at[0], head=right),
        remote(pair.at[x_far, 1], far.at[1], far_s.at[1], far_r.at[1], head=left),
    ]
    for copy in fars:
        copy.start()
    pair_sum(x_right)
    pair_sum(x_left)
    nears = [
        remote(pair.at[x_right, 1], near.at[0, 1], near_s.at[0, 1], near_r.at[0, 1], head=right),
        remote(pair.at[x_left, 0], near.at[1, 0], near_s.at[1, 0], near_r.at[1, 0], head=left),
        remote(pair.at[x_right, 0], near.at[0, 0], near_s.at[0, 0], near_r.at[0, 0], head=right),
        remote(pair.at[x_left, 1], near.at[1, 1], near_s.at[1, 1], near_r.at[1, 1], head=left),
    ]
    nears[0].start()
    nears[1].start()
    send_pair(x)
    attn_sum.hand_out_y()
    pair_sum(x)
    fars[0].wait_recv()
    pair[x_right, 0] = (pair[x_right, 0].astype(f32) + far[0].astype(f32)).astype(bf16)
    nears[2].start()
    fars[1].wait_recv()
    pair[x_left, 1] = (pair[x_left, 1].astype(f32) + far[1].astype(f32)).astype(bf16)
    nears[3].start()
    qkv.settle()
    for copy in (*sum(rows_out, ()), *sum(back, []), *pairs):
        copy.wait_send()

    @pl.when(has_right)
    def _():
        for copy in to_right:
            copy.wait_send()

    @pl.when(has_left)
    def _():
        for copy in to_left:
            copy.wait_send()

    for copy in nears:
        copy.wait_recv()
    for half in range(halves):
        at = half * model // halves
        out[:, at : at + model // halves] = (
            pair[x, half].astype(f32) + near[0, half].astype(f32) + near[1, half].astype(f32)
        ).astype(bf16)

    attn_sum.end()
    for h in range(heads):
        total = text_out[h].reshape(HEAD_SIZE, txt) / text_out[heads, 0, 0, h : h + 1]
        text_final[:, h * HEAD_SIZE : (h + 1) * HEAD_SIZE] = total.T.astype(bf16)
    attn_sum.settle()
    for copy in (*fars, *nears):
        copy.wait_send()


def run_whole(slab_count, head_count, operands):
    video, text, wq = operands[0], operands[1], operands[2]
    depth, width = wq.shape
    tokens, model = video.shape
    txt = text.shape[0]
    heads = width // HEAD_SIZE
    nz, nx = slab_count // Y, head_count // 2
    rows = tokens // head_count
    bf16, f32 = jnp.bfloat16, jnp.float32
    na = nz // NB
    text_block = jax.ShapeDtypeStruct((3, na, NB, txt * heads // nz, HEAD_SIZE), bf16)
    sum_block = jax.ShapeDtypeStruct((heads + 1, na, NB, HEAD_SIZE // nz, txt), f32)
    half = model // 2
    vmem = pl.BlockSpec(memory_space=VMEM)
    return pl.pallas_call(
        whole_kernel,
        out_shape=(
            jax.ShapeDtypeStruct((rows, model), bf16),
            jax.ShapeDtypeStruct((txt, width), bf16),
        ),
        in_specs=[pl.BlockSpec(memory_space=pltpu.HBM)] * OPERANDS,
        out_specs=(vmem, vmem),
        scratch_shapes=[
            *(VMEM(a.shape, a.dtype) for a in operands[:-1]),
            pltpu.SMEM(operands[-1].shape, operands[-1].dtype),
            DMA((OPERANDS,)),
            VMEM((3, depth, width), bf16),
            VMEM((nz, Y, depth, width), bf16),
            VMEM((nz, Y, 3, depth, width), bf16),
            VMEM((tokens, model), bf16),
            VMEM((txt, 2 * LANES), bf16),
            VMEM((2 * LANES, 3 * width), bf16),
            VMEM(text_block.shape, bf16),
            VMEM(text_block.shape, bf16),
            VMEM((tokens, 3 * width), f32),
            VMEM((3, heads, tokens, HEAD_SIZE), bf16),
            VMEM((3, heads, tokens, HEAD_SIZE), bf16),
            VMEM((3, heads, HEAD_SIZE, tokens), bf16),
            VMEM((3, heads, HEAD_SIZE, tokens), f32),
            VMEM((3, heads, 8, tokens), f32),
            VMEM((2, heads, HEAD_SIZE, tokens), bf16),
            VMEM((2, heads, HEAD_SIZE, tokens), bf16),
            VMEM((2, heads, 8, tokens), f32),
            VMEM((tokens, width), bf16),
            VMEM((txt, txt), f32),
            VMEM(sum_block.shape, f32),
            VMEM(sum_block.shape, f32),
            VMEM((nx, 2, 2, rows, half), bf16),
            VMEM((nx, 2, rows, half), bf16),
            VMEM((2, rows, half), bf16),
            VMEM((2, 2, rows, half), bf16),
            *TorusGather.scratch(nz),
            *SlabSum.scratch(text_block),
            *SlabSum.scratch(sum_block),
            *[DMA((2, heads))] * 10,
            DMA((nx,)), DMA((nx,)), DMA((2,)), DMA((2,)), DMA((2, 2)), DMA((2, 2)),
        ],
        compiler_params=pltpu.CompilerParams(
            collective_id=0, has_side_effects=True, vmem_limit_bytes=32 * MIB
        ),
        name="whole",
    )(*(pltpu.with_memory_space_constraint(a, pltpu.HBM) for a in operands))


def on_device(
    video_token_state,
    text_tokens,
    text_mask,
    head_window,
    video_query_weight,
    video_key_weight,
    video_value_weight,
    wout_video,
    wquery_text,
    wkey_text,
    wvalue_text,
    video_query_gain,
    video_key_gain,
    qgain_text,
    kgain_text,
):
    operands = (
        video_token_state, text_tokens,
        video_query_weight, video_key_weight, video_value_weight, wout_video.T,
        wquery_text, wkey_text, wvalue_text,
        *(row.reshape(1, -1) for row in (video_query_gain, video_key_gain, qgain_text, kgain_text, text_mask)),
        head_window.T,
    )
    return run_whole(lax.axis_size("slab"), lax.axis_size("head"), operands)


def solution(mesh):
    return jax.shard_map(
        on_device,
        mesh=mesh,
        in_specs=(
            P("slab", None),
            P(),
            P(),
            P(),
            P("slab", "head"),
            P("slab", "head"),
            P("slab", "head"),
            P("head", "slab"),
            P("slab", "head"),
            P("slab", "head"),
            P("slab", "head"),
            P(),
            P(),
            P(),
            P(),
        ),
        out_specs=(P(("slab", "head"), None), P(None, "head")),
        check_vma=False,
    )
```

```python
import functools
import math

import jax
import jax.numpy as jnp
from jax import lax
from jax.experimental import pallas as pl
from jax.experimental.pallas import tpu as pltpu
from jax.sharding import PartitionSpec as P

HEAD_SIZE = 128
COLUMN_TILES = 8
Y = 4
MIB = 1 << 20
LANES = 128
VMEM = pltpu.VMEM
DMA = pltpu.SemaphoreType.DMA

norm_eps = 1e-06


def mod(a, n):
    return lax.rem(a, jnp.int32(n))


def remote(src, dst, send, recv, **device):
    return pltpu.make_async_remote_copy(
        src_ref=src, dst_ref=dst, send_sem=send, recv_sem=recv,
        device_id=device, device_id_type=pl.DeviceIdType.MESH,
    )


def greet(slabs=(), heads=()):
    barrier = pltpu.get_barrier_semaphore()
    for slab in slabs:
        pl.semaphore_signal(barrier, 1, device_id={"slab": slab}, device_id_type=pl.DeviceIdType.MESH)
    for head in heads:
        pl.semaphore_signal(barrier, 1, device_id={"head": head}, device_id_type=pl.DeviceIdType.MESH)
    return barrier


def when(condition, step):
    if isinstance(condition, bool):
        if condition:
            step()
    else:
        pl.when(condition)(step)


def hello_slab(z, y, nz):
    barrier = pltpu.get_barrier_semaphore()

    def greet_one(slab):
        pl.semaphore_signal(barrier, 1, device_id={"slab": slab}, device_id_type=pl.DeviceIdType.MESH)

    for d in range(1, Y):
        greet_one(z * Y + mod(y + d, Y))

    def body(d, carry):
        greet_one(mod(z + d, nz) * Y + y)
        return carry

    lax.fori_loop(1, nz, body, 0)
    return barrier, Y - 1 + nz - 1


class SlabSum:
    @staticmethod
    def scratch(block):
        owners, nz, rows, lanes = block.shape
        return [
            VMEM((Y, nz, rows, lanes), block.dtype),
            VMEM((nz, rows, lanes), block.dtype),
            VMEM((nz, rows, lanes), block.dtype),
            DMA((2, 2, Y)),
            DMA((2, 2)),
        ]

    def __init__(self, part, out, scratch):
        self.part, self.out = part, out
        self.from_y, self.sum_y, self.from_z, self.ysem, self.zsem = scratch
        self.owners, self.nz = part.shape[:2]
        slab = lax.axis_index("slab")
        self.z, self.y = slab // Y, mod(slab, Y)

    def _owns(self, y):
        return True if self.owners == Y else y < self.owners

    def _y(self, d, give):
        y, to = self.y, mod(self.y + d, Y)
        src = self.out.at[y] if give else self.part.at[to]
        dst = self.out.at[y] if give else self.from_y.at[y]
        return remote(src, dst, self.ysem.at[give, 0, to], self.ysem.at[give, 1, y], slab=self.z * Y + to)

    def _y_in(self, d, give):
        of = mod(self.y + d, Y)
        dst = self.out.at[of] if give else self.from_y.at[of]
        return remote(dst, dst, self.ysem.at[give, 0, of], self.ysem.at[give, 1, of], slab=self.z * Y + of)

    def _z(self, d, give):
        z, to = self.z, mod(self.z + d, self.nz)
        src = self.out.at[self.y, z] if give else self.sum_y.at[to]
        dst = self.out.at[self.y, z] if give else self.from_z.at[z]
        return remote(src, dst, self.zsem.at[give, 0], self.zsem.at[give, 1], slab=to * Y + self.y)

    def _all_z(self, give):
        blocks = self.from_z.at[pl.ds(0, self.nz - 1)]
        to = mod(self.z + 1, self.nz)
        return remote(blocks, blocks, self.zsem.at[give, 0], self.zsem.at[give, 1], slab=to * Y + self.y)

    def _each_z(self, step):
        def body(d, carry):
            step(d)
            return carry

        lax.fori_loop(1, self.nz, body, 0)

    def start(self):
        for d in range(1, Y):
            when(self._owns(mod(self.y + d, Y)), lambda: self._y(d, 0).start())

    def along_z(self):
        def step():
            for d in range(1, Y):
                self._y_in(d, 0).wait_recv()
            total = self.part[self.y].astype(jnp.float32)
            for d in range(1, Y):
                total = total + self.from_y[mod(self.y + d, Y)].astype(jnp.float32)
            self.sum_y[...] = total.astype(self.sum_y.dtype)
            self._each_z(lambda d: self._z(d, 0).start())

        when(self._owns(self.y), step)

    def hand_out_z(self, finish):
        def step():
            self._all_z(0).wait_recv()
            total = self.sum_y[self.z].astype(jnp.float32)
            for d in range(1, self.nz):
                total = total + self.from_z[mod(self.z + d, self.nz)].astype(jnp.float32)
            self.out[self.y, self.z] = finish(total).astype(self.out.dtype)
            self._each_z(lambda d: self._z(d, 1).start())

        when(self._owns(self.y), step)

    def hand_out_y(self):
        def step():
            self._all_z(1).wait_recv()
            for d in range(1, Y):
                self._y(d, 1).start()

        when(self._owns(self.y), step)

    def end(self):
        for d in range(1, Y):
            when(self._owns(mod(self.y + d, Y)), lambda: self._y_in(d, 1).wait_recv())

    def settle(self):
        for d in range(1, Y):
            when(self._owns(mod(self.y + d, Y)), lambda: self._y(d, 0).wait_send())

        def mine():
            for d in range(1, Y):
                self._y(d, 1).wait_send()

            self._all_z(0).wait_send()
            self._all_z(1).wait_send()

        when(self._owns(self.y), mine)


class TorusGather:
    RELAYED = 6
    NEAR = 5

    @staticmethod
    def scratch(nz):
        return [
            DMA((1,)), DMA((nz, 2)), DMA((3,)), DMA((3,)),
            DMA((1,)), DMA((nz,)), DMA((1,)), DMA((2, nz)), DMA((1,)), DMA((2,)), DMA((3,)),
            DMA((2, 2)), DMA((2, 2)), DMA((2,)), DMA((2,)),
        ]

    def __init__(self, wa, wb, ga, gb, sems):
        self.wa, self.wb, self.ga, self.gb = wa, wb, ga, gb
        (self.az_s, self.az_r, self.ay_s, self.ay_r, self.bz_s, self.bz_r,
         self.by_s, self.by_r, self.bo_s, self.bo_r, self.own_sem,
         self.ly_s, self.ly_r, self.lo_s, self.lo_r) = sems
        self.nz = nz = gb.shape[0]
        self.half = nz // 2
        slab = lax.axis_index("slab")
        self.z, self.y = z, y = slab // Y, mod(slab, Y)
        self.next = mod(z + 1, nz), mod(z + nz - 1, nz)
        self.right, self.left, self.across = mod(y + 1, Y), mod(y + Y - 1, Y), mod(y + 2, Y)
        self.sides = self.right, self.left
        self.parts = (pl.ds(0, self.half), pl.ds(self.half, self.half))
        self.sent = []

    def _go(self, copy):
        copy.start()
        self.sent.append(copy)

    def _landed(self, dst, sem):
        remote(dst, dst, self.own_sem.at[2], sem, slab=self.z * Y + self.right).wait_recv()

    def _pair(self, origin, p):
        return self.ga.at[origin, pl.ds(2 * p, 2)]

    def _a_z(self, origin, p, way):
        block = self._pair(origin, p)
        remote(block, block, self.az_s.at[0], self.az_r.at[origin, p],
               slab=self.next[way] * Y + self.y).start()

    def _b_z(self, origin, src, way):
        remote(src, self.gb.at[origin, self.y], self.bz_s.at[0], self.bz_r.at[origin],
               slab=self.next[way] * Y + self.y).start()

    def _two(self, origin, j):
        return self.gb.at[origin, j, pl.ds(0, 2)]

    def _b_y(self, origin, src):
        for way, to in enumerate(self.sides):
            remote(src, self._two(origin, self.y), self.by_s.at[0], self.by_r.at[way, origin],
                   slab=self.z * Y + to).start()

    def _b_relay(self, origin, t):
        self._landed(self._two(origin, self.left), self.by_r.at[0, origin])
        self._landed(self._two(origin, self.right), self.by_r.at[1, origin])
        turn = 1 - 2 * mod(origin, 2)
        block = self._two(origin, mod(self.y - turn + Y, Y))
        remote(block, block, self.bo_s.at[0], self.bo_r.at[int(t > self.NEAR)],
               slab=self.z * Y + mod(self.y + turn + Y, Y)).start()

    def start(self, meanwhile):
        z, y, wa, wb = self.z, self.y, self.wa, self.wb
        self._b_z(z, wb, 0)
        self._b_z(z, wb, 1)
        for i, to in enumerate((self.right, self.left, self.across)):
            self._go(remote(wa, self.ga.at[z, y], self.ay_s.at[i], self.ay_r.at[i], slab=z * Y + to))
        self.own_a = pltpu.make_async_copy(wa, self.ga.at[z, y], self.own_sem.at[0])
        self.own_a.start()
        self._b_y(z, wb.at[pl.ds(0, 2)])
        self.own_b = pltpu.make_async_copy(wb, self.gb.at[z, y], self.own_sem.at[1])
        self.own_b.start()
        meanwhile()
        odd = mod(y, 2)
        self._landed(self.ga.at[z, y + 1 - 2 * odd], self.ay_r.at[1 - odd])
        self.own_a.wait()
        self._a_z(z, y // 2, 0)
        self._a_z(z, y // 2, 1)
        self._landed(self.ga.at[z, mod(y + Y - 1 + 2 * odd, Y)], self.ay_r.at[odd])
        self._landed(self.ga.at[z, self.across], self.ay_r.at[2])
        self._a_z(z, 1 - y // 2, 0)
        self._a_z(z, 1 - y // 2, 1)

    def step(self, t):
        nz, half, y = self.nz, self.half, self.y
        ways = [(mod(self.z - t + nz, nz), 0, half)]
        if t < half:
            ways.append((mod(self.z + t, nz), 1, half - 1))
        for origin, way, last in ways:
            block = self.gb.at[origin, y]
            self._landed(block, self.bz_r.at[origin])
            if t < last:
                self._b_z(origin, block, way)
        if t > self.RELAYED:
            self._along_y(ways, t)
        for p in (y // 2, 1 - y // 2):
            for origin, way, last in ways:
                self._landed(self._pair(origin, p), self.az_r.at[origin, p])
                if t < last:
                    self._a_z(origin, p, way)
        if t <= self.RELAYED:
            self._along_y(ways, t)
        if t > 1:
            self._b_relay(mod(self.z - t + 2 + nz, nz), t - 2)
            if t > 2:
                self._b_relay(mod(self.z + t - 2, nz), t - 2)

    def _along_y(self, ways, t):
        for origin, _, _ in ways:
            two = self._two(origin, self.y)
            self._b_y(origin, two)
            if t > self.RELAYED:
                remote(two, two, self.bo_s.at[0], self.bo_r.at[1],
                       slab=self.z * Y + self.across).start()

    def near_landed(self):
        self._landed(self.gb.at[pl.ds(0, 2 * self.NEAR + 1), 0, pl.ds(0, 2)], self.bo_r.at[0])

    def far_landed(self):
        for t in range(self.RELAYED + 1, self.half + 1):
            for origin in (mod(self.z - t + self.nz, self.nz), mod(self.z + t, self.nz))[: 1 + (t < self.half)]:
                self._landed(self._two(origin, self.left), self.by_r.at[0, origin])
                self._landed(self._two(origin, self.right), self.by_r.at[1, origin])
        self._landed(self.gb.at[pl.ds(0, self.nz - 2 * self.NEAR - 1), 0, pl.ds(0, 2)], self.bo_r.at[1])

    def _late(self, part, j):
        return self.gb.at[self.parts[part], j, 2]

    def late_start(self):
        for turn in range(2):
            for way in range(2):
                part = way if turn == 0 else 1 - way
                block = self._late(part, self.y)
                self._go(remote(block, block, self.ly_s.at[way, part], self.ly_r.at[way, part],
                                slab=self.z * Y + self.sides[way]))

    def late_relay(self):
        for way in range(2):
            block = self._late(way, self.sides[1 - way])
            self._landed(block, self.ly_r.at[way, way])
            self._go(remote(block, block, self.lo_s.at[way], self.lo_r.at[way], slab=self.z * Y + self.sides[way]))

    def late_end(self):
        for way in range(2):
            self._landed(self._late(1 - way, self.sides[1 - way]), self.ly_r.at[way, 1 - way])
        for way in range(2):
            self._landed(self._late(way, self.across), self.lo_r.at[way])

    def settle(self):
        nz, one, two = self.nz, pl.ds(0, 1), pl.ds(0, 2)
        for block, sem in (
            (self.ga.at[pl.ds(0, nz - 1)], self.az_s),
            (self.gb.at[pl.ds(0, nz - 1), one], self.bz_s),
            (self.gb.at[:, two, two], self.by_s),
            (self.gb.at[:, one, two], self.bo_s),
        ):
            remote(block, block, sem.at[0], self.own_sem.at[2], slab=self.z * Y + self.right).wait_send()
        for copy in self.sent:
            copy.wait_send()


def row_scale(values):
    return lax.rsqrt(jnp.mean(values * values, axis=-1, keepdims=True) + norm_eps)


OPERANDS = 15
FETCH_ORDER = (2, 3, 4, 5, 0, 1, 6, 7, 8, 9, 10, 11, 12, 13, 14)
QKV_SEMS = 15


def whole_kernel(*refs):
    f32, bf16 = jnp.float32, jnp.bfloat16

    def take(count):
        nonlocal refs
        some, refs = refs[:count], refs[count:]
        return some

    fetched = take(OPERANDS)
    out, text_final = take(2)
    held = take(OPERANDS)
    video, text, wq, wk, wv, wo, twq, twk, twv, qg, kg, tqg, tkg, mask, window = held
    (fetch_sem, wb, ga, gb, normed, tnormed, tweight, text_part, text_rows, acc) = take(10)
    (q, k, v, num, den, num_out, num_in, den_in, attn, live, tsum_part, text_out) = take(12)
    (part, pair, far, near) = take(4)
    qkv = TorusGather(wq, wb, ga, gb, take(QKV_SEMS))
    text_sum = SlabSum(text_part, text_rows, take(5))
    attn_sum = SlabSum(tsum_part, text_out, take(5))
    q_s, q_r, k_s, k_r, v_s, v_r, n_s, n_r, d_s, d_r = take(10)
    pair_s, pair_r, far_s, far_r, near_s, near_r = take(6)

    nz = gb.shape[0]
    nx = part.shape[0]
    slab, head = lax.axis_index("slab"), lax.axis_index("head")
    slab_count = lax.axis_size("slab")
    z, y = slab // Y, mod(slab, Y)
    row, column = slab // COLUMN_TILES, mod(slab, COLUMN_TILES)
    above, below = mod(slab + slab_count - COLUMN_TILES, slab_count), mod(slab + COLUMN_TILES, slab_count)
    has_left, has_right = column > 0, column < COLUMN_TILES - 1
    has_above, has_below = row > 0, row < slab_count // COLUMN_TILES - 1
    jump_left, jump_right = has_left & (y == 0), has_right & (y == Y - 1)
    x, core = head // 2, mod(head, 2)
    x_right, x_left, x_far = mod(x + 1, nx), mod(x + nx - 1, nx), mod(x + 2, nx)
    other, right, left = x * 2 + 1 - core, x_right * 2 + core, x_left * 2 + core
    depth, width = wq.shape
    heads = width // HEAD_SIZE
    tokens, model = video.shape
    txt = text.shape[0]
    score_scale = 1.0 / math.sqrt(HEAD_SIZE)
    steps = nz // 2
    nt = (((1,), (1,)), ((), ()))

    fetches = [
        pltpu.make_async_copy(src, dst, fetch_sem.at[i]) for i, (src, dst) in enumerate(zip(fetched, held))
    ]
    for i in FETCH_ORDER:
        fetches[i].start()

    barrier, peers = hello_slab(z, y, nz)
    greet((), (other, right, left))

    @pl.when(jump_left)
    def _():
        greet((slab - 1,))

    @pl.when(jump_right)
    def _():
        greet((slab + 1,))

    for i in FETCH_ORDER[:4]:
        fetches[i].wait()
    for i, weight in enumerate((wk, wv, wo)):
        wb[i] = weight[...]
    pl.semaphore_wait(barrier, peers + 3 + jump_left.astype(jnp.int32) + jump_right.astype(jnp.int32))
    def normalize_video(i, carry):
        at = pl.ds(pl.multiple_of(i * 16, 16), 16)
        values = video[at, :].astype(f32)
        center = values - jnp.mean(values, axis=-1, keepdims=True)
        normed[at, :] = (center * row_scale(center)).astype(bf16)
        return carry

    blocks = tokens // 16
    early = blocks // 4

    def first_rows():
        fetches[0].wait()
        lax.fori_loop(0, early, normalize_video, 0)

    qkv.start(first_rows)

    span = tweight.shape[0]
    aligned = jnp.minimum(slab * depth // LANES * LANES, model - span)
    aligned = pl.multiple_of(aligned, LANES)
    offset = pl.multiple_of(slab * depth - aligned, 16)
    share = nz // heads

    def fill_text_weights():
        tweight[...] = jnp.zeros_like(tweight)
        for i, weight in enumerate((twq, twk, twv)):
            tweight[pl.ds(offset, depth), i * width : (i + 1) * width] = weight[...]

    def normalize_text(i, carry):
        at = pl.ds(pl.multiple_of(i * 16, 16), 16)
        values = text[at, :].astype(f32)
        mean = jnp.mean(values, axis=-1, keepdims=True)
        scale = row_scale(values - mean)
        columns = text[at, pl.ds(aligned, span)].astype(f32)
        tnormed[at, :] = ((columns - mean) * scale).astype(bf16)
        return carry

    def multiply_text():
        for i in range(3):
            product = jnp.dot(
                tnormed[...], tweight[:, i * width : (i + 1) * width], preferred_element_type=f32
            ).astype(bf16)
            for h in range(heads):
                block = product[:, h * HEAD_SIZE : (h + 1) * HEAD_SIZE]
                text_part[i, h * share : (h + 1) * share] = block.reshape(share, *text_part.shape[2:])

    def finish_text(total):
        gain = jnp.where(y == 0, tqg[...], tkg[...])
        return jnp.where(y == 2, total, total * row_scale(total) * gain)

    for t in range(1, steps + 1):
        qkv.step(t)
        if t == 1:
            for i in FETCH_ORDER[5:]:
                fetches[i].wait()
            fill_text_weights()
            lax.fori_loop(0, txt // 32, normalize_text, 0)
        if t == 2:
            lax.fori_loop(txt // 32, txt // 16, normalize_text, 0)
            multiply_text()
            text_sum.start()
        if t == 4:
            text_sum.along_z()
        if t == 7:
            text_sum.hand_out_z(finish_text)
        rest = blocks - early
        lax.fori_loop(early + (t - 1) * rest // steps, early + t * rest // steps, normalize_video, 0)

    qkv.own_b.wait()
    qkv.late_start()

    acc[...] = jnp.zeros_like(acc)
    group = 4 if nz % 4 == 0 else nz
    span = group * Y * depth

    def multiply_query(c, carry):
        rows = normed[:, pl.ds(pl.multiple_of(c * span, span), span)]
        acc[:, :width] += jnp.dot(
            rows, ga[pl.ds(c * group, group)].reshape(span, width), preferred_element_type=f32
        )
        return carry

    lax.fori_loop(0, nz // group, multiply_query, 0)
    rows_out = []
    for h in range(heads):
        values = acc[:, h * HEAD_SIZE : (h + 1) * HEAD_SIZE]
        q[0, h] = (values * row_scale(values) * qg[...]).astype(bf16)
        to_below = remote(q.at[0, h], q.at[1, h], q_s.at[0, h], q_r.at[0, h], slab=below)
        to_above = remote(q.at[0, h], q.at[2, h], q_s.at[1, h], q_r.at[1, h], slab=above)
        to_below.start()
        to_above.start()
        rows_out.append((to_below, to_above))
    text_sum.hand_out_y()

    pair_depth = 2 * Y * depth

    def multiply_rest(i, carry):
        at = mod(z // 2 + i + nz // 2 - 2, nz // 2)
        rows = normed[:, pl.ds(pl.multiple_of(at * pair_depth, pair_depth), pair_depth)]
        for j in range(2):
            acc[:, (j + 1) * width : (j + 2) * width] += jnp.dot(
                rows, gb[pl.ds(at * 2, 2), :, j].reshape(pair_depth, width), preferred_element_type=f32
            )
        return carry

    qkv.near_landed()
    lax.fori_loop(0, 5, multiply_rest, 0)
    qkv.far_landed()
    lax.fori_loop(5, nz // 2, multiply_rest, 0)

    to_right, to_left = [], []
    for h in range(heads):
        values = acc[:, width + h * HEAD_SIZE : width + (h + 1) * HEAD_SIZE]
        k[0, h] = (values * row_scale(values) * kg[...]).astype(bf16)
        v[0, h] = acc[:, 2 * width + h * HEAD_SIZE : 2 * width + (h + 1) * HEAD_SIZE].T.astype(bf16)
        right_now = [
            remote(k.at[0, h], k.at[1, h], k_s.at[0, h], k_r.at[0, h], slab=slab + 1),
            remote(v.at[0, h], v.at[1, h], v_s.at[0, h], v_r.at[0, h], slab=slab + 1),
        ]
        left_now = [
            remote(k.at[0, h], k.at[2, h], k_s.at[1, h], k_r.at[1, h], slab=slab - 1),
            remote(v.at[0, h], v.at[2, h], v_s.at[1, h], v_r.at[1, h], slab=slab - 1),
        ]
        to_right += right_now
        to_left += left_now

        def start_all(copies):
            for copy in copies:
                copy.start()

        pl.when(has_right)(functools.partial(start_all, right_now))
        pl.when(has_left)(functools.partial(start_all, left_now))

    @pl.when(jnp.logical_not(has_left))
    def _():
        k[1] = jnp.zeros_like(k[1])
        v[1] = jnp.zeros_like(v[1])

    @pl.when(jnp.logical_not(has_right))
    def _():
        k[2] = jnp.zeros_like(k[2])
        v[2] = jnp.zeros_like(v[2])

    def scores(keys, queries):
        return jnp.exp(lax.dot_general(keys, queries, nt, preferred_element_type=f32) * score_scale)

    def weigh(values, e):
        return jnp.dot(values, e.astype(bf16), preferred_element_type=f32)

    def column_sum(e):
        return jnp.sum(e, axis=0, keepdims=True)

    tsum_part[heads] = jnp.zeros_like(tsum_part[heads])
    for h in range(heads):
        e = scores(k[0, h], q[0, h])
        num[0, h] = weigh(v[0, h], e)
        den[0, h, 0:1] = column_sum(e)

    qkv.late_relay()

    for h in range(heads):
        for copy in rows_out[h]:
            copy.wait_recv()

        def neighbour(tile, carry, h=h):
            e = scores(k[0, h], q[tile, h])
            num[tile, h] = weigh(v[0, h], e)
            den[tile, h] = jnp.broadcast_to(column_sum(e), den.shape[2:])
            return carry

        lax.fori_loop(1, 3, neighbour, 0)
    live[...] = jnp.broadcast_to(mask[...].astype(f32), live.shape).T
    is_first = jnp.where(slab == 0, 1.0, 0.0)
    text_sum.end()

    def text_head(i, h):
        return text_rows[i, h * share : (h + 1) * share].reshape(txt, HEAD_SIZE)

    text_values = []
    for h in range(heads):
        tq = text_head(0, h)
        text_values.append(text_head(2, h).astype(f32).T.astype(bf16))
        e = scores(k[0, h], tq)
        own = scores(text_head(1, h), tq) * live[...] * is_first
        total = weigh(v[0, h], e) + weigh(text_values[h], own)
        tsum_part[h] = total.reshape(tsum_part.shape[1:])
        tsum_part[heads, 0, h : h + 1] = column_sum(e) + column_sum(own)
    attn_sum.start()

    live_wide = jnp.concatenate([live[...]] * (tokens // txt), axis=1)
    for h in range(heads):
        e = scores(text_head(1, h), q[0, h]) * live_wide
        num[0, h] += weigh(text_values[h], e)
        den[0, h, 0:1] += column_sum(e)


    def add_side(slot, tile, h):
        reach = jnp.where(jnp.where(slot == 1, has_left, has_right), 1.0, 0.0)
        e = scores(k[slot, h], q[tile, h])
        e = e * (reach * window[1, head * heads + h].astype(f32))
        num[tile, h] += weigh(v[slot, h], e)
        den[tile, h, 0:1] += column_sum(e)

    back = []
    for h in range(heads):

        @pl.when(has_left)
        def _():
            for sem, dst in ((k_r, k), (v_r, v)):
                remote(dst.at[1, h], dst.at[1, h], sem.at[0, h], sem.at[0, h], slab=slab - 1).wait_recv()

        @pl.when(has_right)
        def _():
            for sem, dst in ((k_r, k), (v_r, v)):
                remote(dst.at[2, h], dst.at[2, h], sem.at[1, h], sem.at[1, h], slab=slab + 1).wait_recv()

        def side(i, carry, h=h):
            add_side(1 + i % 2, 1 + i // 2, h)
            return carry

        lax.fori_loop(0, 4, side, 0)
        for tile in (1, 2):
            num_out[tile - 1, h] = num[tile, h].astype(bf16)
        now = [
            remote(num_out.at[0, h], num_in.at[1, h], n_s.at[1, h], n_r.at[1, h], slab=above),
            remote(num_out.at[1, h], num_in.at[0, h], n_s.at[0, h], n_r.at[0, h], slab=below),
            remote(den.at[1, h], den_in.at[1, h], d_s.at[1, h], d_r.at[1, h], slab=above),
            remote(den.at[2, h], den_in.at[0, h], d_s.at[0, h], d_r.at[0, h], slab=below),
        ]
        for copy in now:
            copy.start()
        back.append(now)

    def own_side(i, carry):
        add_side(1 + i % 2, 0, i // 2)
        return carry

    lax.fori_loop(0, 2 * heads, own_side, 0)
    attn_sum.along_z()
    text_sum.settle()
    for h in range(heads):
        for copy in back[h]:
            copy.wait_recv()
        total, under = num[0, h], den[0, h, 0:1]
        for side_row, exists in ((0, has_above), (1, has_below)):
            reach = jnp.where(exists, 1.0, 0.0) * window[0, head * heads + h].astype(f32)
            total = total + num_in[side_row, h].astype(f32) * reach
            under = under + den_in[side_row, h, 0:1] * reach
        attn[:, h * HEAD_SIZE : (h + 1) * HEAD_SIZE] = (total / under).T.astype(bf16)

    qkv.late_end()
    order = (x_far, x_right, x_left, x)
    rows = tokens // nx
    halves = part.shape[2]
    pairs = []

    def send_pair(xx):
        mine = attn[pl.ds(pl.multiple_of(xx * rows, 16), rows), :]
        for half in range(halves):
            weight = gb[half * nz // halves : (half + 1) * nz // halves, :, 2].reshape(model // halves, width)
            product = lax.dot_general(mine, weight, nt, preferred_element_type=f32).astype(bf16)
            for c in range(2):
                part[xx, c, half] = product[c * rows // 2 : (c + 1) * rows // 2]
        pairs.append(remote(part.at[xx, 1 - core], pair.at[xx], pair_s.at[xx], pair_r.at[xx], head=other))
        pairs[-1].start()

    def pair_sum(xx):
        remote(pair.at[xx], pair.at[xx], pair_s.at[xx], pair_r.at[xx], head=other).wait_recv()
        pair[xx] = (pair[xx].astype(f32) + part[xx, core].astype(f32)).astype(bf16)

    send_pair(x_far)
    send_pair(x_right)
    send_pair(x_left)
    pair_sum(x_far)
    fars = [
        remote(pair.at[x_far, 0], far.at[0], far_s.at[0], far_r.at[0], head=right),
        remote(pair.at[x_far, 1], far.at[1], far_s.at[1], far_r.at[1], head=left),
    ]
    for copy in fars:
        copy.start()
    pair_sum(x_right)
    pair_sum(x_left)
    nears = [
        remote(pair.at[x_right, 1], near.at[0, 1], near_s.at[0, 1], near_r.at[0, 1], head=right),
        remote(pair.at[x_left, 0], near.at[1, 0], near_s.at[1, 0], near_r.at[1, 0], head=left),
        remote(pair.at[x_right, 0], near.at[0, 0], near_s.at[0, 0], near_r.at[0, 0], head=right),
        remote(pair.at[x_left, 1], near.at[1, 1], near_s.at[1, 1], near_r.at[1, 1], head=left),
    ]
    nears[0].start()
    nears[1].start()
    send_pair(x)
    attn_sum.hand_out_z(lambda total: total)
    pair_sum(x)
    fars[0].wait_recv()
    pair[x_right, 0] = (pair[x_right, 0].astype(f32) + far[0].astype(f32)).astype(bf16)
    nears[2].start()
    fars[1].wait_recv()
    pair[x_left, 1] = (pair[x_left, 1].astype(f32) + far[1].astype(f32)).astype(bf16)
    nears[3].start()
    qkv.settle()
    attn_sum.hand_out_y()
    for copy in (*sum(rows_out, ()), *sum(back, []), *pairs):
        copy.wait_send()

    @pl.when(has_right)
    def _():
        for copy in to_right:
            copy.wait_send()

    @pl.when(has_left)
    def _():
        for copy in to_left:
            copy.wait_send()

    for copy in nears:
        copy.wait_recv()
    for half in range(halves):
        at = half * model // halves
        out[:, at : at + model // halves] = (
            pair[x, half].astype(f32) + near[0, half].astype(f32) + near[1, half].astype(f32)
        ).astype(bf16)

    attn_sum.end()
    for h in range(heads):
        total = text_out[h].reshape(HEAD_SIZE, txt) / text_out[heads, 0, h : h + 1]
        text_final[:, h * HEAD_SIZE : (h + 1) * HEAD_SIZE] = total.T.astype(bf16)
    attn_sum.settle()
    for copy in (*fars, *nears):
        copy.wait_send()


def run_whole(slab_count, head_count, operands):
    video, text, wq = operands[0], operands[1], operands[2]
    depth, width = wq.shape
    tokens, model = video.shape
    txt = text.shape[0]
    heads = width // HEAD_SIZE
    nz, nx = slab_count // Y, head_count // 2
    rows = tokens // head_count
    bf16, f32 = jnp.bfloat16, jnp.float32
    text_block = jax.ShapeDtypeStruct((3, nz, txt * heads // nz, HEAD_SIZE), bf16)
    sum_block = jax.ShapeDtypeStruct((heads + 1, nz, HEAD_SIZE // nz, txt), f32)
    half = model // 2
    vmem = pl.BlockSpec(memory_space=VMEM)
    return pl.pallas_call(
        whole_kernel,
        out_shape=(
            jax.ShapeDtypeStruct((rows, model), bf16),
            jax.ShapeDtypeStruct((txt, width), bf16),
        ),
        in_specs=[pl.BlockSpec(memory_space=pltpu.HBM)] * OPERANDS,
        out_specs=(vmem, vmem),
        scratch_shapes=[
            *(VMEM(a.shape, a.dtype) for a in operands[:-1]),
            pltpu.SMEM(operands[-1].shape, operands[-1].dtype),
            DMA((OPERANDS,)),
            VMEM((3, depth, width), bf16),
            VMEM((nz, Y, depth, width), bf16),
            VMEM((nz, Y, 3, depth, width), bf16),
            VMEM((tokens, model), bf16),
            VMEM((txt, 2 * LANES), bf16),
            VMEM((2 * LANES, 3 * width), bf16),
            VMEM(text_block.shape, bf16),
            VMEM(text_block.shape, bf16),
            VMEM((tokens, 3 * width), f32),
            VMEM((3, heads, tokens, HEAD_SIZE), bf16),
            VMEM((3, heads, tokens, HEAD_SIZE), bf16),
            VMEM((3, heads, HEAD_SIZE, tokens), bf16),
            VMEM((3, heads, HEAD_SIZE, tokens), f32),
            VMEM((3, heads, 8, tokens), f32),
            VMEM((2, heads, HEAD_SIZE, tokens), bf16),
            VMEM((2, heads, HEAD_SIZE, tokens), bf16),
            VMEM((2, heads, 8, tokens), f32),
            VMEM((tokens, width), bf16),
            VMEM((txt, txt), f32),
            VMEM(sum_block.shape, f32),
            VMEM(sum_block.shape, f32),
            VMEM((nx, 2, 2, rows, half), bf16),
            VMEM((nx, 2, rows, half), bf16),
            VMEM((2, rows, half), bf16),
            VMEM((2, 2, rows, half), bf16),
            *TorusGather.scratch(nz),
            *SlabSum.scratch(text_block),
            *SlabSum.scratch(sum_block),
            *[DMA((2, heads))] * 10,
            DMA((nx,)), DMA((nx,)), DMA((2,)), DMA((2,)), DMA((2, 2)), DMA((2, 2)),
        ],
        compiler_params=pltpu.CompilerParams(
            collective_id=0, has_side_effects=True, vmem_limit_bytes=32 * MIB
        ),
        name="whole",
    )(*(pltpu.with_memory_space_constraint(a, pltpu.HBM) for a in operands))


def on_device(
    video_token_state,
    text_tokens,
    text_mask,
    head_window,
    video_query_weight,
    video_key_weight,
    video_value_weight,
    wout_video,
    wquery_text,
    wkey_text,
    wvalue_text,
    video_query_gain,
    video_key_gain,
    qgain_text,
    kgain_text,
):
    operands = (
        video_token_state, text_tokens,
        video_query_weight, video_key_weight, video_value_weight, wout_video.T,
        wquery_text, wkey_text, wvalue_text,
        *(row.reshape(1, -1) for row in (video_query_gain, video_key_gain, qgain_text, kgain_text, text_mask)),
        head_window.T,
    )
    return run_whole(lax.axis_size("slab"), lax.axis_size("head"), operands)


def solution(mesh):
    return jax.shard_map(
        on_device,
        mesh=mesh,
        in_specs=(
            P("slab", None),
            P(),
            P(),
            P(),
            P("slab", "head"),
            P("slab", "head"),
            P("slab", "head"),
            P("head", "slab"),
            P("slab", "head"),
            P("slab", "head"),
            P("slab", "head"),
            P(),
            P(),
            P(),
            P(),
        ),
        out_specs=(P(("slab", "head"), None), P(None, "head")),
        check_vma=False,
    )
```

```python
import functools
import math

import jax
import jax.numpy as jnp
from jax import lax
from jax.experimental import pallas as pl
from jax.experimental.pallas import tpu as pltpu
from jax.sharding import PartitionSpec as P

HEAD_SIZE = 128
COLUMN_TILES = 8
Y = 4
MIB = 1 << 20
LANES = 128
VMEM = pltpu.VMEM
DMA = pltpu.SemaphoreType.DMA

norm_eps = 1e-06


def mod(a, n):
    return lax.rem(a, jnp.int32(n))


def remote(src, dst, send, recv, **device):
    return pltpu.make_async_remote_copy(
        src_ref=src, dst_ref=dst, send_sem=send, recv_sem=recv,
        device_id=device, device_id_type=pl.DeviceIdType.MESH,
    )


def greet(slabs=(), heads=()):
    barrier = pltpu.get_barrier_semaphore()
    for slab in slabs:
        pl.semaphore_signal(barrier, 1, device_id={"slab": slab}, device_id_type=pl.DeviceIdType.MESH)
    for head in heads:
        pl.semaphore_signal(barrier, 1, device_id={"head": head}, device_id_type=pl.DeviceIdType.MESH)
    return barrier


def when(condition, step):
    if isinstance(condition, bool):
        if condition:
            step()
    else:
        pl.when(condition)(step)


def hello_slab(z, y, nz):
    barrier = pltpu.get_barrier_semaphore()

    def greet_one(slab):
        pl.semaphore_signal(barrier, 1, device_id={"slab": slab}, device_id_type=pl.DeviceIdType.MESH)

    for d in range(1, Y):
        greet_one(z * Y + mod(y + d, Y))

    def body(d, carry):
        greet_one(mod(z + d, nz) * Y + y)
        return carry

    lax.fori_loop(1, nz, body, 0)
    return barrier, Y - 1 + nz - 1


class SlabSum:
    @staticmethod
    def scratch(block):
        owners, nz, rows, lanes = block.shape
        return [
            VMEM((Y, nz, rows, lanes), block.dtype),
            VMEM((nz, rows, lanes), block.dtype),
            VMEM((nz, rows, lanes), block.dtype),
            DMA((2, 2, Y)),
            DMA((2, 2)),
        ]

    def __init__(self, part, out, scratch):
        self.part, self.out = part, out
        self.from_y, self.sum_y, self.from_z, self.ysem, self.zsem = scratch
        self.owners, self.nz = part.shape[:2]
        slab = lax.axis_index("slab")
        self.z, self.y = slab // Y, mod(slab, Y)

    def _owns(self, y):
        return True if self.owners == Y else y < self.owners

    def _y(self, d, give):
        y, to = self.y, mod(self.y + d, Y)
        src = self.out.at[y] if give else self.part.at[to]
        dst = self.out.at[y] if give else self.from_y.at[y]
        return remote(src, dst, self.ysem.at[give, 0, to], self.ysem.at[give, 1, y], slab=self.z * Y + to)

    def _y_in(self, d, give):
        of = mod(self.y + d, Y)
        dst = self.out.at[of] if give else self.from_y.at[of]
        return remote(dst, dst, self.ysem.at[give, 0, of], self.ysem.at[give, 1, of], slab=self.z * Y + of)

    def _z(self, d, give):
        z, to = self.z, mod(self.z + d, self.nz)
        src = self.out.at[self.y, z] if give else self.sum_y.at[to]
        dst = self.out.at[self.y, z] if give else self.from_z.at[z]
        return remote(src, dst, self.zsem.at[give, 0], self.zsem.at[give, 1], slab=to * Y + self.y)

    def _all_z(self, give):
        blocks = self.from_z.at[pl.ds(0, self.nz - 1)]
        to = mod(self.z + 1, self.nz)
        return remote(blocks, blocks, self.zsem.at[give, 0], self.zsem.at[give, 1], slab=to * Y + self.y)

    def _each_z(self, step):
        def body(d, carry):
            step(d)
            return carry

        lax.fori_loop(1, self.nz, body, 0)

    def start(self):
        for d in range(1, Y):
            when(self._owns(mod(self.y + d, Y)), lambda: self._y(d, 0).start())

    def along_z(self):
        def step():
            for d in range(1, Y):
                self._y_in(d, 0).wait_recv()
            total = self.part[self.y].astype(jnp.float32)
            for d in range(1, Y):
                total = total + self.from_y[mod(self.y + d, Y)].astype(jnp.float32)
            self.sum_y[...] = total.astype(self.sum_y.dtype)
            self._each_z(lambda d: self._z(d, 0).start())

        when(self._owns(self.y), step)

    def hand_out_z(self, finish):
        def step():
            self._all_z(0).wait_recv()
            total = self.sum_y[self.z].astype(jnp.float32)
            for d in range(1, self.nz):
                total = total + self.from_z[mod(self.z + d, self.nz)].astype(jnp.float32)
            self.out[self.y, self.z] = finish(total).astype(self.out.dtype)
            self._each_z(lambda d: self._z(d, 1).start())

        when(self._owns(self.y), step)

    def hand_out_y(self):
        def step():
            self._all_z(1).wait_recv()
            for d in range(1, Y):
                self._y(d, 1).start()

        when(self._owns(self.y), step)

    def end(self):
        for d in range(1, Y):
            when(self._owns(mod(self.y + d, Y)), lambda: self._y_in(d, 1).wait_recv())

    def settle(self):
        for d in range(1, Y):
            when(self._owns(mod(self.y + d, Y)), lambda: self._y(d, 0).wait_send())

        def mine():
            for d in range(1, Y):
                self._y(d, 1).wait_send()

            self._all_z(0).wait_send()
            self._all_z(1).wait_send()

        when(self._owns(self.y), mine)


class TorusGather:
    RELAYED = 6
    NEAR = 5

    @staticmethod
    def scratch(nz):
        return [
            DMA((1,)), DMA((nz, 2)), DMA((3,)), DMA((3,)),
            DMA((1,)), DMA((nz,)), DMA((1,)), DMA((2, nz)), DMA((1,)), DMA((2,)), DMA((3,)),
            DMA((2, 2)), DMA((2, 2)), DMA((2,)), DMA((2,)),
        ]

    def __init__(self, wa, wb, ga, gb, sems):
        self.wa, self.wb, self.ga, self.gb = wa, wb, ga, gb
        (self.az_s, self.az_r, self.ay_s, self.ay_r, self.bz_s, self.bz_r,
         self.by_s, self.by_r, self.bo_s, self.bo_r, self.own_sem,
         self.ly_s, self.ly_r, self.lo_s, self.lo_r) = sems
        self.nz = nz = gb.shape[0]
        self.half = nz // 2
        slab = lax.axis_index("slab")
        self.z, self.y = z, y = slab // Y, mod(slab, Y)
        self.next = mod(z + 1, nz), mod(z + nz - 1, nz)
        self.right, self.left, self.across = mod(y + 1, Y), mod(y + Y - 1, Y), mod(y + 2, Y)
        self.sides = self.right, self.left
        self.parts = (pl.ds(0, self.half), pl.ds(self.half, self.half))
        self.sent = []

    def _go(self, copy):
        copy.start()
        self.sent.append(copy)

    def _landed(self, dst, sem):
        remote(dst, dst, self.own_sem.at[2], sem, slab=self.z * Y + self.right).wait_recv()

    def _pair(self, origin, p):
        return self.ga.at[origin, pl.ds(2 * p, 2)]

    def _a_z(self, origin, p, way):
        block = self._pair(origin, p)
        remote(block, block, self.az_s.at[0], self.az_r.at[origin, p],
               slab=self.next[way] * Y + self.y).start()

    def _b_z(self, origin, src, way):
        remote(src, self.gb.at[origin, self.y], self.bz_s.at[0], self.bz_r.at[origin],
               slab=self.next[way] * Y + self.y).start()

    def _two(self, origin, j):
        return self.gb.at[origin, j, pl.ds(0, 2)]

    def _b_y(self, origin, src):
        for way, to in enumerate(self.sides):
            remote(src, self._two(origin, self.y), self.by_s.at[0], self.by_r.at[way, origin],
                   slab=self.z * Y + to).start()

    def _b_relay(self, origin, t):
        self._landed(self._two(origin, self.left), self.by_r.at[0, origin])
        self._landed(self._two(origin, self.right), self.by_r.at[1, origin])
        turn = 1 - 2 * mod(origin, 2)
        block = self._two(origin, mod(self.y - turn + Y, Y))
        remote(block, block, self.bo_s.at[0], self.bo_r.at[int(t > self.NEAR)],
               slab=self.z * Y + mod(self.y + turn + Y, Y)).start()

    def start(self, meanwhile):
        z, y, wa, wb = self.z, self.y, self.wa, self.wb
        self._b_z(z, wb, 0)
        self._b_z(z, wb, 1)
        for i, to in enumerate((self.right, self.left, self.across)):
            self._go(remote(wa, self.ga.at[z, y], self.ay_s.at[i], self.ay_r.at[i], slab=z * Y + to))
        self.own_a = pltpu.make_async_copy(wa, self.ga.at[z, y], self.own_sem.at[0])
        self.own_a.start()
        self._b_y(z, wb.at[pl.ds(0, 2)])
        self.own_b = pltpu.make_async_copy(wb, self.gb.at[z, y], self.own_sem.at[1])
        self.own_b.start()
        meanwhile()
        odd = mod(y, 2)
        self._landed(self.ga.at[z, y + 1 - 2 * odd], self.ay_r.at[1 - odd])
        self.own_a.wait()
        self._a_z(z, y // 2, 0)
        self._a_z(z, y // 2, 1)
        self._landed(self.ga.at[z, mod(y + Y - 1 + 2 * odd, Y)], self.ay_r.at[odd])
        self._landed(self.ga.at[z, self.across], self.ay_r.at[2])
        self._a_z(z, 1 - y // 2, 0)
        self._a_z(z, 1 - y // 2, 1)

    def step(self, t):
        nz, half, y = self.nz, self.half, self.y
        ways = [(mod(self.z - t + nz, nz), 0, half)]
        if t < half:
            ways.append((mod(self.z + t, nz), 1, half - 1))
        for origin, way, last in ways:
            block = self.gb.at[origin, y]
            self._landed(block, self.bz_r.at[origin])
            if t < last:
                self._b_z(origin, block, way)
        if t > self.RELAYED:
            self._along_y(ways, t)
        for p in (y // 2, 1 - y // 2):
            for origin, way, last in ways:
                self._landed(self._pair(origin, p), self.az_r.at[origin, p])
                if t < last:
                    self._a_z(origin, p, way)
        if t <= self.RELAYED:
            self._along_y(ways, t)
        if t > 1:
            self._b_relay(mod(self.z - t + 2 + nz, nz), t - 2)
            if t > 2:
                self._b_relay(mod(self.z + t - 2, nz), t - 2)

    def _along_y(self, ways, t):
        for origin, _, _ in ways:
            two = self._two(origin, self.y)
            self._b_y(origin, two)
            if t > self.RELAYED:
                remote(two, two, self.bo_s.at[0], self.bo_r.at[1],
                       slab=self.z * Y + self.across).start()

    def near_landed(self):
        self._landed(self.gb.at[pl.ds(0, 2 * self.NEAR + 1), 0, pl.ds(0, 2)], self.bo_r.at[0])

    def far_landed(self):
        for t in range(self.RELAYED + 1, self.half + 1):
            for origin in (mod(self.z - t + self.nz, self.nz), mod(self.z + t, self.nz))[: 1 + (t < self.half)]:
                self._landed(self._two(origin, self.left), self.by_r.at[0, origin])
                self._landed(self._two(origin, self.right), self.by_r.at[1, origin])
        self._landed(self.gb.at[pl.ds(0, self.nz - 2 * self.NEAR - 1), 0, pl.ds(0, 2)], self.bo_r.at[1])

    def _late(self, part, j):
        return self.gb.at[self.parts[part], j, 2]

    def late_start(self, turn):
        for way in range(2):
            part = way if turn == 0 else 1 - way
            block = self._late(part, self.y)
            self._go(remote(block, block, self.ly_s.at[way, part], self.ly_r.at[way, part],
                            slab=self.z * Y + self.sides[way]))

    def late_relay(self):
        for way in range(2):
            block = self._late(way, self.sides[1 - way])
            self._landed(block, self.ly_r.at[way, way])
            self._go(remote(block, block, self.lo_s.at[way], self.lo_r.at[way], slab=self.z * Y + self.sides[way]))

    def late_end(self):
        for way in range(2):
            self._landed(self._late(1 - way, self.sides[1 - way]), self.ly_r.at[way, 1 - way])
        for way in range(2):
            self._landed(self._late(way, self.across), self.lo_r.at[way])

    def settle(self):
        nz, one, two = self.nz, pl.ds(0, 1), pl.ds(0, 2)
        for block, sem in (
            (self.ga.at[pl.ds(0, nz - 1)], self.az_s),
            (self.gb.at[pl.ds(0, nz - 1), one], self.bz_s),
            (self.gb.at[:, two, two], self.by_s),
            (self.gb.at[:, one, two], self.bo_s),
        ):
            remote(block, block, sem.at[0], self.own_sem.at[2], slab=self.z * Y + self.right).wait_send()
        for copy in self.sent:
            copy.wait_send()


def row_scale(values):
    return lax.rsqrt(jnp.mean(values * values, axis=-1, keepdims=True) + norm_eps)


OPERANDS = 15
FETCH_ORDER = (2, 3, 4, 5, 0, 1, 6, 7, 8, 9, 10, 11, 12, 13, 14)
QKV_SEMS = 15


def whole_kernel(*refs):
    f32, bf16 = jnp.float32, jnp.bfloat16

    def take(count):
        nonlocal refs
        some, refs = refs[:count], refs[count:]
        return some

    fetched = take(OPERANDS)
    out, text_final = take(2)
    held = take(OPERANDS)
    video, text, wq, wk, wv, wo, twq, twk, twv, qg, kg, tqg, tkg, mask, window = held
    (fetch_sem, wb, ga, gb, normed, tnormed, tweight, text_part, text_rows, acc) = take(10)
    (q, k, v, num, den, num_out, num_in, den_in, attn, live, tsum_part, text_out) = take(12)
    (part, pair, far, near) = take(4)
    qkv = TorusGather(wq, wb, ga, gb, take(QKV_SEMS))
    text_sum = SlabSum(text_part, text_rows, take(5))
    attn_sum = SlabSum(tsum_part, text_out, take(5))
    q_s, q_r, k_s, k_r, v_s, v_r, n_s, n_r, d_s, d_r = take(10)
    pair_s, pair_r, far_s, far_r, near_s, near_r = take(6)

    nz = gb.shape[0]
    nx = part.shape[0]
    slab, head = lax.axis_index("slab"), lax.axis_index("head")
    slab_count = lax.axis_size("slab")
    z, y = slab // Y, mod(slab, Y)
    row, column = slab // COLUMN_TILES, mod(slab, COLUMN_TILES)
    above, below = mod(slab + slab_count - COLUMN_TILES, slab_count), mod(slab + COLUMN_TILES, slab_count)
    has_left, has_right = column > 0, column < COLUMN_TILES - 1
    has_above, has_below = row > 0, row < slab_count // COLUMN_TILES - 1
    jump_left, jump_right = has_left & (y == 0), has_right & (y == Y - 1)
    x, core = head // 2, mod(head, 2)
    x_right, x_left, x_far = mod(x + 1, nx), mod(x + nx - 1, nx), mod(x + 2, nx)
    other, right, left = x * 2 + 1 - core, x_right * 2 + core, x_left * 2 + core
    depth, width = wq.shape
    heads = width // HEAD_SIZE
    tokens, model = video.shape
    txt = text.shape[0]
    score_scale = 1.0 / math.sqrt(HEAD_SIZE)
    steps = nz // 2
    nt = (((1,), (1,)), ((), ()))

    fetches = [
        pltpu.make_async_copy(src, dst, fetch_sem.at[i]) for i, (src, dst) in enumerate(zip(fetched, held))
    ]
    for i in FETCH_ORDER:
        fetches[i].start()

    barrier, peers = hello_slab(z, y, nz)
    greet((), (other, right, left))

    @pl.when(jump_left)
    def _():
        greet((slab - 1,))

    @pl.when(jump_right)
    def _():
        greet((slab + 1,))

    for i in FETCH_ORDER[:4]:
        fetches[i].wait()
    for i, weight in enumerate((wk, wv, wo)):
        wb[i] = weight[...]
    pl.semaphore_wait(barrier, peers + 3 + jump_left.astype(jnp.int32) + jump_right.astype(jnp.int32))
    def normalize_video(i, carry):
        at = pl.ds(pl.multiple_of(i * 16, 16), 16)
        values = video[at, :].astype(f32)
        center = values - jnp.mean(values, axis=-1, keepdims=True)
        normed[at, :] = (center * row_scale(center)).astype(bf16)
        return carry

    blocks = tokens // 16
    early = blocks // 4

    def first_rows():
        fetches[0].wait()
        lax.fori_loop(0, early, normalize_video, 0)

    qkv.start(first_rows)

    span = tweight.shape[0]
    aligned = jnp.minimum(slab * depth // LANES * LANES, model - span)
    aligned = pl.multiple_of(aligned, LANES)
    offset = pl.multiple_of(slab * depth - aligned, 16)
    share = nz // heads

    def fill_text_weights():
        tweight[...] = jnp.zeros_like(tweight)
        for i, weight in enumerate((twq, twk, twv)):
            tweight[pl.ds(offset, depth), i * width : (i + 1) * width] = weight[...]

    def normalize_text(i, carry):
        at = pl.ds(pl.multiple_of(i * 16, 16), 16)
        values = text[at, :].astype(f32)
        mean = jnp.mean(values, axis=-1, keepdims=True)
        scale = row_scale(values - mean)
        columns = text[at, pl.ds(aligned, span)].astype(f32)
        tnormed[at, :] = ((columns - mean) * scale).astype(bf16)
        return carry

    def multiply_text():
        for i in range(3):
            product = jnp.dot(
                tnormed[...], tweight[:, i * width : (i + 1) * width], preferred_element_type=f32
            ).astype(bf16)
            for h in range(heads):
                block = product[:, h * HEAD_SIZE : (h + 1) * HEAD_SIZE]
                text_part[i, h * share : (h + 1) * share] = block.reshape(share, *text_part.shape[2:])

    def finish_text(total):
        gain = jnp.where(y == 0, tqg[...], tkg[...])
        return jnp.where(y == 2, total, total * row_scale(total) * gain)

    for t in range(1, steps + 1):
        qkv.step(t)
        if t == 1:
            for i in FETCH_ORDER[5:]:
                fetches[i].wait()
            fill_text_weights()
            lax.fori_loop(0, txt // 32, normalize_text, 0)
        if t == 2:
            lax.fori_loop(txt // 32, txt // 16, normalize_text, 0)
            multiply_text()
            text_sum.start()
        if t == 4:
            text_sum.along_z()
        if t == 7:
            text_sum.hand_out_z(finish_text)
        if t > 2:
            rest, steps_left = blocks - early, steps - 2
            lax.fori_loop(
                early + (t - 3) * rest // steps_left, early + (t - 2) * rest // steps_left, normalize_video, 0
            )

    qkv.own_b.wait()
    qkv.late_start(0)

    acc[...] = jnp.zeros_like(acc)
    group = 4 if nz % 4 == 0 else nz
    span = group * Y * depth

    def multiply_query(c, carry):
        rows = normed[:, pl.ds(pl.multiple_of(c * span, span), span)]
        acc[:, :width] += jnp.dot(
            rows, ga[pl.ds(c * group, group)].reshape(span, width), preferred_element_type=f32
        )
        return carry

    lax.fori_loop(0, nz // group, multiply_query, 0)
    rows_out = []
    for h in range(heads):
        values = acc[:, h * HEAD_SIZE : (h + 1) * HEAD_SIZE]
        q[0, h] = (values * row_scale(values) * qg[...]).astype(bf16)
        to_below = remote(q.at[0, h], q.at[1, h], q_s.at[0, h], q_r.at[0, h], slab=below)
        to_above = remote(q.at[0, h], q.at[2, h], q_s.at[1, h], q_r.at[1, h], slab=above)
        to_below.start()
        to_above.start()
        rows_out.append((to_below, to_above))

    pair_depth = 2 * Y * depth

    def multiply_rest(i, carry):
        at = mod(z // 2 + i + nz // 2 - 2, nz // 2)
        rows = normed[:, pl.ds(pl.multiple_of(at * pair_depth, pair_depth), pair_depth)]
        for j in range(2):
            acc[:, (j + 1) * width : (j + 2) * width] += jnp.dot(
                rows, gb[pl.ds(at * 2, 2), :, j].reshape(pair_depth, width), preferred_element_type=f32
            )
        return carry

    qkv.near_landed()
    lax.fori_loop(0, 5, multiply_rest, 0)
    qkv.far_landed()
    lax.fori_loop(5, nz // 2, multiply_rest, 0)
    text_sum.hand_out_y()

    to_right, to_left = [], []
    for h in range(heads):
        values = acc[:, width + h * HEAD_SIZE : width + (h + 1) * HEAD_SIZE]
        k[0, h] = (values * row_scale(values) * kg[...]).astype(bf16)
        v[0, h] = acc[:, 2 * width + h * HEAD_SIZE : 2 * width + (h + 1) * HEAD_SIZE].T.astype(bf16)
        right_now = [
            remote(k.at[0, h], k.at[1, h], k_s.at[0, h], k_r.at[0, h], slab=slab + 1),
            remote(v.at[0, h], v.at[1, h], v_s.at[0, h], v_r.at[0, h], slab=slab + 1),
        ]
        left_now = [
            remote(k.at[0, h], k.at[2, h], k_s.at[1, h], k_r.at[1, h], slab=slab - 1),
            remote(v.at[0, h], v.at[2, h], v_s.at[1, h], v_r.at[1, h], slab=slab - 1),
        ]
        to_right += right_now
        to_left += left_now

        def start_all(copies):
            for copy in copies:
                copy.start()

        pl.when(has_right)(functools.partial(start_all, right_now))
        pl.when(has_left)(functools.partial(start_all, left_now))

    qkv.late_start(1)

    @pl.when(jnp.logical_not(has_left))
    def _():
        k[1] = jnp.zeros_like(k[1])
        v[1] = jnp.zeros_like(v[1])

    @pl.when(jnp.logical_not(has_right))
    def _():
        k[2] = jnp.zeros_like(k[2])
        v[2] = jnp.zeros_like(v[2])

    def scores(keys, queries):
        return jnp.exp(lax.dot_general(keys, queries, nt, preferred_element_type=f32) * score_scale)

    def weigh(values, e):
        return jnp.dot(values, e.astype(bf16), preferred_element_type=f32)

    def column_sum(e):
        return jnp.sum(e, axis=0, keepdims=True)

    tsum_part[heads] = jnp.zeros_like(tsum_part[heads])
    for h in range(heads):
        e = scores(k[0, h], q[0, h])
        num[0, h] = weigh(v[0, h], e)
        den[0, h, 0:1] = column_sum(e)

    for h in range(heads):
        for copy in rows_out[h]:
            copy.wait_recv()

        def neighbour(tile, carry, h=h):
            e = scores(k[0, h], q[tile, h])
            num[tile, h] = weigh(v[0, h], e)
            den[tile, h] = jnp.broadcast_to(column_sum(e), den.shape[2:])
            return carry

        lax.fori_loop(1, 3, neighbour, 0)
    qkv.late_relay()

    def has_side(slot):
        return column != (COLUMN_TILES - 1) * (slot - 1)

    def add_side(slot, tile, h):
        reach = jnp.where(has_side(slot), 1.0, 0.0)
        e = scores(k[slot, h], q[tile, h])
        e = e * (reach * window[1, head * heads + h].astype(f32))
        num[tile, h] += weigh(v[slot, h], e)
        den[tile, h, 0:1] += column_sum(e)

    def text_phase():
        live[...] = jnp.broadcast_to(mask[...].astype(f32), live.shape).T
        is_first = jnp.where(slab == 0, 1.0, 0.0)
        text_sum.end()

        def text_head(i, h):
            return text_rows[i, h * share : (h + 1) * share].reshape(txt, HEAD_SIZE)

        text_values = []
        for h in range(heads):
            tq = text_head(0, h)
            text_values.append(text_head(2, h).astype(f32).T.astype(bf16))
            e = scores(k[0, h], tq)
            own = scores(text_head(1, h), tq) * live[...] * is_first
            total = weigh(v[0, h], e) + weigh(text_values[h], own)
            tsum_part[h] = total.reshape(tsum_part.shape[1:])
            tsum_part[heads, 0, h : h + 1] = column_sum(e) + column_sum(own)
        attn_sum.start()

        live_wide = jnp.concatenate([live[...]] * (tokens // txt), axis=1)
        for h in range(heads):
            e = scores(text_head(1, h), q[0, h]) * live_wide
            num[0, h] += weigh(text_values[h], e)
            den[0, h, 0:1] += column_sum(e)

    back = []
    for h in range(heads):

        for i in range(2):
            slot = 1 + mod(i + jump_left.astype(jnp.int32), 2)

            @pl.when(has_side(slot))
            def _():
                for sem, dst in ((k_r, k), (v_r, v)):
                    block = dst.at[slot, h]
                    arrived = sem.at[slot - 1, h]
                    remote(block, block, arrived, arrived, slab=slab + 2 * slot - 3).wait_recv()

            def side(tile, carry, h=h, slot=slot):
                add_side(slot, tile, h)
                return carry

            lax.fori_loop(1, 3, side, 0)
        for tile in (1, 2):
            num_out[tile - 1, h] = num[tile, h].astype(bf16)
        now = [
            remote(num_out.at[0, h], num_in.at[1, h], n_s.at[1, h], n_r.at[1, h], slab=above),
            remote(num_out.at[1, h], num_in.at[0, h], n_s.at[0, h], n_r.at[0, h], slab=below),
            remote(den.at[1, h], den_in.at[1, h], d_s.at[1, h], d_r.at[1, h], slab=above),
            remote(den.at[2, h], den_in.at[0, h], d_s.at[0, h], d_r.at[0, h], slab=below),
        ]
        for copy in now:
            copy.start()
        back.append(now)
        if h == 0:
            text_phase()

    def own_side(i, carry):
        add_side(1 + i % 2, 0, i // 2)
        return carry

    lax.fori_loop(0, 2 * heads, own_side, 0)
    attn_sum.along_z()
    text_sum.settle()
    for h in range(heads):
        for copy in back[h]:
            copy.wait_recv()
        total, under = num[0, h], den[0, h, 0:1]
        for side_row, exists in ((0, has_above), (1, has_below)):
            reach = jnp.where(exists, 1.0, 0.0) * window[0, head * heads + h].astype(f32)
            total = total + num_in[side_row, h].astype(f32) * reach
            under = under + den_in[side_row, h, 0:1] * reach
        attn[:, h * HEAD_SIZE : (h + 1) * HEAD_SIZE] = (total / under).T.astype(bf16)

    qkv.late_end()
    order = (x_far, x_right, x_left, x)
    rows = tokens // nx
    halves = part.shape[2]
    pairs = []

    def send_pair(xx):
        mine = attn[pl.ds(pl.multiple_of(xx * rows, 16), rows), :]
        for half in range(halves):
            weight = gb[half * nz // halves : (half + 1) * nz // halves, :, 2].reshape(model // halves, width)
            product = lax.dot_general(mine, weight, nt, preferred_element_type=f32).astype(bf16)
            for c in range(2):
                part[xx, c, half] = product[c * rows // 2 : (c + 1) * rows // 2]
        pairs.append(remote(part.at[xx, 1 - core], pair.at[xx], pair_s.at[xx], pair_r.at[xx], head=other))
        pairs[-1].start()

    def pair_sum(xx):
        remote(pair.at[xx], pair.at[xx], pair_s.at[xx], pair_r.at[xx], head=other).wait_recv()
        pair[xx] = (pair[xx].astype(f32) + part[xx, core].astype(f32)).astype(bf16)

    send_pair(x_far)
    send_pair(x_right)
    send_pair(x_left)
    pair_sum(x_far)
    fars = [
        remote(pair.at[x_far, 0], far.at[0], far_s.at[0], far_r.at[0], head=right),
        remote(pair.at[x_far, 1], far.at[1], far_s.at[1], far_r.at[1], head=left),
    ]
    for copy in fars:
        copy.start()
    pair_sum(x_right)
    pair_sum(x_left)
    nears = [
        remote(pair.at[x_right, 1], near.at[0, 1], near_s.at[0, 1], near_r.at[0, 1], head=right),
        remote(pair.at[x_left, 0], near.at[1, 0], near_s.at[1, 0], near_r.at[1, 0], head=left),
        remote(pair.at[x_right, 0], near.at[0, 0], near_s.at[0, 0], near_r.at[0, 0], head=right),
        remote(pair.at[x_left, 1], near.at[1, 1], near_s.at[1, 1], near_r.at[1, 1], head=left),
    ]
    nears[0].start()
    nears[1].start()
    send_pair(x)
    attn_sum.hand_out_z(lambda total: total)
    pair_sum(x)
    fars[0].wait_recv()
    pair[x_right, 0] = (pair[x_right, 0].astype(f32) + far[0].astype(f32)).astype(bf16)
    nears[2].start()
    fars[1].wait_recv()
    pair[x_left, 1] = (pair[x_left, 1].astype(f32) + far[1].astype(f32)).astype(bf16)
    nears[3].start()
    qkv.settle()
    attn_sum.hand_out_y()
    for copy in (*sum(rows_out, ()), *sum(back, []), *pairs):
        copy.wait_send()

    @pl.when(has_right)
    def _():
        for copy in to_right:
            copy.wait_send()

    @pl.when(has_left)
    def _():
        for copy in to_left:
            copy.wait_send()

    for copy in nears:
        copy.wait_recv()
    for half in range(halves):
        at = half * model // halves
        out[:, at : at + model // halves] = (
            pair[x, half].astype(f32) + near[0, half].astype(f32) + near[1, half].astype(f32)
        ).astype(bf16)

    attn_sum.end()
    for h in range(heads):
        total = text_out[h].reshape(HEAD_SIZE, txt) / text_out[heads, 0, h : h + 1]
        text_final[:, h * HEAD_SIZE : (h + 1) * HEAD_SIZE] = total.T.astype(bf16)
    attn_sum.settle()
    for copy in (*fars, *nears):
        copy.wait_send()


def run_whole(slab_count, head_count, operands):
    video, text, wq = operands[0], operands[1], operands[2]
    depth, width = wq.shape
    tokens, model = video.shape
    txt = text.shape[0]
    heads = width // HEAD_SIZE
    nz, nx = slab_count // Y, head_count // 2
    rows = tokens // head_count
    bf16, f32 = jnp.bfloat16, jnp.float32
    text_block = jax.ShapeDtypeStruct((3, nz, txt * heads // nz, HEAD_SIZE), bf16)
    sum_block = jax.ShapeDtypeStruct((heads + 1, nz, HEAD_SIZE // nz, txt), f32)
    half = model // 2
    vmem = pl.BlockSpec(memory_space=VMEM)
    return pl.pallas_call(
        whole_kernel,
        out_shape=(
            jax.ShapeDtypeStruct((rows, model), bf16),
            jax.ShapeDtypeStruct((txt, width), bf16),
        ),
        in_specs=[pl.BlockSpec(memory_space=pltpu.HBM)] * OPERANDS,
        out_specs=(vmem, vmem),
        scratch_shapes=[
            *(VMEM(a.shape, a.dtype) for a in operands[:-1]),
            pltpu.SMEM(operands[-1].shape, operands[-1].dtype),
            DMA((OPERANDS,)),
            VMEM((3, depth, width), bf16),
            VMEM((nz, Y, depth, width), bf16),
            VMEM((nz, Y, 3, depth, width), bf16),
            VMEM((tokens, model), bf16),
            VMEM((txt, 2 * LANES), bf16),
            VMEM((2 * LANES, 3 * width), bf16),
            VMEM(text_block.shape, bf16),
            VMEM(text_block.shape, bf16),
            VMEM((tokens, 3 * width), f32),
            VMEM((3, heads, tokens, HEAD_SIZE), bf16),
            VMEM((3, heads, tokens, HEAD_SIZE), bf16),
            VMEM((3, heads, HEAD_SIZE, tokens), bf16),
            VMEM((3, heads, HEAD_SIZE, tokens), f32),
            VMEM((3, heads, 8, tokens), f32),
            VMEM((2, heads, HEAD_SIZE, tokens), bf16),
            VMEM((2, heads, HEAD_SIZE, tokens), bf16),
            VMEM((2, heads, 8, tokens), f32),
            VMEM((tokens, width), bf16),
            VMEM((txt, txt), f32),
            VMEM(sum_block.shape, f32),
            VMEM(sum_block.shape, f32),
            VMEM((nx, 2, 2, rows, half), bf16),
            VMEM((nx, 2, rows, half), bf16),
            VMEM((2, rows, half), bf16),
            VMEM((2, 2, rows, half), bf16),
            *TorusGather.scratch(nz),
            *SlabSum.scratch(text_block),
            *SlabSum.scratch(sum_block),
            *[DMA((2, heads))] * 10,
            DMA((nx,)), DMA((nx,)), DMA((2,)), DMA((2,)), DMA((2, 2)), DMA((2, 2)),
        ],
        compiler_params=pltpu.CompilerParams(
            collective_id=0, has_side_effects=True, vmem_limit_bytes=32 * MIB
        ),
        name="whole",
    )(*(pltpu.with_memory_space_constraint(a, pltpu.HBM) for a in operands))


def on_device(
    video_token_state,
    text_tokens,
    text_mask,
    head_window,
    video_query_weight,
    video_key_weight,
    video_value_weight,
    wout_video,
    wquery_text,
    wkey_text,
    wvalue_text,
    video_query_gain,
    video_key_gain,
    qgain_text,
    kgain_text,
):
    operands = (
        video_token_state, text_tokens,
        video_query_weight, video_key_weight, video_value_weight, wout_video.T,
        wquery_text, wkey_text, wvalue_text,
        *(row.reshape(1, -1) for row in (video_query_gain, video_key_gain, qgain_text, kgain_text, text_mask)),
        head_window.T,
    )
    return run_whole(lax.axis_size("slab"), lax.axis_size("head"), operands)


def solution(mesh):
    return jax.shard_map(
        on_device,
        mesh=mesh,
        in_specs=(
            P("slab", None),
            P(),
            P(),
            P(),
            P("slab", "head"),
            P("slab", "head"),
            P("slab", "head"),
            P("head", "slab"),
            P("slab", "head"),
            P("slab", "head"),
            P("slab", "head"),
            P(),
            P(),
            P(),
            P(),
        ),
        out_specs=(P(("slab", "head"), None), P(None, "head")),
        check_vma=False,
    )
```

```python
import functools
import math

import jax
import jax.numpy as jnp
from jax import lax
from jax.experimental import pallas as pl
from jax.experimental.pallas import tpu as pltpu
from jax.sharding import PartitionSpec as P

HEAD_SIZE = 128
COLUMN_TILES = 8
Y = 4
MIB = 1 << 20
LANES = 128
VMEM = pltpu.VMEM
DMA = pltpu.SemaphoreType.DMA

norm_eps = 1e-06


def mod(a, n):
    return lax.rem(a, jnp.int32(n))


def remote(src, dst, send, recv, **device):
    return pltpu.make_async_remote_copy(
        src_ref=src, dst_ref=dst, send_sem=send, recv_sem=recv,
        device_id=device, device_id_type=pl.DeviceIdType.MESH,
    )


def greet(slabs=(), heads=()):
    barrier = pltpu.get_barrier_semaphore()
    for slab in slabs:
        pl.semaphore_signal(barrier, 1, device_id={"slab": slab}, device_id_type=pl.DeviceIdType.MESH)
    for head in heads:
        pl.semaphore_signal(barrier, 1, device_id={"head": head}, device_id_type=pl.DeviceIdType.MESH)
    return barrier


def when(condition, step):
    if isinstance(condition, bool):
        if condition:
            step()
    else:
        pl.when(condition)(step)


def hello_slab(z, y, nz):
    barrier = pltpu.get_barrier_semaphore()

    def greet_one(slab):
        pl.semaphore_signal(barrier, 1, device_id={"slab": slab}, device_id_type=pl.DeviceIdType.MESH)

    for d in range(1, Y):
        greet_one(z * Y + mod(y + d, Y))

    def body(d, carry):
        greet_one(mod(z + d, nz) * Y + y)
        return carry

    lax.fori_loop(1, nz, body, 0)
    return barrier, Y - 1 + nz - 1


class SlabSum:
    @staticmethod
    def scratch(block):
        owners, nz, rows, lanes = block.shape
        return [
            VMEM((Y, nz, rows, lanes), block.dtype),
            VMEM((nz, rows, lanes), block.dtype),
            VMEM((nz, rows, lanes), block.dtype),
            DMA((2, 2, Y)),
            DMA((2, 2)),
        ]

    def __init__(self, part, out, scratch):
        self.part, self.out = part, out
        self.from_y, self.sum_y, self.from_z, self.ysem, self.zsem = scratch
        self.owners, self.nz = part.shape[:2]
        slab = lax.axis_index("slab")
        self.z, self.y = slab // Y, mod(slab, Y)

    def _owns(self, y):
        return True if self.owners == Y else y < self.owners

    def _y(self, d, give):
        y, to = self.y, mod(self.y + d, Y)
        src = self.out.at[y] if give else self.part.at[to]
        dst = self.out.at[y] if give else self.from_y.at[y]
        return remote(src, dst, self.ysem.at[give, 0, to], self.ysem.at[give, 1, y], slab=self.z * Y + to)

    def _y_in(self, d, give):
        of = mod(self.y + d, Y)
        dst = self.out.at[of] if give else self.from_y.at[of]
        return remote(dst, dst, self.ysem.at[give, 0, of], self.ysem.at[give, 1, of], slab=self.z * Y + of)

    def _z(self, d, give):
        z, to = self.z, mod(self.z + d, self.nz)
        src = self.out.at[self.y, z] if give else self.sum_y.at[to]
        dst = self.out.at[self.y, z] if give else self.from_z.at[z]
        return remote(src, dst, self.zsem.at[give, 0], self.zsem.at[give, 1], slab=to * Y + self.y)

    def _all_z(self, give):
        blocks = self.from_z.at[pl.ds(0, self.nz - 1)]
        to = mod(self.z + 1, self.nz)
        return remote(blocks, blocks, self.zsem.at[give, 0], self.zsem.at[give, 1], slab=to * Y + self.y)

    def _each_z(self, step):
        def body(d, carry):
            step(d)
            return carry

        lax.fori_loop(1, self.nz, body, 0)

    def start(self):
        for d in range(1, Y):
            when(self._owns(mod(self.y + d, Y)), lambda: self._y(d, 0).start())

    def along_z(self):
        def step():
            for d in range(1, Y):
                self._y_in(d, 0).wait_recv()
            total = self.part[self.y].astype(jnp.float32)
            for d in range(1, Y):
                total = total + self.from_y[mod(self.y + d, Y)].astype(jnp.float32)
            self.sum_y[...] = total.astype(self.sum_y.dtype)
            self._each_z(lambda d: self._z(d, 0).start())

        when(self._owns(self.y), step)

    def hand_out_z(self, finish):
        def step():
            self._all_z(0).wait_recv()
            total = self.sum_y[self.z].astype(jnp.float32)
            for d in range(1, self.nz):
                total = total + self.from_z[mod(self.z + d, self.nz)].astype(jnp.float32)
            self.out[self.y, self.z] = finish(total).astype(self.out.dtype)
            self._each_z(lambda d: self._z(d, 1).start())

        when(self._owns(self.y), step)

    def hand_out_y(self):
        def step():
            self._all_z(1).wait_recv()
            for d in range(1, Y):
                self._y(d, 1).start()

        when(self._owns(self.y), step)

    def end(self):
        for d in range(1, Y):
            when(self._owns(mod(self.y + d, Y)), lambda: self._y_in(d, 1).wait_recv())

    def settle(self):
        for d in range(1, Y):
            when(self._owns(mod(self.y + d, Y)), lambda: self._y(d, 0).wait_send())

        def mine():
            for d in range(1, Y):
                self._y(d, 1).wait_send()

            self._all_z(0).wait_send()
            self._all_z(1).wait_send()

        when(self._owns(self.y), mine)


class TorusGather:
    RELAYED = 6
    NEAR = 5

    @staticmethod
    def scratch(nz):
        return [
            DMA((1,)), DMA((nz, 2)), DMA((3,)), DMA((3,)),
            DMA((1,)), DMA((nz,)), DMA((1,)), DMA((2, nz)), DMA((1,)), DMA((2,)), DMA((3,)),
            DMA((2, 2)), DMA((2, 2)), DMA((2,)), DMA((2,)),
        ]

    def __init__(self, wa, wb, ga, gb, sems):
        self.wa, self.wb, self.ga, self.gb = wa, wb, ga, gb
        (self.az_s, self.az_r, self.ay_s, self.ay_r, self.bz_s, self.bz_r,
         self.by_s, self.by_r, self.bo_s, self.bo_r, self.own_sem,
         self.ly_s, self.ly_r, self.lo_s, self.lo_r) = sems
        self.nz = nz = gb.shape[0]
        self.half = nz // 2
        slab = lax.axis_index("slab")
        self.z, self.y = z, y = slab // Y, mod(slab, Y)
        self.next = mod(z + 1, nz), mod(z + nz - 1, nz)
        self.right, self.left, self.across = mod(y + 1, Y), mod(y + Y - 1, Y), mod(y + 2, Y)
        self.sides = self.right, self.left
        self.parts = (pl.ds(0, self.half), pl.ds(self.half, self.half))
        self.sent = []

    def _go(self, copy):
        copy.start()
        self.sent.append(copy)

    def _landed(self, dst, sem):
        remote(dst, dst, self.own_sem.at[2], sem, slab=self.z * Y + self.right).wait_recv()

    def _pair(self, origin, p):
        return self.ga.at[origin, pl.ds(2 * p, 2)]

    def _a_z(self, origin, p, way):
        block = self._pair(origin, p)
        remote(block, block, self.az_s.at[0], self.az_r.at[origin, p],
               slab=self.next[way] * Y + self.y).start()

    def _b_z(self, origin, src, way):
        remote(src, self.gb.at[origin, self.y], self.bz_s.at[0], self.bz_r.at[origin],
               slab=self.next[way] * Y + self.y).start()

    def _two(self, origin, j):
        return self.gb.at[origin, j, pl.ds(0, 2)]

    def _b_y(self, origin, src):
        for way, to in enumerate(self.sides):
            remote(src, self._two(origin, self.y), self.by_s.at[0], self.by_r.at[way, origin],
                   slab=self.z * Y + to).start()

    def _b_relay(self, origin, t):
        self._landed(self._two(origin, self.left), self.by_r.at[0, origin])
        self._landed(self._two(origin, self.right), self.by_r.at[1, origin])
        turn = 1 - 2 * mod(origin, 2)
        block = self._two(origin, mod(self.y - turn + Y, Y))
        remote(block, block, self.bo_s.at[0], self.bo_r.at[int(t > self.NEAR)],
               slab=self.z * Y + mod(self.y + turn + Y, Y)).start()

    def start(self, meanwhile):
        z, y, wa, wb = self.z, self.y, self.wa, self.wb
        self._b_z(z, wb, 0)
        self._b_z(z, wb, 1)
        for i, to in enumerate((self.right, self.left, self.across)):
            self._go(remote(wa, self.ga.at[z, y], self.ay_s.at[i], self.ay_r.at[i], slab=z * Y + to))
        self.own_a = pltpu.make_async_copy(wa, self.ga.at[z, y], self.own_sem.at[0])
        self.own_a.start()
        self._b_y(z, wb.at[pl.ds(0, 2)])
        self.own_b = pltpu.make_async_copy(wb, self.gb.at[z, y], self.own_sem.at[1])
        self.own_b.start()
        meanwhile()
        odd = mod(y, 2)
        self._landed(self.ga.at[z, y + 1 - 2 * odd], self.ay_r.at[1 - odd])
        self.own_a.wait()
        self._a_z(z, y // 2, 0)
        self._a_z(z, y // 2, 1)
        self._landed(self.ga.at[z, mod(y + Y - 1 + 2 * odd, Y)], self.ay_r.at[odd])
        self._landed(self.ga.at[z, self.across], self.ay_r.at[2])
        self._a_z(z, 1 - y // 2, 0)
        self._a_z(z, 1 - y // 2, 1)

    def step(self, t):
        nz, half, y = self.nz, self.half, self.y
        ways = [(mod(self.z - t + nz, nz), 0, half)]
        if t < half:
            ways.append((mod(self.z + t, nz), 1, half - 1))
        for origin, way, last in ways:
            block = self.gb.at[origin, y]
            self._landed(block, self.bz_r.at[origin])
            if t < last:
                self._b_z(origin, block, way)
        if t > self.RELAYED:
            self._along_y(ways, t)
        for p in (y // 2, 1 - y // 2):
            for origin, way, last in ways:
                self._landed(self._pair(origin, p), self.az_r.at[origin, p])
                if t < last:
                    self._a_z(origin, p, way)
        if t <= self.RELAYED:
            self._along_y(ways, t)
        if t > 1:
            self._b_relay(mod(self.z - t + 2 + nz, nz), t - 2)
            if t > 2:
                self._b_relay(mod(self.z + t - 2, nz), t - 2)

    def _along_y(self, ways, t):
        for origin, _, _ in ways:
            two = self._two(origin, self.y)
            self._b_y(origin, two)
            if t > self.RELAYED:
                remote(two, two, self.bo_s.at[0], self.bo_r.at[1],
                       slab=self.z * Y + self.across).start()

    def near_landed(self):
        self._landed(self.gb.at[pl.ds(0, 2 * self.NEAR + 1), 0, pl.ds(0, 2)], self.bo_r.at[0])

    def far_landed(self):
        for t in range(self.RELAYED + 1, self.half + 1):
            for origin in (mod(self.z - t + self.nz, self.nz), mod(self.z + t, self.nz))[: 1 + (t < self.half)]:
                self._landed(self._two(origin, self.left), self.by_r.at[0, origin])
                self._landed(self._two(origin, self.right), self.by_r.at[1, origin])
        self._landed(self.gb.at[pl.ds(0, self.nz - 2 * self.NEAR - 1), 0, pl.ds(0, 2)], self.bo_r.at[1])

    def _late(self, part, j):
        return self.gb.at[self.parts[part], j, 2]

    def late_start(self, turn):
        for way in range(2):
            part = way if turn == 0 else 1 - way
            block = self._late(part, self.y)
            self._go(remote(block, block, self.ly_s.at[way, part], self.ly_r.at[way, part],
                            slab=self.z * Y + self.sides[way]))

    def late_relay(self):
        for way in range(2):
            block = self._late(way, self.sides[1 - way])
            self._landed(block, self.ly_r.at[way, way])
            self._go(remote(block, block, self.lo_s.at[way], self.lo_r.at[way], slab=self.z * Y + self.sides[way]))

    def late_end(self):
        for way in range(2):
            self._landed(self._late(1 - way, self.sides[1 - way]), self.ly_r.at[way, 1 - way])
        for way in range(2):
            self._landed(self._late(way, self.across), self.lo_r.at[way])

    def settle(self):
        nz, one, two = self.nz, pl.ds(0, 1), pl.ds(0, 2)
        for block, sem in (
            (self.ga.at[pl.ds(0, nz - 1)], self.az_s),
            (self.gb.at[pl.ds(0, nz - 1), one], self.bz_s),
            (self.gb.at[:, two, two], self.by_s),
            (self.gb.at[:, one, two], self.bo_s),
        ):
            remote(block, block, sem.at[0], self.own_sem.at[2], slab=self.z * Y + self.right).wait_send()
        for copy in self.sent:
            copy.wait_send()


def row_scale(values):
    return lax.rsqrt(jnp.mean(values * values, axis=-1, keepdims=True) + norm_eps)


OPERANDS = 15
FETCH_ORDER = (2, 3, 4, 5, 0, 1, 6, 7, 8, 9, 10, 11, 12, 13, 14)
QKV_SEMS = 15


def whole_kernel(*refs):
    f32, bf16 = jnp.float32, jnp.bfloat16

    def take(count):
        nonlocal refs
        some, refs = refs[:count], refs[count:]
        return some

    fetched = take(OPERANDS)
    out, text_final = take(2)
    held = take(OPERANDS)
    video, text, wq, wk, wv, wo, twq, twk, twv, qg, kg, tqg, tkg, mask, window = held
    (fetch_sem, wb, ga, gb, normed, tnormed, tweight, text_part, text_rows, acc) = take(10)
    (q, k, v, num, den, num_out, num_in, den_in, attn, live, tsum_part, text_out) = take(12)
    (part, pair, far, near) = take(4)
    qkv = TorusGather(wq, wb, ga, gb, take(QKV_SEMS))
    text_sum = SlabSum(text_part, text_rows, take(5))
    attn_sum = SlabSum(tsum_part, text_out, take(5))
    q_s, q_r, k_s, k_r, v_s, v_r, n_s, n_r, d_s, d_r = take(10)
    pair_s, pair_r, far_s, far_r, near_s, near_r = take(6)

    nz = gb.shape[0]
    nx = part.shape[0]
    slab, head = lax.axis_index("slab"), lax.axis_index("head")
    slab_count = lax.axis_size("slab")
    z, y = slab // Y, mod(slab, Y)
    row, column = slab // COLUMN_TILES, mod(slab, COLUMN_TILES)
    above, below = mod(slab + slab_count - COLUMN_TILES, slab_count), mod(slab + COLUMN_TILES, slab_count)
    has_left, has_right = column > 0, column < COLUMN_TILES - 1
    has_above, has_below = row > 0, row < slab_count // COLUMN_TILES - 1
    jump_left, jump_right = has_left & (y == 0), has_right & (y == Y - 1)
    x, core = head // 2, mod(head, 2)
    x_right, x_left, x_far = mod(x + 1, nx), mod(x + nx - 1, nx), mod(x + 2, nx)
    other, right, left = x * 2 + 1 - core, x_right * 2 + core, x_left * 2 + core
    depth, width = wq.shape
    heads = width // HEAD_SIZE
    tokens, model = video.shape
    txt = text.shape[0]
    score_scale = math.log2(math.e) / math.sqrt(HEAD_SIZE)
    steps = nz // 2
    nt = (((1,), (1,)), ((), ()))

    fetches = [
        pltpu.make_async_copy(src, dst, fetch_sem.at[i]) for i, (src, dst) in enumerate(zip(fetched, held))
    ]
    for i in FETCH_ORDER:
        fetches[i].start()

    barrier, peers = hello_slab(z, y, nz)
    greet((), (other, right, left))

    @pl.when(jump_left)
    def _():
        greet((slab - 1,))

    @pl.when(jump_right)
    def _():
        greet((slab + 1,))

    for i in FETCH_ORDER[:4]:
        fetches[i].wait()
    for i, weight in enumerate((wk, wv, wo)):
        wb[i] = weight[...]
    pl.semaphore_wait(barrier, peers + 3 + jump_left.astype(jnp.int32) + jump_right.astype(jnp.int32))
    def normalize_video(i, carry):
        at = pl.ds(pl.multiple_of(i * 16, 16), 16)
        values = video[at, :].astype(f32)
        center = values - jnp.mean(values, axis=-1, keepdims=True)
        normed[at, :] = (center * row_scale(center)).astype(bf16)
        return carry

    blocks = tokens // 16
    early = blocks // 4

    def first_rows():
        fetches[0].wait()
        lax.fori_loop(0, early, normalize_video, 0)

    qkv.start(first_rows)

    span = tweight.shape[0]
    aligned = jnp.minimum(slab * depth // LANES * LANES, model - span)
    aligned = pl.multiple_of(aligned, LANES)
    offset = pl.multiple_of(slab * depth - aligned, 16)
    share = nz // heads

    def fill_text_weights():
        tweight[...] = jnp.zeros_like(tweight)
        for i, weight in enumerate((twq, twk, twv)):
            tweight[pl.ds(offset, depth), i * width : (i + 1) * width] = weight[...]

    def normalize_text(i, carry):
        at = pl.ds(pl.multiple_of(i * 16, 16), 16)
        values = text[at, :].astype(f32)
        mean = jnp.mean(values, axis=-1, keepdims=True)
        scale = row_scale(values - mean)
        columns = text[at, pl.ds(aligned, span)].astype(f32)
        tnormed[at, :] = ((columns - mean) * scale).astype(bf16)
        return carry

    def multiply_text():
        for i in range(3):
            product = jnp.dot(
                tnormed[...], tweight[:, i * width : (i + 1) * width], preferred_element_type=f32
            ).astype(bf16)
            for h in range(heads):
                block = product[:, h * HEAD_SIZE : (h + 1) * HEAD_SIZE]
                text_part[i, h * share : (h + 1) * share] = block.reshape(share, *text_part.shape[2:])

    def finish_text(total):
        gain = jnp.where(y == 0, tqg[...], tkg[...])
        return jnp.where(y == 2, total, total * row_scale(total) * gain)

    for t in range(1, steps + 1):
        qkv.step(t)
        if t == 1:
            for i in FETCH_ORDER[5:]:
                fetches[i].wait()
            fill_text_weights()
            lax.fori_loop(0, txt // 32, normalize_text, 0)
        if t == 2:
            lax.fori_loop(txt // 32, txt // 16, normalize_text, 0)
            multiply_text()
            text_sum.start()
        if t == 4:
            text_sum.along_z()
        if t == 7:
            text_sum.hand_out_z(finish_text)
        if t > 2:
            rest, steps_left = blocks - early, steps - 2
            lax.fori_loop(
                early + (t - 3) * rest // steps_left, early + (t - 2) * rest // steps_left, normalize_video, 0
            )

    qkv.own_b.wait()
    qkv.late_start(0)

    acc[...] = jnp.zeros_like(acc)
    group = 4 if nz % 4 == 0 else nz
    span = group * Y * depth

    def multiply_query(c, carry):
        rows = normed[:, pl.ds(pl.multiple_of(c * span, span), span)]
        acc[:, :width] += jnp.dot(
            rows, ga[pl.ds(c * group, group)].reshape(span, width), preferred_element_type=f32
        )
        return carry

    lax.fori_loop(0, nz // group, multiply_query, 0)
    rows_out = []
    for h in range(heads):
        values = acc[:, h * HEAD_SIZE : (h + 1) * HEAD_SIZE]
        q[0, h] = (values * row_scale(values) * qg[...]).astype(bf16)
        to_below = remote(q.at[0, h], q.at[1, h], q_s.at[0, h], q_r.at[0, h], slab=below)
        to_above = remote(q.at[0, h], q.at[2, h], q_s.at[1, h], q_r.at[1, h], slab=above)
        to_below.start()
        to_above.start()
        rows_out.append((to_below, to_above))

    pair_depth = 2 * Y * depth

    def multiply_rest(i, j):
        at = mod(z // 2 + i + nz // 2 - 2, nz // 2)
        rows = normed[:, pl.ds(pl.multiple_of(at * pair_depth, pair_depth), pair_depth)]
        acc[:, (j + 1) * width : (j + 2) * width] += jnp.dot(
            rows, gb[pl.ds(at * 2, 2), :, j].reshape(pair_depth, width), preferred_element_type=f32
        )

    def multiply_pairs(first, last, j):
        def body(i, carry):
            multiply_rest(i, j)
            return carry

        lax.fori_loop(first, last, body, 0)

    qkv.near_landed()
    multiply_pairs(0, 5, 0)
    multiply_pairs(0, 5, 1)
    qkv.far_landed()
    multiply_pairs(5, nz // 2, 0)
    text_sum.hand_out_y()

    to_right, to_left = [], []

    def send_sides(block, send, arrived, h):
        right_now = remote(block.at[0, h], block.at[1, h], send.at[0, h], arrived.at[0, h], slab=slab + 1)
        left_now = remote(block.at[0, h], block.at[2, h], send.at[1, h], arrived.at[1, h], slab=slab - 1)
        pl.when(has_right)(right_now.start)
        pl.when(has_left)(left_now.start)
        to_right.append(right_now)
        to_left.append(left_now)

    for h in range(heads):
        values = acc[:, width + h * HEAD_SIZE : width + (h + 1) * HEAD_SIZE]
        k[0, h] = (values * row_scale(values) * kg[...]).astype(bf16)
        if h == 0:
            send_sides(k, k_s, k_r, h)
    multiply_pairs(5, nz // 2, 1)
    for h in range(heads):
        v[0, h] = acc[:, 2 * width + h * HEAD_SIZE : 2 * width + (h + 1) * HEAD_SIZE].T.astype(bf16)
        if h > 0:
            send_sides(k, k_s, k_r, h)
        send_sides(v, v_s, v_r, h)
    qkv.late_start(1)

    @pl.when(jnp.logical_not(has_left))
    def _():
        k[1] = jnp.zeros_like(k[1])
        v[1] = jnp.zeros_like(v[1])

    @pl.when(jnp.logical_not(has_right))
    def _():
        k[2] = jnp.zeros_like(k[2])
        v[2] = jnp.zeros_like(v[2])

    def scores(keys, queries):
        return jnp.exp2(lax.dot_general(keys, queries, nt, preferred_element_type=f32) * score_scale)

    def weigh(values, e):
        return jnp.dot(values, e.astype(bf16), preferred_element_type=f32)

    def column_sum(e):
        return jnp.sum(e, axis=0, keepdims=True)

    tsum_part[heads] = jnp.zeros_like(tsum_part[heads])
    for h in range(heads):
        e = scores(k[0, h], q[0, h])
        num[0, h] = weigh(v[0, h], e)
        den[0, h, 0:1] = column_sum(e)

    for h in range(heads):
        for copy in rows_out[h]:
            copy.wait_recv()

        def neighbour(tile, carry, h=h):
            e = scores(k[0, h], q[tile, h])
            num[tile, h] = weigh(v[0, h], e)
            den[tile, h] = jnp.broadcast_to(column_sum(e), den.shape[2:])
            return carry

        lax.fori_loop(1, 3, neighbour, 0)
    qkv.late_relay()

    def has_side(slot):
        return column != (COLUMN_TILES - 1) * (slot - 1)

    def add_side(slot, tile, h):
        reach = jnp.where(has_side(slot), 1.0, 0.0) * window[1, head * heads + h].astype(f32)
        e = scores(k[slot, h], q[tile, h])
        num[tile, h] += weigh(v[slot, h], e) * reach
        den[tile, h, 0:1] += column_sum(e) * reach

    def text_phase():
        live[...] = jnp.broadcast_to(mask[...].astype(f32), live.shape).T
        is_first = jnp.where(slab == 0, 1.0, 0.0)
        text_sum.end()

        def text_head(i, h):
            return text_rows[i, h * share : (h + 1) * share].reshape(txt, HEAD_SIZE)

        text_values = []
        for h in range(heads):
            tq = text_head(0, h)
            text_values.append(text_head(2, h).astype(f32).T.astype(bf16))
            e = scores(k[0, h], tq)
            own = scores(text_head(1, h), tq) * live[...] * is_first
            total = weigh(v[0, h], e) + weigh(text_values[h], own)
            tsum_part[h] = total.reshape(tsum_part.shape[1:])
            tsum_part[heads, 0, h : h + 1] = column_sum(e) + column_sum(own)
        attn_sum.start()

        live_wide = jnp.concatenate([live[...]] * (tokens // txt), axis=1)
        for h in range(heads):
            e = scores(text_head(1, h), q[0, h]) * live_wide
            num[0, h] += weigh(text_values[h], e)
            den[0, h, 0:1] += column_sum(e)

    back = []
    for h in range(heads):

        for i in range(2):
            slot = 1 + mod(i + jump_left.astype(jnp.int32), 2)

            @pl.when(has_side(slot))
            def _():
                for sem, dst in ((k_r, k), (v_r, v)):
                    block = dst.at[slot, h]
                    arrived = sem.at[slot - 1, h]
                    remote(block, block, arrived, arrived, slab=slab + 2 * slot - 3).wait_recv()

            def side(tile, carry, h=h, slot=slot):
                add_side(slot, tile, h)
                return carry

            lax.fori_loop(1, 3, side, 0)
        for tile in (1, 2):
            num_out[tile - 1, h] = num[tile, h].astype(bf16)
        now = [
            remote(num_out.at[0, h], num_in.at[1, h], n_s.at[1, h], n_r.at[1, h], slab=above),
            remote(num_out.at[1, h], num_in.at[0, h], n_s.at[0, h], n_r.at[0, h], slab=below),
            remote(den.at[1, h], den_in.at[1, h], d_s.at[1, h], d_r.at[1, h], slab=above),
            remote(den.at[2, h], den_in.at[0, h], d_s.at[0, h], d_r.at[0, h], slab=below),
        ]
        for copy in now:
            copy.start()
        back.append(now)
        if h == 0:
            text_phase()

    def own_side(i, carry):
        add_side(1 + i % 2, 0, i // 2)
        return carry

    lax.fori_loop(0, 2 * heads, own_side, 0)
    attn_sum.along_z()
    text_sum.settle()
    for h in range(heads):
        for copy in back[h]:
            copy.wait_recv()
        total, under = num[0, h], den[0, h, 0:1]
        for side_row, exists in ((0, has_above), (1, has_below)):
            reach = jnp.where(exists, 1.0, 0.0) * window[0, head * heads + h].astype(f32)
            total = total + num_in[side_row, h].astype(f32) * reach
            under = under + den_in[side_row, h, 0:1] * reach
        attn[:, h * HEAD_SIZE : (h + 1) * HEAD_SIZE] = (total / under).T.astype(bf16)

    qkv.late_end()
    rows = tokens // nx
    halves = part.shape[2]
    pairs = []

    def send_pair(xx):
        mine = attn[pl.ds(pl.multiple_of(xx * rows, 16), rows), :]
        for half in range(halves):
            weight = gb[half * nz // halves : (half + 1) * nz // halves, :, 2].reshape(model // halves, width)
            product = lax.dot_general(mine, weight, nt, preferred_element_type=f32).astype(bf16)
            for c in range(2):
                part[xx, c, half] = product[c * rows // 2 : (c + 1) * rows // 2]
            pairs.append(
                remote(part.at[xx, 1 - core, half], pair.at[xx, half], pair_s.at[xx, half], pair_r.at[xx, half],
                       head=other)
            )
            pairs[-1].start()

    def pair_sum(xx, half):
        block = pair.at[xx, half]
        remote(block, block, pair_s.at[xx, half], pair_r.at[xx, half], head=other).wait_recv()
        pair[xx, half] = (pair[xx, half].astype(f32) + part[xx, core, half].astype(f32)).astype(bf16)

    fars = [
        remote(pair.at[x_far, 0], far.at[0], far_s.at[0], far_r.at[0], head=right),
        remote(pair.at[x_far, 1], far.at[1], far_s.at[1], far_r.at[1], head=left),
    ]
    send_pair(x_far)
    send_pair(x_right)
    for half in range(halves):
        pair_sum(x_far, half)
        fars[half].start()
    send_pair(x_left)
    nears = [
        remote(pair.at[x_right, 1], near.at[0, 1], near_s.at[0, 1], near_r.at[0, 1], head=right),
        remote(pair.at[x_left, 0], near.at[1, 0], near_s.at[1, 0], near_r.at[1, 0], head=left),
        remote(pair.at[x_right, 0], near.at[0, 0], near_s.at[0, 0], near_r.at[0, 0], head=right),
        remote(pair.at[x_left, 1], near.at[1, 1], near_s.at[1, 1], near_r.at[1, 1], head=left),
    ]
    pair_sum(x_right, 1)
    nears[0].start()
    pair_sum(x_left, 0)
    nears[1].start()
    pair_sum(x_right, 0)
    pair_sum(x_left, 1)
    send_pair(x)
    attn_sum.hand_out_z(lambda total: total)
    for half in range(halves):
        pair_sum(x, half)
    fars[0].wait_recv()
    pair[x_right, 0] = (pair[x_right, 0].astype(f32) + far[0].astype(f32)).astype(bf16)
    nears[2].start()
    fars[1].wait_recv()
    pair[x_left, 1] = (pair[x_left, 1].astype(f32) + far[1].astype(f32)).astype(bf16)
    nears[3].start()
    qkv.settle()
    attn_sum.hand_out_y()
    for copy in (*sum(rows_out, ()), *sum(back, []), *pairs):
        copy.wait_send()

    @pl.when(has_right)
    def _():
        for copy in to_right:
            copy.wait_send()

    @pl.when(has_left)
    def _():
        for copy in to_left:
            copy.wait_send()

    for copy in nears:
        copy.wait_recv()
    for half in range(halves):
        at = half * model // halves
        out[:, at : at + model // halves] = (
            pair[x, half].astype(f32) + near[0, half].astype(f32) + near[1, half].astype(f32)
        ).astype(bf16)

    attn_sum.end()
    for h in range(heads):
        total = text_out[h].reshape(HEAD_SIZE, txt) / text_out[heads, 0, h : h + 1]
        text_final[:, h * HEAD_SIZE : (h + 1) * HEAD_SIZE] = total.T.astype(bf16)
    attn_sum.settle()
    for copy in (*fars, *nears):
        copy.wait_send()


def run_whole(slab_count, head_count, operands):
    video, text, wq = operands[0], operands[1], operands[2]
    depth, width = wq.shape
    tokens, model = video.shape
    txt = text.shape[0]
    heads = width // HEAD_SIZE
    nz, nx = slab_count // Y, head_count // 2
    rows = tokens // head_count
    bf16, f32 = jnp.bfloat16, jnp.float32
    text_block = jax.ShapeDtypeStruct((3, nz, txt * heads // nz, HEAD_SIZE), bf16)
    sum_block = jax.ShapeDtypeStruct((heads + 1, nz, HEAD_SIZE // nz, txt), f32)
    half = model // 2
    vmem = pl.BlockSpec(memory_space=VMEM)
    return pl.pallas_call(
        whole_kernel,
        out_shape=(
            jax.ShapeDtypeStruct((rows, model), bf16),
            jax.ShapeDtypeStruct((txt, width), bf16),
        ),
        in_specs=[pl.BlockSpec(memory_space=pltpu.HBM)] * OPERANDS,
        out_specs=(vmem, vmem),
        scratch_shapes=[
            *(VMEM(a.shape, a.dtype) for a in operands[:-1]),
            pltpu.SMEM(operands[-1].shape, operands[-1].dtype),
            DMA((OPERANDS,)),
            VMEM((3, depth, width), bf16),
            VMEM((nz, Y, depth, width), bf16),
            VMEM((nz, Y, 3, depth, width), bf16),
            VMEM((tokens, model), bf16),
            VMEM((txt, 2 * LANES), bf16),
            VMEM((2 * LANES, 3 * width), bf16),
            VMEM(text_block.shape, bf16),
            VMEM(text_block.shape, bf16),
            VMEM((tokens, 3 * width), f32),
            VMEM((3, heads, tokens, HEAD_SIZE), bf16),
            VMEM((3, heads, tokens, HEAD_SIZE), bf16),
            VMEM((3, heads, HEAD_SIZE, tokens), bf16),
            VMEM((3, heads, HEAD_SIZE, tokens), f32),
            VMEM((3, heads, 8, tokens), f32),
            VMEM((2, heads, HEAD_SIZE, tokens), bf16),
            VMEM((2, heads, HEAD_SIZE, tokens), bf16),
            VMEM((2, heads, 8, tokens), f32),
            VMEM((tokens, width), bf16),
            VMEM((txt, txt), f32),
            VMEM(sum_block.shape, f32),
            VMEM(sum_block.shape, f32),
            VMEM((nx, 2, 2, rows, half), bf16),
            VMEM((nx, 2, rows, half), bf16),
            VMEM((2, rows, half), bf16),
            VMEM((2, 2, rows, half), bf16),
            *TorusGather.scratch(nz),
            *SlabSum.scratch(text_block),
            *SlabSum.scratch(sum_block),
            *[DMA((2, heads))] * 10,
            DMA((nx, 2)), DMA((nx, 2)), DMA((2,)), DMA((2,)), DMA((2, 2)), DMA((2, 2)),
        ],
        compiler_params=pltpu.CompilerParams(
            collective_id=0, has_side_effects=True, vmem_limit_bytes=32 * MIB
        ),
        name="whole",
    )(*(pltpu.with_memory_space_constraint(a, pltpu.HBM) for a in operands))


def on_device(
    video_token_state,
    text_tokens,
    text_mask,
    head_window,
    video_query_weight,
    video_key_weight,
    video_value_weight,
    wout_video,
    wquery_text,
    wkey_text,
    wvalue_text,
    video_query_gain,
    video_key_gain,
    qgain_text,
    kgain_text,
):
    operands = (
        video_token_state, text_tokens,
        video_query_weight, video_key_weight, video_value_weight, wout_video.T,
        wquery_text, wkey_text, wvalue_text,
        *(row.reshape(1, -1) for row in (video_query_gain, video_key_gain, qgain_text, kgain_text, text_mask)),
        head_window.T,
    )
    return run_whole(lax.axis_size("slab"), lax.axis_size("head"), operands)


def solution(mesh):
    return jax.shard_map(
        on_device,
        mesh=mesh,
        in_specs=(
            P("slab", None),
            P(),
            P(),
            P(),
            P("slab", "head"),
            P("slab", "head"),
            P("slab", "head"),
            P("head", "slab"),
            P("slab", "head"),
            P("slab", "head"),
            P("slab", "head"),
            P(),
            P(),
            P(),
            P(),
        ),
        out_specs=(P(("slab", "head"), None), P(None, "head")),
        check_vma=False,
    )
```

```python
import functools
import math

import jax
import jax.numpy as jnp
from jax import lax
from jax.experimental import pallas as pl
from jax.experimental.pallas import tpu as pltpu
from jax.sharding import PartitionSpec as P

HEAD_SIZE = 128
COLUMN_TILES = 8
Y = 4
MIB = 1 << 20
LANES = 128
VMEM = pltpu.VMEM
DMA = pltpu.SemaphoreType.DMA

norm_eps = 1e-06


def mod(a, n):
    return lax.rem(a, jnp.int32(n))


def remote(src, dst, send, recv, **device):
    return pltpu.make_async_remote_copy(
        src_ref=src, dst_ref=dst, send_sem=send, recv_sem=recv,
        device_id=device, device_id_type=pl.DeviceIdType.MESH,
    )


def greet(slabs=(), heads=()):
    barrier = pltpu.get_barrier_semaphore()
    for slab in slabs:
        pl.semaphore_signal(barrier, 1, device_id={"slab": slab}, device_id_type=pl.DeviceIdType.MESH)
    for head in heads:
        pl.semaphore_signal(barrier, 1, device_id={"head": head}, device_id_type=pl.DeviceIdType.MESH)
    return barrier


def when(condition, step):
    if isinstance(condition, bool):
        if condition:
            step()
    else:
        pl.when(condition)(step)


def hello_slab(z, y, nz):
    barrier = pltpu.get_barrier_semaphore()

    def greet_one(slab):
        pl.semaphore_signal(barrier, 1, device_id={"slab": slab}, device_id_type=pl.DeviceIdType.MESH)

    for d in range(1, Y):
        greet_one(z * Y + mod(y + d, Y))

    def body(d, carry):
        greet_one(mod(z + d, nz) * Y + y)
        return carry

    lax.fori_loop(1, nz, body, 0)
    return barrier, Y - 1 + nz - 1


class SlabSum:
    @staticmethod
    def scratch(block):
        owners, nz, rows, lanes = block.shape
        return [
            VMEM((Y, nz, rows, lanes), block.dtype),
            VMEM((nz, rows, lanes), block.dtype),
            VMEM((nz, rows, lanes), block.dtype),
            DMA((2, 2, Y)),
            DMA((2, 2)),
        ]

    def __init__(self, part, out, scratch):
        self.part, self.out = part, out
        self.from_y, self.sum_y, self.from_z, self.ysem, self.zsem = scratch
        self.owners, self.nz = part.shape[:2]
        slab = lax.axis_index("slab")
        self.z, self.y = slab // Y, mod(slab, Y)

    def _owns(self, y):
        return True if self.owners == Y else y < self.owners

    def _y(self, d, give):
        y, to = self.y, mod(self.y + d, Y)
        src = self.out.at[y] if give else self.part.at[to]
        dst = self.out.at[y] if give else self.from_y.at[y]
        return remote(src, dst, self.ysem.at[give, 0, to], self.ysem.at[give, 1, y], slab=self.z * Y + to)

    def _y_in(self, d, give):
        of = mod(self.y + d, Y)
        dst = self.out.at[of] if give else self.from_y.at[of]
        return remote(dst, dst, self.ysem.at[give, 0, of], self.ysem.at[give, 1, of], slab=self.z * Y + of)

    def _z(self, d, give):
        z, to = self.z, mod(self.z + d, self.nz)
        src = self.out.at[self.y, z] if give else self.sum_y.at[to]
        dst = self.out.at[self.y, z] if give else self.from_z.at[z]
        return remote(src, dst, self.zsem.at[give, 0], self.zsem.at[give, 1], slab=to * Y + self.y)

    def _all_z(self, give):
        blocks = self.from_z.at[pl.ds(0, self.nz - 1)]
        to = mod(self.z + 1, self.nz)
        return remote(blocks, blocks, self.zsem.at[give, 0], self.zsem.at[give, 1], slab=to * Y + self.y)

    def _each_z(self, step):
        def body(d, carry):
            step(d)
            return carry

        lax.fori_loop(1, self.nz, body, 0)

    def start(self):
        for d in range(1, Y):
            when(self._owns(mod(self.y + d, Y)), lambda: self._y(d, 0).start())

    def along_z(self):
        def step():
            for d in range(1, Y):
                self._y_in(d, 0).wait_recv()
            total = self.part[self.y].astype(jnp.float32)
            for d in range(1, Y):
                total = total + self.from_y[mod(self.y + d, Y)].astype(jnp.float32)
            self.sum_y[...] = total.astype(self.sum_y.dtype)
            self._each_z(lambda d: self._z(d, 0).start())

        when(self._owns(self.y), step)

    def hand_out_z(self, finish):
        def step():
            self._all_z(0).wait_recv()
            total = self.sum_y[self.z].astype(jnp.float32)
            for d in range(1, self.nz):
                total = total + self.from_z[mod(self.z + d, self.nz)].astype(jnp.float32)
            self.out[self.y, self.z] = finish(total).astype(self.out.dtype)
            self._each_z(lambda d: self._z(d, 1).start())

        when(self._owns(self.y), step)

    def hand_out_y(self):
        def step():
            self._all_z(1).wait_recv()
            for d in range(1, Y):
                self._y(d, 1).start()

        when(self._owns(self.y), step)

    def end(self):
        for d in range(1, Y):
            when(self._owns(mod(self.y + d, Y)), lambda: self._y_in(d, 1).wait_recv())

    def settle(self):
        for d in range(1, Y):
            when(self._owns(mod(self.y + d, Y)), lambda: self._y(d, 0).wait_send())

        def mine():
            for d in range(1, Y):
                self._y(d, 1).wait_send()

            self._all_z(0).wait_send()
            self._all_z(1).wait_send()

        when(self._owns(self.y), mine)


class TorusGather:
    RELAYED = 6
    NEAR = 5

    @staticmethod
    def scratch(nz):
        return [
            DMA((1,)), DMA((nz, 2)), DMA((3,)), DMA((3,)),
            DMA((1,)), DMA((nz,)), DMA((1,)), DMA((2, nz)), DMA((1,)), DMA((2,)), DMA((3,)),
            DMA((2, 2)), DMA((2, 2)), DMA((2,)), DMA((2,)),
        ]

    def __init__(self, wa, wb, ga, gb, sems):
        self.wa, self.wb, self.ga, self.gb = wa, wb, ga, gb
        (self.az_s, self.az_r, self.ay_s, self.ay_r, self.bz_s, self.bz_r,
         self.by_s, self.by_r, self.bo_s, self.bo_r, self.own_sem,
         self.ly_s, self.ly_r, self.lo_s, self.lo_r) = sems
        self.nz = nz = gb.shape[0]
        self.half = nz // 2
        slab = lax.axis_index("slab")
        self.z, self.y = z, y = slab // Y, mod(slab, Y)
        self.next = mod(z + 1, nz), mod(z + nz - 1, nz)
        self.right, self.left, self.across = mod(y + 1, Y), mod(y + Y - 1, Y), mod(y + 2, Y)
        self.sides = self.right, self.left
        self.parts = (pl.ds(0, self.half), pl.ds(self.half, self.half))
        self.sent = []

    def _go(self, copy):
        copy.start()
        self.sent.append(copy)

    def _landed(self, dst, sem):
        remote(dst, dst, self.own_sem.at[2], sem, slab=self.z * Y + self.right).wait_recv()

    def _pair(self, origin, p):
        return self.ga.at[origin, pl.ds(2 * p, 2)]

    def _a_z(self, origin, p, way):
        block = self._pair(origin, p)
        remote(block, block, self.az_s.at[0], self.az_r.at[origin, p],
               slab=self.next[way] * Y + self.y).start()

    def _b_z(self, origin, src, way):
        remote(src, self.gb.at[origin, self.y], self.bz_s.at[0], self.bz_r.at[origin],
               slab=self.next[way] * Y + self.y).start()

    def _two(self, origin, j):
        return self.gb.at[origin, j, pl.ds(0, 2)]

    def _b_y(self, origin, src):
        for way, to in enumerate(self.sides):
            remote(src, self._two(origin, self.y), self.by_s.at[0], self.by_r.at[way, origin],
                   slab=self.z * Y + to).start()

    def _b_relay(self, origin, t):
        self._landed(self._two(origin, self.left), self.by_r.at[0, origin])
        self._landed(self._two(origin, self.right), self.by_r.at[1, origin])
        turn = 1 - 2 * mod(origin, 2)
        block = self._two(origin, mod(self.y - turn + Y, Y))
        remote(block, block, self.bo_s.at[0], self.bo_r.at[int(t > self.NEAR)],
               slab=self.z * Y + mod(self.y + turn + Y, Y)).start()

    def start(self, meanwhile):
        z, y, wa, wb = self.z, self.y, self.wa, self.wb
        self._b_z(z, wb, 0)
        self._b_z(z, wb, 1)
        for i, to in enumerate((self.right, self.left, self.across)):
            self._go(remote(wa, self.ga.at[z, y], self.ay_s.at[i], self.ay_r.at[i], slab=z * Y + to))
        self.own_a = pltpu.make_async_copy(wa, self.ga.at[z, y], self.own_sem.at[0])
        self.own_a.start()
        self._b_y(z, wb.at[pl.ds(0, 2)])
        self.own_b = pltpu.make_async_copy(wb, self.gb.at[z, y], self.own_sem.at[1])
        self.own_b.start()
        meanwhile()
        odd = mod(y, 2)
        self._landed(self.ga.at[z, y + 1 - 2 * odd], self.ay_r.at[1 - odd])
        self.own_a.wait()
        self._a_z(z, y // 2, 0)
        self._a_z(z, y // 2, 1)
        self._landed(self.ga.at[z, mod(y + Y - 1 + 2 * odd, Y)], self.ay_r.at[odd])
        self._landed(self.ga.at[z, self.across], self.ay_r.at[2])
        self._a_z(z, 1 - y // 2, 0)
        self._a_z(z, 1 - y // 2, 1)

    def step(self, t):
        nz, half, y = self.nz, self.half, self.y
        ways = [(mod(self.z - t + nz, nz), 0, half)]
        if t < half:
            ways.append((mod(self.z + t, nz), 1, half - 1))
        for origin, way, last in ways:
            block = self.gb.at[origin, y]
            self._landed(block, self.bz_r.at[origin])
            if t < last:
                self._b_z(origin, block, way)
        if t > self.RELAYED:
            self._along_y(ways, t)
        for p in (y // 2, 1 - y // 2):
            for origin, way, last in ways:
                self._landed(self._pair(origin, p), self.az_r.at[origin, p])
                if t < last:
                    self._a_z(origin, p, way)
        if t <= self.RELAYED:
            self._along_y(ways, t)
        if t > 1:
            self._b_relay(mod(self.z - t + 2 + nz, nz), t - 2)
            if t > 2:
                self._b_relay(mod(self.z + t - 2, nz), t - 2)

    def _along_y(self, ways, t):
        for origin, _, _ in ways:
            two = self._two(origin, self.y)
            self._b_y(origin, two)
            if t > self.RELAYED:
                remote(two, two, self.bo_s.at[0], self.bo_r.at[1],
                       slab=self.z * Y + self.across).start()

    def near_landed(self):
        self._landed(self.gb.at[pl.ds(0, 2 * self.NEAR + 1), 0, pl.ds(0, 2)], self.bo_r.at[0])

    def far_landed(self):
        for t in range(self.RELAYED + 1, self.half + 1):
            for origin in (mod(self.z - t + self.nz, self.nz), mod(self.z + t, self.nz))[: 1 + (t < self.half)]:
                self._landed(self._two(origin, self.left), self.by_r.at[0, origin])
                self._landed(self._two(origin, self.right), self.by_r.at[1, origin])
        self._landed(self.gb.at[pl.ds(0, self.nz - 2 * self.NEAR - 1), 0, pl.ds(0, 2)], self.bo_r.at[1])

    def _late(self, part, j):
        return self.gb.at[self.parts[part], j, 2]

    def late_start(self, turn):
        for way in range(2):
            part = way if turn == 0 else 1 - way
            block = self._late(part, self.y)
            self._go(remote(block, block, self.ly_s.at[way, part], self.ly_r.at[way, part],
                            slab=self.z * Y + self.sides[way]))

    def late_relay(self):
        for way in range(2):
            block = self._late(way, self.sides[1 - way])
            self._landed(block, self.ly_r.at[way, way])
            self._go(remote(block, block, self.lo_s.at[way], self.lo_r.at[way], slab=self.z * Y + self.sides[way]))

    def late_end(self):
        for way in range(2):
            self._landed(self._late(1 - way, self.sides[1 - way]), self.ly_r.at[way, 1 - way])
        for way in range(2):
            self._landed(self._late(way, self.across), self.lo_r.at[way])

    def settle(self):
        nz, one, two = self.nz, pl.ds(0, 1), pl.ds(0, 2)
        for block, sem in (
            (self.ga.at[pl.ds(0, nz - 1)], self.az_s),
            (self.gb.at[pl.ds(0, nz - 1), one], self.bz_s),
            (self.gb.at[:, two, two], self.by_s),
            (self.gb.at[:, one, two], self.bo_s),
        ):
            remote(block, block, sem.at[0], self.own_sem.at[2], slab=self.z * Y + self.right).wait_send()
        for copy in self.sent:
            copy.wait_send()


def row_scale(values):
    return lax.rsqrt(jnp.mean(values * values, axis=-1, keepdims=True) + norm_eps)


OPERANDS = 15
FETCH_ORDER = (2, 3, 4, 5, 0, 1, 6, 7, 8, 9, 10, 11, 12, 13, 14)
QKV_SEMS = 15


def whole_kernel(*refs):
    f32, bf16 = jnp.float32, jnp.bfloat16

    def take(count):
        nonlocal refs
        some, refs = refs[:count], refs[count:]
        return some

    fetched = take(OPERANDS)
    out, text_final = take(2)
    held = take(OPERANDS)
    video, text, wq, wk, wv, wo, twq, twk, twv, qg, kg, tqg, tkg, mask, window = held
    (fetch_sem, wb, ga, gb, normed, tnormed, tweight, text_part, text_rows, acc) = take(10)
    (q, k, v, num, den, num_out, num_in, den_in, attn, live, tsum_part, text_out) = take(12)
    (part, pair, far, near) = take(4)
    qkv = TorusGather(wq, wb, ga, gb, take(QKV_SEMS))
    text_sum = SlabSum(text_part, text_rows, take(5))
    attn_sum = SlabSum(tsum_part, text_out, take(5))
    q_s, q_r, k_s, k_r, v_s, v_r, n_s, n_r, d_s, d_r = take(10)
    pair_s, pair_r, far_s, far_r, near_s, near_r = take(6)

    nz = gb.shape[0]
    nx = part.shape[0]
    slab, head = lax.axis_index("slab"), lax.axis_index("head")
    slab_count = lax.axis_size("slab")
    z, y = slab // Y, mod(slab, Y)
    row, column = slab // COLUMN_TILES, mod(slab, COLUMN_TILES)
    above, below = mod(slab + slab_count - COLUMN_TILES, slab_count), mod(slab + COLUMN_TILES, slab_count)
    has_left, has_right = column > 0, column < COLUMN_TILES - 1
    has_above, has_below = row > 0, row < slab_count // COLUMN_TILES - 1
    jump_left, jump_right = has_left & (y == 0), has_right & (y == Y - 1)
    x, core = head // 2, mod(head, 2)
    x_right, x_left, x_far = mod(x + 1, nx), mod(x + nx - 1, nx), mod(x + 2, nx)
    other, right, left = x * 2 + 1 - core, x_right * 2 + core, x_left * 2 + core
    depth, width = wq.shape
    heads = width // HEAD_SIZE
    tokens, model = video.shape
    txt = text.shape[0]
    score_scale = math.log2(math.e) / math.sqrt(HEAD_SIZE)
    steps = nz // 2
    nt = (((1,), (1,)), ((), ()))

    fetches = [
        pltpu.make_async_copy(src, dst, fetch_sem.at[i]) for i, (src, dst) in enumerate(zip(fetched, held))
    ]
    for i in FETCH_ORDER:
        fetches[i].start()

    barrier, peers = hello_slab(z, y, nz)
    greet((), (other, right, left))

    @pl.when(jump_left)
    def _():
        greet((slab - 1,))

    @pl.when(jump_right)
    def _():
        greet((slab + 1,))

    for i in FETCH_ORDER[:4]:
        fetches[i].wait()
    for i, weight in enumerate((wk, wv, wo)):
        wb[i] = weight[...]
    pl.semaphore_wait(barrier, peers + 3 + jump_left.astype(jnp.int32) + jump_right.astype(jnp.int32))
    def normalize_video(i, carry):
        at = pl.ds(pl.multiple_of(i * 16, 16), 16)
        values = video[at, :].astype(f32)
        center = values - jnp.mean(values, axis=-1, keepdims=True)
        normed[at, :] = (center * row_scale(center)).astype(bf16)
        return carry

    blocks = tokens // 16
    early = blocks // 4

    def first_rows():
        fetches[0].wait()
        lax.fori_loop(0, early, normalize_video, 0)

    qkv.start(first_rows)

    span = tweight.shape[0]
    aligned = jnp.minimum(slab * depth // LANES * LANES, model - span)
    aligned = pl.multiple_of(aligned, LANES)
    offset = pl.multiple_of(slab * depth - aligned, 16)
    share = nz // heads

    def fill_text_weights():
        tweight[...] = jnp.zeros_like(tweight)
        for i, weight in enumerate((twq, twk, twv)):
            tweight[pl.ds(offset, depth), i * width : (i + 1) * width] = weight[...]

    def normalize_text(i, carry):
        at = pl.ds(pl.multiple_of(i * 16, 16), 16)
        values = text[at, :].astype(f32)
        mean = jnp.mean(values, axis=-1, keepdims=True)
        scale = row_scale(values - mean)
        columns = text[at, pl.ds(aligned, span)].astype(f32)
        tnormed[at, :] = ((columns - mean) * scale).astype(bf16)
        return carry

    def multiply_text():
        for i in range(3):
            product = jnp.dot(
                tnormed[...], tweight[:, i * width : (i + 1) * width], preferred_element_type=f32
            ).astype(bf16)
            for h in range(heads):
                block = product[:, h * HEAD_SIZE : (h + 1) * HEAD_SIZE]
                text_part[i, h * share : (h + 1) * share] = block.reshape(share, *text_part.shape[2:])

    def finish_text(total):
        gain = jnp.where(y == 0, tqg[...], tkg[...])
        return jnp.where(y == 2, total, total * row_scale(total) * gain)

    for t in range(1, steps + 1):
        qkv.step(t)
        if t == 1:
            for i in FETCH_ORDER[5:]:
                fetches[i].wait()
            fill_text_weights()
            lax.fori_loop(0, txt // 32, normalize_text, 0)
        if t == 2:
            lax.fori_loop(txt // 32, txt // 16, normalize_text, 0)
            multiply_text()
            text_sum.start()
        if t == 4:
            text_sum.along_z()
        if t == 7:
            text_sum.hand_out_z(finish_text)
        if t > 2:
            rest, steps_left = blocks - early, steps - 2
            lax.fori_loop(
                early + (t - 3) * rest // steps_left, early + (t - 2) * rest // steps_left, normalize_video, 0
            )

    qkv.own_b.wait()

    acc[...] = jnp.zeros_like(acc)
    group = 4 if nz % 4 == 0 else nz
    span = group * Y * depth

    def multiply_query(c, carry):
        rows = normed[:, pl.ds(pl.multiple_of(c * span, span), span)]
        acc[:, :width] += jnp.dot(
            rows, ga[pl.ds(c * group, group)].reshape(span, width), preferred_element_type=f32
        )
        return carry

    lax.fori_loop(0, nz // group, multiply_query, 0)
    rows_out = []
    for h in range(heads):
        values = acc[:, h * HEAD_SIZE : (h + 1) * HEAD_SIZE]
        q[0, h] = (values * row_scale(values) * qg[...]).astype(bf16)
        to_below = remote(q.at[0, h], q.at[1, h], q_s.at[0, h], q_r.at[0, h], slab=below)
        to_above = remote(q.at[0, h], q.at[2, h], q_s.at[1, h], q_r.at[1, h], slab=above)
        to_below.start()
        to_above.start()
        rows_out.append((to_below, to_above))

    pair_depth = 2 * Y * depth

    def multiply_rest(i, j):
        at = mod(z // 2 + i + nz // 2 - 2, nz // 2)
        rows = normed[:, pl.ds(pl.multiple_of(at * pair_depth, pair_depth), pair_depth)]
        acc[:, (j + 1) * width : (j + 2) * width] += jnp.dot(
            rows, gb[pl.ds(at * 2, 2), :, j].reshape(pair_depth, width), preferred_element_type=f32
        )

    def multiply_pairs(first, last, j):
        def body(i, carry):
            multiply_rest(i, j)
            return carry

        lax.fori_loop(first, last, body, 0)

    qkv.near_landed()
    multiply_pairs(0, 5, 0)
    multiply_pairs(0, 5, 1)
    qkv.far_landed()
    multiply_pairs(5, nz // 2, 0)
    text_sum.hand_out_y()

    to_right, to_left = [], []

    def send_sides(block, send, arrived, h):
        right_now = remote(block.at[0, h], block.at[1, h], send.at[0, h], arrived.at[0, h], slab=slab + 1)
        left_now = remote(block.at[0, h], block.at[2, h], send.at[1, h], arrived.at[1, h], slab=slab - 1)
        pl.when(has_right)(right_now.start)
        pl.when(has_left)(left_now.start)
        to_right.append(right_now)
        to_left.append(left_now)

    for h in range(heads):
        values = acc[:, width + h * HEAD_SIZE : width + (h + 1) * HEAD_SIZE]
        k[0, h] = (values * row_scale(values) * kg[...]).astype(bf16)
        if h == 0:
            send_sides(k, k_s, k_r, h)
    multiply_pairs(5, nz // 2, 1)
    for h in range(heads):
        v[0, h] = acc[:, 2 * width + h * HEAD_SIZE : 2 * width + (h + 1) * HEAD_SIZE].T.astype(bf16)
        if h > 0:
            send_sides(k, k_s, k_r, h)
        send_sides(v, v_s, v_r, h)
    qkv.late_start(0)
    qkv.late_start(1)

    @pl.when(jnp.logical_not(has_left))
    def _():
        k[1] = jnp.zeros_like(k[1])
        v[1] = jnp.zeros_like(v[1])

    @pl.when(jnp.logical_not(has_right))
    def _():
        k[2] = jnp.zeros_like(k[2])
        v[2] = jnp.zeros_like(v[2])

    def scores(keys, queries):
        return jnp.exp2(lax.dot_general(keys, queries, nt, preferred_element_type=f32) * score_scale)

    def weigh(values, e):
        return jnp.dot(values, e.astype(bf16), preferred_element_type=f32)

    def column_sum(e):
        return jnp.sum(e, axis=0, keepdims=True)

    tsum_part[heads] = jnp.zeros_like(tsum_part[heads])
    for h in range(heads):
        e = scores(k[0, h], q[0, h])
        num[0, h] = weigh(v[0, h], e)
        den[0, h, 0:1] = column_sum(e)

    for h in range(heads):
        for copy in rows_out[h]:
            copy.wait_recv()

        def neighbour(tile, carry, h=h):
            e = scores(k[0, h], q[tile, h])
            num[tile, h] = weigh(v[0, h], e)
            den[tile, h] = jnp.broadcast_to(column_sum(e), den.shape[2:])
            return carry

        lax.fori_loop(1, 3, neighbour, 0)
    def has_side(slot):
        return column != (COLUMN_TILES - 1) * (slot - 1)

    def add_side(slot, tile, h):
        reach = jnp.where(has_side(slot), 1.0, 0.0) * window[1, head * heads + h].astype(f32)
        e = scores(k[slot, h], q[tile, h])
        num[tile, h] += weigh(v[slot, h], e) * reach
        den[tile, h, 0:1] += column_sum(e) * reach

    def text_phase():
        live[...] = jnp.broadcast_to(mask[...].astype(f32), live.shape).T
        is_first = jnp.where(slab == 0, 1.0, 0.0)
        text_sum.end()

        def text_head(i, h):
            return text_rows[i, h * share : (h + 1) * share].reshape(txt, HEAD_SIZE)

        text_values = []
        for h in range(heads):
            tq = text_head(0, h)
            text_values.append(text_head(2, h).astype(f32).T.astype(bf16))
            e = scores(k[0, h], tq)
            own = scores(text_head(1, h), tq) * live[...] * is_first
            total = weigh(v[0, h], e) + weigh(text_values[h], own)
            tsum_part[h] = total.reshape(tsum_part.shape[1:])
            tsum_part[heads, 0, h : h + 1] = column_sum(e) + column_sum(own)
        attn_sum.start()

        live_wide = jnp.concatenate([live[...]] * (tokens // txt), axis=1)
        for h in range(heads):
            e = scores(text_head(1, h), q[0, h]) * live_wide
            num[0, h] += weigh(text_values[h], e)
            den[0, h, 0:1] += column_sum(e)

    back = []
    for h in range(heads):

        for i in range(2):
            slot = 1 + mod(i + jump_left.astype(jnp.int32), 2)

            @pl.when(has_side(slot))
            def _():
                for sem, dst in ((k_r, k), (v_r, v)):
                    block = dst.at[slot, h]
                    arrived = sem.at[slot - 1, h]
                    remote(block, block, arrived, arrived, slab=slab + 2 * slot - 3).wait_recv()

            def side(tile, carry, h=h, slot=slot):
                add_side(slot, tile, h)
                return carry

            lax.fori_loop(1, 3, side, 0)
        for tile in (1, 2):
            num_out[tile - 1, h] = num[tile, h].astype(bf16)
        now = [
            remote(num_out.at[0, h], num_in.at[1, h], n_s.at[1, h], n_r.at[1, h], slab=above),
            remote(num_out.at[1, h], num_in.at[0, h], n_s.at[0, h], n_r.at[0, h], slab=below),
            remote(den.at[1, h], den_in.at[1, h], d_s.at[1, h], d_r.at[1, h], slab=above),
            remote(den.at[2, h], den_in.at[0, h], d_s.at[0, h], d_r.at[0, h], slab=below),
        ]
        for copy in now:
            copy.start()
        back.append(now)
        if h == 0:
            text_phase()
    qkv.late_relay()

    def own_side(i, carry):
        add_side(1 + i % 2, 0, i // 2)
        return carry

    lax.fori_loop(0, 2 * heads, own_side, 0)
    text_sum.settle()
    for h in range(heads):
        for copy in back[h]:
            copy.wait_recv()
        total, under = num[0, h], den[0, h, 0:1]
        for side_row, exists in ((0, has_above), (1, has_below)):
            reach = jnp.where(exists, 1.0, 0.0) * window[0, head * heads + h].astype(f32)
            total = total + num_in[side_row, h].astype(f32) * reach
            under = under + den_in[side_row, h, 0:1] * reach
        attn[:, h * HEAD_SIZE : (h + 1) * HEAD_SIZE] = (total / under).T.astype(bf16)

    qkv.late_end()
    rows = tokens // nx
    halves = part.shape[2]
    pairs = []

    def send_pair(xx):
        mine = attn[pl.ds(pl.multiple_of(xx * rows, 16), rows), :]
        for half in range(halves):
            weight = gb[half * nz // halves : (half + 1) * nz // halves, :, 2].reshape(model // halves, width)
            product = lax.dot_general(mine, weight, nt, preferred_element_type=f32).astype(bf16)
            for c in range(2):
                part[xx, c, half] = product[c * rows // 2 : (c + 1) * rows // 2]
            pairs.append(
                remote(part.at[xx, 1 - core, half], pair.at[xx, half], pair_s.at[xx, half], pair_r.at[xx, half],
                       head=other)
            )
            pairs[-1].start()

    def pair_sum(xx, half):
        block = pair.at[xx, half]
        remote(block, block, pair_s.at[xx, half], pair_r.at[xx, half], head=other).wait_recv()
        pair[xx, half] = (pair[xx, half].astype(f32) + part[xx, core, half].astype(f32)).astype(bf16)

    fars = [
        remote(pair.at[x_far, 0], far.at[0], far_s.at[0], far_r.at[0], head=right),
        remote(pair.at[x_far, 1], far.at[1], far_s.at[1], far_r.at[1], head=left),
    ]
    send_pair(x_far)
    send_pair(x_right)
    attn_sum.along_z()
    for half in range(halves):
        pair_sum(x_far, half)
        fars[half].start()
    send_pair(x_left)
    nears = [
        remote(pair.at[x_right, 1], near.at[0, 1], near_s.at[0, 1], near_r.at[0, 1], head=right),
        remote(pair.at[x_left, 0], near.at[1, 0], near_s.at[1, 0], near_r.at[1, 0], head=left),
        remote(pair.at[x_right, 0], near.at[0, 0], near_s.at[0, 0], near_r.at[0, 0], head=right),
        remote(pair.at[x_left, 1], near.at[1, 1], near_s.at[1, 1], near_r.at[1, 1], head=left),
    ]
    pair_sum(x_right, 1)
    nears[0].start()
    pair_sum(x_left, 0)
    nears[1].start()
    pair_sum(x_right, 0)
    pair_sum(x_left, 1)
    send_pair(x)
    attn_sum.hand_out_z(lambda total: total)
    for half in range(halves):
        pair_sum(x, half)
    fars[0].wait_recv()
    pair[x_right, 0] = (pair[x_right, 0].astype(f32) + far[0].astype(f32)).astype(bf16)
    nears[2].start()
    fars[1].wait_recv()
    pair[x_left, 1] = (pair[x_left, 1].astype(f32) + far[1].astype(f32)).astype(bf16)
    nears[3].start()
    qkv.settle()
    attn_sum.hand_out_y()
    for copy in (*sum(rows_out, ()), *sum(back, []), *pairs):
        copy.wait_send()

    @pl.when(has_right)
    def _():
        for copy in to_right:
            copy.wait_send()

    @pl.when(has_left)
    def _():
        for copy in to_left:
            copy.wait_send()

    for copy in nears:
        copy.wait_recv()
    for half in range(halves):
        at = half * model // halves
        out[:, at : at + model // halves] = (
            pair[x, half].astype(f32) + near[0, half].astype(f32) + near[1, half].astype(f32)
        ).astype(bf16)

    attn_sum.end()
    for h in range(heads):
        total = text_out[h].reshape(HEAD_SIZE, txt) / text_out[heads, 0, h : h + 1]
        text_final[:, h * HEAD_SIZE : (h + 1) * HEAD_SIZE] = total.T.astype(bf16)
    attn_sum.settle()
    for copy in (*fars, *nears):
        copy.wait_send()


def run_whole(slab_count, head_count, operands):
    video, text, wq = operands[0], operands[1], operands[2]
    depth, width = wq.shape
    tokens, model = video.shape
    txt = text.shape[0]
    heads = width // HEAD_SIZE
    nz, nx = slab_count // Y, head_count // 2
    rows = tokens // head_count
    bf16, f32 = jnp.bfloat16, jnp.float32
    text_block = jax.ShapeDtypeStruct((3, nz, txt * heads // nz, HEAD_SIZE), bf16)
    sum_block = jax.ShapeDtypeStruct((heads + 1, nz, HEAD_SIZE // nz, txt), f32)
    half = model // 2
    vmem = pl.BlockSpec(memory_space=VMEM)
    return pl.pallas_call(
        whole_kernel,
        out_shape=(
            jax.ShapeDtypeStruct((rows, model), bf16),
            jax.ShapeDtypeStruct((txt, width), bf16),
        ),
        in_specs=[pl.BlockSpec(memory_space=pltpu.HBM)] * OPERANDS,
        out_specs=(vmem, vmem),
        scratch_shapes=[
            *(VMEM(a.shape, a.dtype) for a in operands[:-1]),
            pltpu.SMEM(operands[-1].shape, operands[-1].dtype),
            DMA((OPERANDS,)),
            VMEM((3, depth, width), bf16),
            VMEM((nz, Y, depth, width), bf16),
            VMEM((nz, Y, 3, depth, width), bf16),
            VMEM((tokens, model), bf16),
            VMEM((txt, 2 * LANES), bf16),
            VMEM((2 * LANES, 3 * width), bf16),
            VMEM(text_block.shape, bf16),
            VMEM(text_block.shape, bf16),
            VMEM((tokens, 3 * width), f32),
            VMEM((3, heads, tokens, HEAD_SIZE), bf16),
            VMEM((3, heads, tokens, HEAD_SIZE), bf16),
            VMEM((3, heads, HEAD_SIZE, tokens), bf16),
            VMEM((3, heads, HEAD_SIZE, tokens), f32),
            VMEM((3, heads, 8, tokens), f32),
            VMEM((2, heads, HEAD_SIZE, tokens), bf16),
            VMEM((2, heads, HEAD_SIZE, tokens), bf16),
            VMEM((2, heads, 8, tokens), f32),
            VMEM((tokens, width), bf16),
            VMEM((txt, txt), f32),
            VMEM(sum_block.shape, f32),
            VMEM(sum_block.shape, f32),
            VMEM((nx, 2, 2, rows, half), bf16),
            VMEM((nx, 2, rows, half), bf16),
            VMEM((2, rows, half), bf16),
            VMEM((2, 2, rows, half), bf16),
            *TorusGather.scratch(nz),
            *SlabSum.scratch(text_block),
            *SlabSum.scratch(sum_block),
            *[DMA((2, heads))] * 10,
            DMA((nx, 2)), DMA((nx, 2)), DMA((2,)), DMA((2,)), DMA((2, 2)), DMA((2, 2)),
        ],
        compiler_params=pltpu.CompilerParams(
            collective_id=0, has_side_effects=True, vmem_limit_bytes=32 * MIB
        ),
        name="whole",
    )(*(pltpu.with_memory_space_constraint(a, pltpu.HBM) for a in operands))


def on_device(
    video_token_state,
    text_tokens,
    text_mask,
    head_window,
    video_query_weight,
    video_key_weight,
    video_value_weight,
    wout_video,
    wquery_text,
    wkey_text,
    wvalue_text,
    video_query_gain,
    video_key_gain,
    qgain_text,
    kgain_text,
):
    operands = (
        video_token_state, text_tokens,
        video_query_weight, video_key_weight, video_value_weight, wout_video.T,
        wquery_text, wkey_text, wvalue_text,
        *(row.reshape(1, -1) for row in (video_query_gain, video_key_gain, qgain_text, kgain_text, text_mask)),
        head_window.T,
    )
    return run_whole(lax.axis_size("slab"), lax.axis_size("head"), operands)


def solution(mesh):
    return jax.shard_map(
        on_device,
        mesh=mesh,
        in_specs=(
            P("slab", None),
            P(),
            P(),
            P(),
            P("slab", "head"),
            P("slab", "head"),
            P("slab", "head"),
            P("head", "slab"),
            P("slab", "head"),
            P("slab", "head"),
            P("slab", "head"),
            P(),
            P(),
            P(),
            P(),
        ),
        out_specs=(P(("slab", "head"), None), P(None, "head")),
        check_vma=False,
    )
```

```python
import functools
import math

import jax
import jax.numpy as jnp
from jax import lax
from jax.experimental import pallas as pl
from jax.experimental.pallas import tpu as pltpu
from jax.sharding import PartitionSpec as P

HEAD_SIZE = 128
COLUMN_TILES = 8
Y = 4
MIB = 1 << 20
LANES = 128
VMEM = pltpu.VMEM
DMA = pltpu.SemaphoreType.DMA

norm_eps = 1e-06


def mod(a, n):
    return lax.rem(a, jnp.int32(n))


def remote(src, dst, send, recv, **device):
    return pltpu.make_async_remote_copy(
        src_ref=src, dst_ref=dst, send_sem=send, recv_sem=recv,
        device_id=device, device_id_type=pl.DeviceIdType.MESH,
    )


def greet(slabs=(), heads=()):
    barrier = pltpu.get_barrier_semaphore()
    for slab in slabs:
        pl.semaphore_signal(barrier, 1, device_id={"slab": slab}, device_id_type=pl.DeviceIdType.MESH)
    for head in heads:
        pl.semaphore_signal(barrier, 1, device_id={"head": head}, device_id_type=pl.DeviceIdType.MESH)
    return barrier


def when(condition, step):
    if isinstance(condition, bool):
        if condition:
            step()
    else:
        pl.when(condition)(step)


def hello_slab(z, y, nz):
    barrier = pltpu.get_barrier_semaphore()

    def greet_one(slab):
        pl.semaphore_signal(barrier, 1, device_id={"slab": slab}, device_id_type=pl.DeviceIdType.MESH)

    for d in range(1, Y):
        greet_one(z * Y + mod(y + d, Y))

    def body(d, carry):
        greet_one(mod(z + d, nz) * Y + y)
        return carry

    lax.fori_loop(1, nz, body, 0)
    return barrier, Y - 1 + nz - 1


class SlabSum:
    @staticmethod
    def scratch(block):
        owners, nz, rows, lanes = block.shape
        return [
            VMEM((Y, nz, rows, lanes), block.dtype),
            VMEM((nz, rows, lanes), block.dtype),
            VMEM((nz, rows, lanes), block.dtype),
            DMA((2, 2, Y)),
            DMA((2, 2)),
        ]

    def __init__(self, part, out, scratch):
        self.part, self.out = part, out
        self.from_y, self.sum_y, self.from_z, self.ysem, self.zsem = scratch
        self.owners, self.nz = part.shape[:2]
        slab = lax.axis_index("slab")
        self.z, self.y = slab // Y, mod(slab, Y)

    def _owns(self, y):
        return True if self.owners == Y else y < self.owners

    def _y(self, d, give):
        y, to = self.y, mod(self.y + d, Y)
        src = self.out.at[y] if give else self.part.at[to]
        dst = self.out.at[y] if give else self.from_y.at[y]
        return remote(src, dst, self.ysem.at[give, 0, to], self.ysem.at[give, 1, y], slab=self.z * Y + to)

    def _y_in(self, d, give):
        of = mod(self.y + d, Y)
        dst = self.out.at[of] if give else self.from_y.at[of]
        return remote(dst, dst, self.ysem.at[give, 0, of], self.ysem.at[give, 1, of], slab=self.z * Y + of)

    def _z(self, d, give):
        z, to = self.z, mod(self.z + d, self.nz)
        src = self.out.at[self.y, z] if give else self.sum_y.at[to]
        dst = self.out.at[self.y, z] if give else self.from_z.at[z]
        return remote(src, dst, self.zsem.at[give, 0], self.zsem.at[give, 1], slab=to * Y + self.y)

    def _all_z(self, give):
        blocks = self.from_z.at[pl.ds(0, self.nz - 1)]
        to = mod(self.z + 1, self.nz)
        return remote(blocks, blocks, self.zsem.at[give, 0], self.zsem.at[give, 1], slab=to * Y + self.y)

    def _each_z(self, step):
        def body(d, carry):
            step(d)
            return carry

        lax.fori_loop(1, self.nz, body, 0)

    def start(self):
        for d in range(1, Y):
            when(self._owns(mod(self.y + d, Y)), lambda: self._y(d, 0).start())

    def along_z(self):
        def step():
            for d in range(1, Y):
                self._y_in(d, 0).wait_recv()
            total = self.part[self.y].astype(jnp.float32)
            for d in range(1, Y):
                total = total + self.from_y[mod(self.y + d, Y)].astype(jnp.float32)
            self.sum_y[...] = total.astype(self.sum_y.dtype)
            self._each_z(lambda d: self._z(d, 0).start())

        when(self._owns(self.y), step)

    def hand_out_z(self, finish):
        def step():
            self._all_z(0).wait_recv()
            total = self.sum_y[self.z].astype(jnp.float32)
            for d in range(1, self.nz):
                total = total + self.from_z[mod(self.z + d, self.nz)].astype(jnp.float32)
            self.out[self.y, self.z] = finish(total).astype(self.out.dtype)
            self._each_z(lambda d: self._z(d, 1).start())

        when(self._owns(self.y), step)

    def hand_out_y(self):
        def step():
            self._all_z(1).wait_recv()
            for d in range(1, Y):
                self._y(d, 1).start()

        when(self._owns(self.y), step)

    def end(self):
        for d in range(1, Y):
            when(self._owns(mod(self.y + d, Y)), lambda: self._y_in(d, 1).wait_recv())

    def settle(self):
        for d in range(1, Y):
            when(self._owns(mod(self.y + d, Y)), lambda: self._y(d, 0).wait_send())

        def mine():
            for d in range(1, Y):
                self._y(d, 1).wait_send()

            self._all_z(0).wait_send()
            self._all_z(1).wait_send()

        when(self._owns(self.y), mine)


class TorusGather:
    RELAYED = 6
    NEAR = 5

    @staticmethod
    def scratch(nz):
        return [
            DMA((1,)), DMA((nz, 2)), DMA((3,)), DMA((3,)),
            DMA((1,)), DMA((nz,)), DMA((1,)), DMA((2, nz)), DMA((1,)), DMA((2,)), DMA((3,)),
            DMA((2, 2)), DMA((2, 2)), DMA((2,)), DMA((2,)),
        ]

    def __init__(self, wa, wb, ga, gb, sems):
        self.wa, self.wb, self.ga, self.gb = wa, wb, ga, gb
        (self.az_s, self.az_r, self.ay_s, self.ay_r, self.bz_s, self.bz_r,
         self.by_s, self.by_r, self.bo_s, self.bo_r, self.own_sem,
         self.ly_s, self.ly_r, self.lo_s, self.lo_r) = sems
        self.nz = nz = gb.shape[0]
        self.half = nz // 2
        slab = lax.axis_index("slab")
        self.z, self.y = z, y = slab // Y, mod(slab, Y)
        self.next = mod(z + 1, nz), mod(z + nz - 1, nz)
        self.right, self.left, self.across = mod(y + 1, Y), mod(y + Y - 1, Y), mod(y + 2, Y)
        self.sides = self.right, self.left
        self.parts = (pl.ds(0, self.half), pl.ds(self.half, self.half))
        self.sent = []

    def _go(self, copy):
        copy.start()
        self.sent.append(copy)

    def _landed(self, dst, sem):
        remote(dst, dst, self.own_sem.at[2], sem, slab=self.z * Y + self.right).wait_recv()

    def _pair(self, origin, p):
        return self.ga.at[origin, pl.ds(2 * p, 2)]

    def _a_z(self, origin, p, way):
        block = self._pair(origin, p)
        remote(block, block, self.az_s.at[0], self.az_r.at[origin, p],
               slab=self.next[way] * Y + self.y).start()

    def _b_z(self, origin, src, way):
        remote(src, self.gb.at[origin, self.y], self.bz_s.at[0], self.bz_r.at[origin],
               slab=self.next[way] * Y + self.y).start()

    def _two(self, origin, j):
        return self.gb.at[origin, j, pl.ds(0, 2)]

    def _b_y(self, origin, src):
        for way, to in enumerate(self.sides):
            remote(src, self._two(origin, self.y), self.by_s.at[0], self.by_r.at[way, origin],
                   slab=self.z * Y + to).start()

    def _b_relay(self, origin, t):
        self._landed(self._two(origin, self.left), self.by_r.at[0, origin])
        self._landed(self._two(origin, self.right), self.by_r.at[1, origin])
        turn = 1 - 2 * mod(origin, 2)
        block = self._two(origin, mod(self.y - turn + Y, Y))
        remote(block, block, self.bo_s.at[0], self.bo_r.at[int(t > self.NEAR)],
               slab=self.z * Y + mod(self.y + turn + Y, Y)).start()

    def start(self, meanwhile):
        z, y, wa, wb = self.z, self.y, self.wa, self.wb
        self._b_z(z, wb, 0)
        self._b_z(z, wb, 1)
        for i, to in enumerate((self.right, self.left, self.across)):
            self._go(remote(wa, self.ga.at[z, y], self.ay_s.at[i], self.ay_r.at[i], slab=z * Y + to))
        self.own_a = pltpu.make_async_copy(wa, self.ga.at[z, y], self.own_sem.at[0])
        self.own_a.start()
        self._b_y(z, wb.at[pl.ds(0, 2)])
        self.own_b = pltpu.make_async_copy(wb, self.gb.at[z, y], self.own_sem.at[1])
        self.own_b.start()
        meanwhile()
        odd = mod(y, 2)
        self._landed(self.ga.at[z, y + 1 - 2 * odd], self.ay_r.at[1 - odd])
        self.own_a.wait()
        self._a_z(z, y // 2, 0)
        self._a_z(z, y // 2, 1)
        self._landed(self.ga.at[z, mod(y + Y - 1 + 2 * odd, Y)], self.ay_r.at[odd])
        self._landed(self.ga.at[z, self.across], self.ay_r.at[2])
        self._a_z(z, 1 - y // 2, 0)
        self._a_z(z, 1 - y // 2, 1)

    def step(self, t):
        nz, half, y = self.nz, self.half, self.y
        ways = [(mod(self.z - t + nz, nz), 0, half)]
        if t < half:
            ways.append((mod(self.z + t, nz), 1, half - 1))
        for origin, way, last in ways:
            block = self.gb.at[origin, y]
            self._landed(block, self.bz_r.at[origin])
            if t < last:
                self._b_z(origin, block, way)
        if t > self.RELAYED:
            self._along_y(ways, t)
        for p in (y // 2, 1 - y // 2):
            for origin, way, last in ways:
                self._landed(self._pair(origin, p), self.az_r.at[origin, p])
                if t < last:
                    self._a_z(origin, p, way)
        if t <= self.RELAYED:
            self._along_y(ways, t)
        if t > 1:
            self._b_relay(mod(self.z - t + 2 + nz, nz), t - 2)
            if t > 2:
                self._b_relay(mod(self.z + t - 2, nz), t - 2)

    def _along_y(self, ways, t):
        for origin, _, _ in ways:
            two = self._two(origin, self.y)
            self._b_y(origin, two)
            if t > self.RELAYED:
                remote(two, two, self.bo_s.at[0], self.bo_r.at[1],
                       slab=self.z * Y + self.across).start()

    def near_landed(self):
        self._landed(self.gb.at[pl.ds(0, 2 * self.NEAR + 1), 0, pl.ds(0, 2)], self.bo_r.at[0])

    def far_landed(self):
        for t in range(self.RELAYED + 1, self.half + 1):
            for origin in (mod(self.z - t + self.nz, self.nz), mod(self.z + t, self.nz))[: 1 + (t < self.half)]:
                self._landed(self._two(origin, self.left), self.by_r.at[0, origin])
                self._landed(self._two(origin, self.right), self.by_r.at[1, origin])
        self._landed(self.gb.at[pl.ds(0, self.nz - 2 * self.NEAR - 1), 0, pl.ds(0, 2)], self.bo_r.at[1])

    def _late(self, part, j):
        return self.gb.at[self.parts[part], j, 2]

    def late_start(self, turn):
        for way in range(2):
            part = way if turn == 0 else 1 - way
            block = self._late(part, self.y)
            self._go(remote(block, block, self.ly_s.at[way, part], self.ly_r.at[way, part],
                            slab=self.z * Y + self.sides[way]))

    def late_relay(self):
        for way in range(2):
            block = self._late(way, self.sides[1 - way])
            self._landed(block, self.ly_r.at[way, way])
            self._go(remote(block, block, self.lo_s.at[way], self.lo_r.at[way], slab=self.z * Y + self.sides[way]))

    def late_end(self):
        for way in range(2):
            self._landed(self._late(1 - way, self.sides[1 - way]), self.ly_r.at[way, 1 - way])
        for way in range(2):
            self._landed(self._late(way, self.across), self.lo_r.at[way])

    def settle(self):
        nz, one, two = self.nz, pl.ds(0, 1), pl.ds(0, 2)
        for block, sem in (
            (self.ga.at[pl.ds(0, nz - 1)], self.az_s),
            (self.gb.at[pl.ds(0, nz - 1), one], self.bz_s),
            (self.gb.at[:, two, two], self.by_s),
            (self.gb.at[:, one, two], self.bo_s),
        ):
            remote(block, block, sem.at[0], self.own_sem.at[2], slab=self.z * Y + self.right).wait_send()
        for copy in self.sent:
            copy.wait_send()


def row_scale(values):
    return lax.rsqrt(jnp.mean(values * values, axis=-1, keepdims=True) + norm_eps)


OPERANDS = 15
FETCH_ORDER = (2, 3, 4, 5, 0, 1, 6, 7, 8, 9, 10, 11, 12, 13, 14)
QKV_SEMS = 15


def whole_kernel(*refs):
    f32, bf16 = jnp.float32, jnp.bfloat16

    def take(count):
        nonlocal refs
        some, refs = refs[:count], refs[count:]
        return some

    fetched = take(OPERANDS)
    out, text_final = take(2)
    held = take(OPERANDS)
    video, text, wq, wk, wv, wo, twq, twk, twv, qg, kg, tqg, tkg, mask, window = held
    (fetch_sem, wb, ga, gb, normed, tnormed, tweight, text_part, text_rows, acc) = take(10)
    (q, k, v, num, den, num_out, num_in, den_in, attn, live, tsum_part, text_out) = take(12)
    (part, pair, far, near) = take(4)
    qkv = TorusGather(wq, wb, ga, gb, take(QKV_SEMS))
    text_sum = SlabSum(text_part, text_rows, take(5))
    attn_sum = SlabSum(tsum_part, text_out, take(5))
    q_s, q_r, k_s, k_r, v_s, v_r, n_s, n_r, d_s, d_r = take(10)
    pair_s, pair_r, far_s, far_r, near_s, near_r = take(6)

    nz = gb.shape[0]
    nx = part.shape[0]
    slab, head = lax.axis_index("slab"), lax.axis_index("head")
    slab_count = lax.axis_size("slab")
    z, y = slab // Y, mod(slab, Y)
    row, column = slab // COLUMN_TILES, mod(slab, COLUMN_TILES)
    above, below = mod(slab + slab_count - COLUMN_TILES, slab_count), mod(slab + COLUMN_TILES, slab_count)
    has_left, has_right = column > 0, column < COLUMN_TILES - 1
    has_above, has_below = row > 0, row < slab_count // COLUMN_TILES - 1
    jump_left, jump_right = has_left & (y == 0), has_right & (y == Y - 1)
    x, core = head // 2, mod(head, 2)
    x_right, x_left, x_far = mod(x + 1, nx), mod(x + nx - 1, nx), mod(x + 2, nx)
    other, right, left = x * 2 + 1 - core, x_right * 2 + core, x_left * 2 + core
    depth, width = wq.shape
    heads = width // HEAD_SIZE
    tokens, model = video.shape
    txt = text.shape[0]
    score_scale = math.log2(math.e) / math.sqrt(HEAD_SIZE)
    steps = nz // 2
    nt = (((1,), (1,)), ((), ()))

    fetches = [
        pltpu.make_async_copy(src, dst, fetch_sem.at[i]) for i, (src, dst) in enumerate(zip(fetched, held))
    ]
    for i in FETCH_ORDER:
        fetches[i].start()

    barrier, peers = hello_slab(z, y, nz)
    greet((), (other, right, left))

    @pl.when(jump_left)
    def _():
        greet((slab - 1,))

    @pl.when(jump_right)
    def _():
        greet((slab + 1,))

    for i in FETCH_ORDER[:4]:
        fetches[i].wait()
    for i, weight in enumerate((wk, wv, wo)):
        wb[i] = weight[...]
    pl.semaphore_wait(barrier, peers + 3 + jump_left.astype(jnp.int32) + jump_right.astype(jnp.int32))
    def normalize_video(i, carry):
        at = pl.ds(pl.multiple_of(i * 16, 16), 16)
        values = video[at, :].astype(f32)
        center = values - jnp.mean(values, axis=-1, keepdims=True)
        normed[at, :] = (center * row_scale(center)).astype(bf16)
        return carry

    blocks = tokens // 16
    early = blocks // 4

    def first_rows():
        fetches[0].wait()
        lax.fori_loop(0, early, normalize_video, 0)

    qkv.start(first_rows)

    span = tweight.shape[0]
    aligned = jnp.minimum(slab * depth // LANES * LANES, model - span)
    aligned = pl.multiple_of(aligned, LANES)
    offset = pl.multiple_of(slab * depth - aligned, 16)
    share = nz // heads

    def fill_text_weights():
        tweight[...] = jnp.zeros_like(tweight)
        for i, weight in enumerate((twq, twk, twv)):
            tweight[pl.ds(offset, depth), i * width : (i + 1) * width] = weight[...]

    def normalize_text(i, carry):
        at = pl.ds(pl.multiple_of(i * 16, 16), 16)
        values = text[at, :].astype(f32)
        mean = jnp.mean(values, axis=-1, keepdims=True)
        scale = row_scale(values - mean)
        columns = text[at, pl.ds(aligned, span)].astype(f32)
        tnormed[at, :] = ((columns - mean) * scale).astype(bf16)
        return carry

    def multiply_text():
        for i in range(3):
            product = jnp.dot(
                tnormed[...], tweight[:, i * width : (i + 1) * width], preferred_element_type=f32
            ).astype(bf16)
            for h in range(heads):
                block = product[:, h * HEAD_SIZE : (h + 1) * HEAD_SIZE]
                text_part[i, h * share : (h + 1) * share] = block.reshape(share, *text_part.shape[2:])

    def finish_text(total):
        gain = jnp.where(y == 0, tqg[...], tkg[...])
        return jnp.where(y == 2, total, total * row_scale(total) * gain)

    for t in range(1, steps + 1):
        qkv.step(t)
        if t == 1:
            for i in FETCH_ORDER[5:]:
                fetches[i].wait()
            fill_text_weights()
            lax.fori_loop(0, txt // 32, normalize_text, 0)
        if t == 2:
            lax.fori_loop(txt // 32, txt // 16, normalize_text, 0)
            multiply_text()
            text_sum.start()
        if t == 4:
            text_sum.along_z()
        if t == 7:
            text_sum.hand_out_z(finish_text)
        if t > 2:
            rest, steps_left = blocks - early, steps - 2
            lax.fori_loop(
                early + (t - 3) * rest // steps_left, early + (t - 2) * rest // steps_left, normalize_video, 0
            )

    qkv.own_b.wait()
    qkv.late_start(0)

    acc[...] = jnp.zeros_like(acc)
    group = 4 if nz % 4 == 0 else nz
    span = group * Y * depth

    def multiply_query(c, carry):
        rows = normed[:, pl.ds(pl.multiple_of(c * span, span), span)]
        acc[:, :width] += jnp.dot(
            rows, ga[pl.ds(c * group, group)].reshape(span, width), preferred_element_type=f32
        )
        return carry

    lax.fori_loop(0, nz // group, multiply_query, 0)
    rows_out = []
    for h in range(heads):
        values = acc[:, h * HEAD_SIZE : (h + 1) * HEAD_SIZE]
        q[0, h] = (values * row_scale(values) * qg[...]).astype(bf16)
        to_below = remote(q.at[0, h], q.at[1, h], q_s.at[0, h], q_r.at[0, h], slab=below)
        to_above = remote(q.at[0, h], q.at[2, h], q_s.at[1, h], q_r.at[1, h], slab=above)
        to_below.start()
        to_above.start()
        rows_out.append((to_below, to_above))

    pair_depth = 2 * Y * depth

    def multiply_rest(i, j):
        at = mod(z // 2 + i + nz // 2 - 2, nz // 2)
        rows = normed[:, pl.ds(pl.multiple_of(at * pair_depth, pair_depth), pair_depth)]
        acc[:, (j + 1) * width : (j + 2) * width] += jnp.dot(
            rows, gb[pl.ds(at * 2, 2), :, j].reshape(pair_depth, width), preferred_element_type=f32
        )

    def multiply_pairs(first, last, j):
        def body(i, carry):
            multiply_rest(i, j)
            return carry

        lax.fori_loop(first, last, body, 0)

    qkv.near_landed()
    multiply_pairs(0, 5, 0)
    multiply_pairs(0, 5, 1)
    qkv.far_landed()
    multiply_pairs(5, nz // 2, 0)

    to_right, to_left = [], []

    def send_sides(block, send, arrived, h):
        right_now = remote(block.at[0, h], block.at[1, h], send.at[0, h], arrived.at[0, h], slab=slab + 1)
        left_now = remote(block.at[0, h], block.at[2, h], send.at[1, h], arrived.at[1, h], slab=slab - 1)
        pl.when(has_right)(right_now.start)
        pl.when(has_left)(left_now.start)
        to_right.append(right_now)
        to_left.append(left_now)

    for h in range(heads):
        values = acc[:, width + h * HEAD_SIZE : width + (h + 1) * HEAD_SIZE]
        k[0, h] = (values * row_scale(values) * kg[...]).astype(bf16)
        if h == 0:
            send_sides(k, k_s, k_r, h)
    multiply_pairs(5, nz // 2, 1)
    for h in range(heads):
        v[0, h] = acc[:, 2 * width + h * HEAD_SIZE : 2 * width + (h + 1) * HEAD_SIZE].T.astype(bf16)
        if h > 0:
            send_sides(k, k_s, k_r, h)
        send_sides(v, v_s, v_r, h)
    text_sum.hand_out_y()
    qkv.late_start(1)

    @pl.when(jnp.logical_not(has_left))
    def _():
        k[1] = jnp.zeros_like(k[1])
        v[1] = jnp.zeros_like(v[1])

    @pl.when(jnp.logical_not(has_right))
    def _():
        k[2] = jnp.zeros_like(k[2])
        v[2] = jnp.zeros_like(v[2])

    def scores(keys, queries):
        return jnp.exp2(lax.dot_general(keys, queries, nt, preferred_element_type=f32) * score_scale)

    def weigh(values, e):
        return jnp.dot(values, e.astype(bf16), preferred_element_type=f32)

    def column_sum(e):
        return jnp.sum(e, axis=0, keepdims=True)

    tsum_part[heads] = jnp.zeros_like(tsum_part[heads])
    for h in range(heads):
        e = scores(k[0, h], q[0, h])
        num[0, h] = weigh(v[0, h], e)
        den[0, h, 0:1] = column_sum(e)

    for h in range(heads):
        for copy in rows_out[h]:
            copy.wait_recv()

        def neighbour(tile, carry, h=h):
            e = scores(k[0, h], q[tile, h])
            num[tile, h] = weigh(v[0, h], e)
            den[tile, h] = jnp.broadcast_to(column_sum(e), den.shape[2:])
            return carry

        lax.fori_loop(1, 3, neighbour, 0)
    qkv.late_relay()

    def has_side(slot):
        return column != (COLUMN_TILES - 1) * (slot - 1)

    def add_side(slot, tile, h):
        reach = jnp.where(has_side(slot), 1.0, 0.0) * window[1, head * heads + h].astype(f32)
        e = scores(k[slot, h], q[tile, h])
        num[tile, h] += weigh(v[slot, h], e) * reach
        den[tile, h, 0:1] += column_sum(e) * reach

    def text_phase():
        live[...] = jnp.broadcast_to(mask[...].astype(f32), live.shape).T
        is_first = jnp.where(slab == 0, 1.0, 0.0)
        text_sum.end()

        def text_head(i, h):
            return text_rows[i, h * share : (h + 1) * share].reshape(txt, HEAD_SIZE)

        text_values = []
        for h in range(heads):
            tq = text_head(0, h)
            text_values.append(text_head(2, h).astype(f32).T.astype(bf16))
            e = scores(k[0, h], tq)
            own = scores(text_head(1, h), tq) * live[...] * is_first
            total = weigh(v[0, h], e) + weigh(text_values[h], own)
            tsum_part[h] = total.reshape(tsum_part.shape[1:])
            tsum_part[heads, 0, h : h + 1] = column_sum(e) + column_sum(own)
        attn_sum.start()

        live_wide = jnp.concatenate([live[...]] * (tokens // txt), axis=1)
        for h in range(heads):
            e = scores(text_head(1, h), q[0, h]) * live_wide
            num[0, h] += weigh(text_values[h], e)
            den[0, h, 0:1] += column_sum(e)

    back = []
    for h in range(heads):

        for i in range(2):
            slot = 1 + mod(i + jump_left.astype(jnp.int32), 2)

            @pl.when(has_side(slot))
            def _():
                for sem, dst in ((k_r, k), (v_r, v)):
                    block = dst.at[slot, h]
                    arrived = sem.at[slot - 1, h]
                    remote(block, block, arrived, arrived, slab=slab + 2 * slot - 3).wait_recv()

            def side(tile, carry, h=h, slot=slot):
                add_side(slot, tile, h)
                return carry

            lax.fori_loop(1, 3, side, 0)
        for tile in (1, 2):
            num_out[tile - 1, h] = num[tile, h].astype(bf16)
        now = [
            remote(num_out.at[0, h], num_in.at[1, h], n_s.at[1, h], n_r.at[1, h], slab=above),
            remote(num_out.at[1, h], num_in.at[0, h], n_s.at[0, h], n_r.at[0, h], slab=below),
            remote(den.at[1, h], den_in.at[1, h], d_s.at[1, h], d_r.at[1, h], slab=above),
            remote(den.at[2, h], den_in.at[0, h], d_s.at[0, h], d_r.at[0, h], slab=below),
        ]
        for copy in now:
            copy.start()
        back.append(now)

    text_phase()

    def own_side(i, carry):
        add_side(1 + i % 2, 0, i // 2)
        return carry

    lax.fori_loop(0, 2 * heads, own_side, 0)
    text_sum.settle()
    for h in range(heads):
        for copy in back[h]:
            copy.wait_recv()
        total, under = num[0, h], den[0, h, 0:1]
        for side_row, exists in ((0, has_above), (1, has_below)):
            reach = jnp.where(exists, 1.0, 0.0) * window[0, head * heads + h].astype(f32)
            total = total + num_in[side_row, h].astype(f32) * reach
            under = under + den_in[side_row, h, 0:1] * reach
        attn[:, h * HEAD_SIZE : (h + 1) * HEAD_SIZE] = (total / under).T.astype(bf16)

    qkv.late_end()
    rows = tokens // nx
    halves = part.shape[2]
    pairs = []

    def send_pair(xx):
        mine = attn[pl.ds(pl.multiple_of(xx * rows, 16), rows), :]
        for half in range(halves):
            weight = gb[half * nz // halves : (half + 1) * nz // halves, :, 2].reshape(model // halves, width)
            product = lax.dot_general(mine, weight, nt, preferred_element_type=f32).astype(bf16)
            for c in range(2):
                part[xx, c, half] = product[c * rows // 2 : (c + 1) * rows // 2]
            pairs.append(
                remote(part.at[xx, 1 - core, half], pair.at[xx, half], pair_s.at[xx, half], pair_r.at[xx, half],
                       head=other)
            )
            pairs[-1].start()

    def pair_sum(xx, half):
        block = pair.at[xx, half]
        remote(block, block, pair_s.at[xx, half], pair_r.at[xx, half], head=other).wait_recv()
        pair[xx, half] = (pair[xx, half].astype(f32) + part[xx, core, half].astype(f32)).astype(bf16)

    fars = [
        remote(pair.at[x_far, 0], far.at[0], far_s.at[0], far_r.at[0], head=right),
        remote(pair.at[x_far, 1], far.at[1], far_s.at[1], far_r.at[1], head=left),
    ]
    send_pair(x_far)
    send_pair(x_right)
    attn_sum.along_z()
    for half in range(halves):
        pair_sum(x_far, half)
        fars[half].start()
    send_pair(x_left)
    nears = [
        remote(pair.at[x_right, 1], near.at[0, 1], near_s.at[0, 1], near_r.at[0, 1], head=right),
        remote(pair.at[x_left, 0], near.at[1, 0], near_s.at[1, 0], near_r.at[1, 0], head=left),
        remote(pair.at[x_right, 0], near.at[0, 0], near_s.at[0, 0], near_r.at[0, 0], head=right),
        remote(pair.at[x_left, 1], near.at[1, 1], near_s.at[1, 1], near_r.at[1, 1], head=left),
    ]
    pair_sum(x_right, 1)
    nears[0].start()
    pair_sum(x_left, 0)
    nears[1].start()
    pair_sum(x_right, 0)
    pair_sum(x_left, 1)
    send_pair(x)
    attn_sum.hand_out_z(lambda total: total)
    for half in range(halves):
        pair_sum(x, half)
    fars[0].wait_recv()
    pair[x_right, 0] = (pair[x_right, 0].astype(f32) + far[0].astype(f32)).astype(bf16)
    nears[2].start()
    fars[1].wait_recv()
    pair[x_left, 1] = (pair[x_left, 1].astype(f32) + far[1].astype(f32)).astype(bf16)
    nears[3].start()
    qkv.settle()
    attn_sum.hand_out_y()
    for copy in (*sum(rows_out, ()), *sum(back, []), *pairs):
        copy.wait_send()

    @pl.when(has_right)
    def _():
        for copy in to_right:
            copy.wait_send()

    @pl.when(has_left)
    def _():
        for copy in to_left:
            copy.wait_send()

    for copy in nears:
        copy.wait_recv()
    for half in range(halves):
        at = half * model // halves
        out[:, at : at + model // halves] = (
            pair[x, half].astype(f32) + near[0, half].astype(f32) + near[1, half].astype(f32)
        ).astype(bf16)

    attn_sum.end()
    for h in range(heads):
        total = text_out[h].reshape(HEAD_SIZE, txt) / text_out[heads, 0, h : h + 1]
        text_final[:, h * HEAD_SIZE : (h + 1) * HEAD_SIZE] = total.T.astype(bf16)
    attn_sum.settle()
    for copy in (*fars, *nears):
        copy.wait_send()


def run_whole(slab_count, head_count, operands):
    video, text, wq = operands[0], operands[1], operands[2]
    depth, width = wq.shape
    tokens, model = video.shape
    txt = text.shape[0]
    heads = width // HEAD_SIZE
    nz, nx = slab_count // Y, head_count // 2
    rows = tokens // head_count
    bf16, f32 = jnp.bfloat16, jnp.float32
    text_block = jax.ShapeDtypeStruct((3, nz, txt * heads // nz, HEAD_SIZE), bf16)
    sum_block = jax.ShapeDtypeStruct((heads + 1, nz, HEAD_SIZE // nz, txt), f32)
    half = model // 2
    vmem = pl.BlockSpec(memory_space=VMEM)
    return pl.pallas_call(
        whole_kernel,
        out_shape=(
            jax.ShapeDtypeStruct((rows, model), bf16),
            jax.ShapeDtypeStruct((txt, width), bf16),
        ),
        in_specs=[pl.BlockSpec(memory_space=pltpu.HBM)] * OPERANDS,
        out_specs=(vmem, vmem),
        scratch_shapes=[
            *(VMEM(a.shape, a.dtype) for a in operands[:-1]),
            pltpu.SMEM(operands[-1].shape, operands[-1].dtype),
            DMA((OPERANDS,)),
            VMEM((3, depth, width), bf16),
            VMEM((nz, Y, depth, width), bf16),
            VMEM((nz, Y, 3, depth, width), bf16),
            VMEM((tokens, model), bf16),
            VMEM((txt, 2 * LANES), bf16),
            VMEM((2 * LANES, 3 * width), bf16),
            VMEM(text_block.shape, bf16),
            VMEM(text_block.shape, bf16),
            VMEM((tokens, 3 * width), f32),
            VMEM((3, heads, tokens, HEAD_SIZE), bf16),
            VMEM((3, heads, tokens, HEAD_SIZE), bf16),
            VMEM((3, heads, HEAD_SIZE, tokens), bf16),
            VMEM((3, heads, HEAD_SIZE, tokens), f32),
            VMEM((3, heads, 8, tokens), f32),
            VMEM((2, heads, HEAD_SIZE, tokens), bf16),
            VMEM((2, heads, HEAD_SIZE, tokens), bf16),
            VMEM((2, heads, 8, tokens), f32),
            VMEM((tokens, width), bf16),
            VMEM((txt, txt), f32),
            VMEM(sum_block.shape, f32),
            VMEM(sum_block.shape, f32),
            VMEM((nx, 2, 2, rows, half), bf16),
            VMEM((nx, 2, rows, half), bf16),
            VMEM((2, rows, half), bf16),
            VMEM((2, 2, rows, half), bf16),
            *TorusGather.scratch(nz),
            *SlabSum.scratch(text_block),
            *SlabSum.scratch(sum_block),
            *[DMA((2, heads))] * 10,
            DMA((nx, 2)), DMA((nx, 2)), DMA((2,)), DMA((2,)), DMA((2, 2)), DMA((2, 2)),
        ],
        compiler_params=pltpu.CompilerParams(
            collective_id=0, has_side_effects=True, vmem_limit_bytes=32 * MIB
        ),
        name="whole",
    )(*(pltpu.with_memory_space_constraint(a, pltpu.HBM) for a in operands))


def on_device(
    video_token_state,
    text_tokens,
    text_mask,
    head_window,
    video_query_weight,
    video_key_weight,
    video_value_weight,
    wout_video,
    wquery_text,
    wkey_text,
    wvalue_text,
    video_query_gain,
    video_key_gain,
    qgain_text,
    kgain_text,
):
    operands = (
        video_token_state, text_tokens,
        video_query_weight, video_key_weight, video_value_weight, wout_video.T,
        wquery_text, wkey_text, wvalue_text,
        *(row.reshape(1, -1) for row in (video_query_gain, video_key_gain, qgain_text, kgain_text, text_mask)),
        head_window.T,
    )
    return run_whole(lax.axis_size("slab"), lax.axis_size("head"), operands)


def solution(mesh):
    return jax.shard_map(
        on_device,
        mesh=mesh,
        in_specs=(
            P("slab", None),
            P(),
            P(),
            P(),
            P("slab", "head"),
            P("slab", "head"),
            P("slab", "head"),
            P("head", "slab"),
            P("slab", "head"),
            P("slab", "head"),
            P("slab", "head"),
            P(),
            P(),
            P(),
            P(),
        ),
        out_specs=(P(("slab", "head"), None), P(None, "head")),
        check_vma=False,
    )
```

```python
import functools
import math

import jax
import jax.numpy as jnp
from jax import lax
from jax.experimental import pallas as pl
from jax.experimental.pallas import tpu as pltpu
from jax.sharding import PartitionSpec as P

HEAD_SIZE = 128
COLUMN_TILES = 8
Y = 4
MIB = 1 << 20
LANES = 128
VMEM = pltpu.VMEM
DMA = pltpu.SemaphoreType.DMA

norm_eps = 1e-06


def mod(a, n):
    return lax.rem(a, jnp.int32(n))


def remote(src, dst, send, recv, **device):
    return pltpu.make_async_remote_copy(
        src_ref=src, dst_ref=dst, send_sem=send, recv_sem=recv,
        device_id=device, device_id_type=pl.DeviceIdType.MESH,
    )


def greet(slabs=(), heads=()):
    barrier = pltpu.get_barrier_semaphore()
    for slab in slabs:
        pl.semaphore_signal(barrier, 1, device_id={"slab": slab}, device_id_type=pl.DeviceIdType.MESH)
    for head in heads:
        pl.semaphore_signal(barrier, 1, device_id={"head": head}, device_id_type=pl.DeviceIdType.MESH)
    return barrier


def when(condition, step):
    if isinstance(condition, bool):
        if condition:
            step()
    else:
        pl.when(condition)(step)


def hello_slab(z, y, nz):
    barrier = pltpu.get_barrier_semaphore()

    def greet_one(slab):
        pl.semaphore_signal(barrier, 1, device_id={"slab": slab}, device_id_type=pl.DeviceIdType.MESH)

    for d in range(1, Y):
        greet_one(z * Y + mod(y + d, Y))

    def body(d, carry):
        greet_one(mod(z + d, nz) * Y + y)
        return carry

    lax.fori_loop(1, nz, body, 0)
    return barrier, Y - 1 + nz - 1


class SlabSum:
    @staticmethod
    def scratch(block):
        owners, nz, rows, lanes = block.shape
        return [
            VMEM((Y, nz, rows, lanes), block.dtype),
            VMEM((nz, rows, lanes), block.dtype),
            VMEM((nz, rows, lanes), block.dtype),
            DMA((2, 2, Y)),
            DMA((2, 2)),
        ]

    def __init__(self, part, out, scratch):
        self.part, self.out = part, out
        self.from_y, self.sum_y, self.from_z, self.ysem, self.zsem = scratch
        self.owners, self.nz = part.shape[:2]
        slab = lax.axis_index("slab")
        self.z, self.y = slab // Y, mod(slab, Y)

    def _owns(self, y):
        return True if self.owners == Y else y < self.owners

    def _y(self, d, give):
        y, to = self.y, mod(self.y + d, Y)
        src = self.out.at[y] if give else self.part.at[to]
        dst = self.out.at[y] if give else self.from_y.at[y]
        return remote(src, dst, self.ysem.at[give, 0, to], self.ysem.at[give, 1, y], slab=self.z * Y + to)

    def _y_in(self, d, give):
        of = mod(self.y + d, Y)
        dst = self.out.at[of] if give else self.from_y.at[of]
        return remote(dst, dst, self.ysem.at[give, 0, of], self.ysem.at[give, 1, of], slab=self.z * Y + of)

    def _z(self, d, give):
        z, to = self.z, mod(self.z + d, self.nz)
        src = self.out.at[self.y, z] if give else self.sum_y.at[to]
        dst = self.out.at[self.y, z] if give else self.from_z.at[z]
        return remote(src, dst, self.zsem.at[give, 0], self.zsem.at[give, 1], slab=to * Y + self.y)

    def _all_z(self, give):
        blocks = self.from_z.at[pl.ds(0, self.nz - 1)]
        to = mod(self.z + 1, self.nz)
        return remote(blocks, blocks, self.zsem.at[give, 0], self.zsem.at[give, 1], slab=to * Y + self.y)

    def _each_z(self, step):
        def body(d, carry):
            step(d)
            return carry

        lax.fori_loop(1, self.nz, body, 0)

    def start(self):
        for d in range(1, Y):
            when(self._owns(mod(self.y + d, Y)), lambda: self._y(d, 0).start())

    def along_z(self):
        def step():
            for d in range(1, Y):
                self._y_in(d, 0).wait_recv()
            total = self.part[self.y].astype(jnp.float32)
            for d in range(1, Y):
                total = total + self.from_y[mod(self.y + d, Y)].astype(jnp.float32)
            self.sum_y[...] = total.astype(self.sum_y.dtype)
            self._each_z(lambda d: self._z(d, 0).start())

        when(self._owns(self.y), step)

    def hand_out_z(self, finish):
        def step():
            self._all_z(0).wait_recv()
            total = self.sum_y[self.z].astype(jnp.float32)
            for d in range(1, self.nz):
                total = total + self.from_z[mod(self.z + d, self.nz)].astype(jnp.float32)
            self.out[self.y, self.z] = finish(total).astype(self.out.dtype)
            self._each_z(lambda d: self._z(d, 1).start())

        when(self._owns(self.y), step)

    def hand_out_y(self):
        def step():
            self._all_z(1).wait_recv()
            for d in range(1, Y):
                self._y(d, 1).start()

        when(self._owns(self.y), step)

    def end(self):
        for d in range(1, Y):
            when(self._owns(mod(self.y + d, Y)), lambda: self._y_in(d, 1).wait_recv())

    def settle(self):
        for d in range(1, Y):
            when(self._owns(mod(self.y + d, Y)), lambda: self._y(d, 0).wait_send())

        def mine():
            for d in range(1, Y):
                self._y(d, 1).wait_send()

            self._all_z(0).wait_send()
            self._all_z(1).wait_send()

        when(self._owns(self.y), mine)


class TorusGather:
    RELAYED = 6
    NEAR = 5

    @staticmethod
    def scratch(nz):
        return [
            DMA((1,)), DMA((nz, 2)), DMA((3,)), DMA((3,)),
            DMA((1,)), DMA((nz,)), DMA((1,)), DMA((2, nz)), DMA((1,)), DMA((2,)), DMA((3,)),
            DMA((2, 2)), DMA((2, 2)), DMA((2,)), DMA((2,)),
        ]

    def __init__(self, wa, wb, ga, gb, sems):
        self.wa, self.wb, self.ga, self.gb = wa, wb, ga, gb
        (self.az_s, self.az_r, self.ay_s, self.ay_r, self.bz_s, self.bz_r,
         self.by_s, self.by_r, self.bo_s, self.bo_r, self.own_sem,
         self.ly_s, self.ly_r, self.lo_s, self.lo_r) = sems
        self.nz = nz = gb.shape[0]
        self.half = nz // 2
        slab = lax.axis_index("slab")
        self.z, self.y = z, y = slab // Y, mod(slab, Y)
        self.next = mod(z + 1, nz), mod(z + nz - 1, nz)
        self.right, self.left, self.across = mod(y + 1, Y), mod(y + Y - 1, Y), mod(y + 2, Y)
        self.sides = self.right, self.left
        self.parts = (pl.ds(0, self.half), pl.ds(self.half, self.half))
        self.sent = []

    def _go(self, copy):
        copy.start()
        self.sent.append(copy)

    def _landed(self, dst, sem):
        remote(dst, dst, self.own_sem.at[2], sem, slab=self.z * Y + self.right).wait_recv()

    def _pair(self, origin, p):
        return self.ga.at[origin, pl.ds(2 * p, 2)]

    def _a_z(self, origin, p, way):
        block = self._pair(origin, p)
        remote(block, block, self.az_s.at[0], self.az_r.at[origin, p],
               slab=self.next[way] * Y + self.y).start()

    def _b_z(self, origin, src, way):
        remote(src, self.gb.at[origin, self.y], self.bz_s.at[0], self.bz_r.at[origin],
               slab=self.next[way] * Y + self.y).start()

    def _two(self, origin, j):
        return self.gb.at[origin, j, pl.ds(0, 2)]

    def _b_y(self, origin, src):
        for way, to in enumerate(self.sides):
            remote(src, self._two(origin, self.y), self.by_s.at[0], self.by_r.at[way, origin],
                   slab=self.z * Y + to).start()

    def _b_relay(self, origin, t):
        self._landed(self._two(origin, self.left), self.by_r.at[0, origin])
        self._landed(self._two(origin, self.right), self.by_r.at[1, origin])
        turn = 1 - 2 * mod(origin, 2)
        block = self._two(origin, mod(self.y - turn + Y, Y))
        remote(block, block, self.bo_s.at[0], self.bo_r.at[int(t > self.NEAR)],
               slab=self.z * Y + mod(self.y + turn + Y, Y)).start()

    def start(self, meanwhile):
        z, y, wa, wb = self.z, self.y, self.wa, self.wb
        self._b_z(z, wb, 0)
        self._b_z(z, wb, 1)
        for i, to in enumerate((self.right, self.left, self.across)):
            self._go(remote(wa, self.ga.at[z, y], self.ay_s.at[i], self.ay_r.at[i], slab=z * Y + to))
        self.own_a = pltpu.make_async_copy(wa, self.ga.at[z, y], self.own_sem.at[0])
        self.own_a.start()
        self._b_y(z, wb.at[pl.ds(0, 2)])
        self.own_b = pltpu.make_async_copy(wb, self.gb.at[z, y], self.own_sem.at[1])
        self.own_b.start()
        meanwhile()
        odd = mod(y, 2)
        self._landed(self.ga.at[z, y + 1 - 2 * odd], self.ay_r.at[1 - odd])
        self.own_a.wait()
        self._a_z(z, y // 2, 0)
        self._a_z(z, y // 2, 1)
        self._landed(self.ga.at[z, mod(y + Y - 1 + 2 * odd, Y)], self.ay_r.at[odd])
        self._landed(self.ga.at[z, self.across], self.ay_r.at[2])
        self._a_z(z, 1 - y // 2, 0)
        self._a_z(z, 1 - y // 2, 1)

    def step(self, t):
        nz, half, y = self.nz, self.half, self.y
        ways = [(mod(self.z - t + nz, nz), 0, half)]
        if t < half:
            ways.append((mod(self.z + t, nz), 1, half - 1))
        for origin, way, last in ways:
            block = self.gb.at[origin, y]
            self._landed(block, self.bz_r.at[origin])
            if t < last:
                self._b_z(origin, block, way)
        if t > self.RELAYED:
            self._along_y(ways, t)
        for p in (y // 2, 1 - y // 2):
            for origin, way, last in ways:
                self._landed(self._pair(origin, p), self.az_r.at[origin, p])
                if t < last:
                    self._a_z(origin, p, way)
        if t <= self.RELAYED:
            self._along_y(ways, t)
        if t > 1:
            self._b_relay(mod(self.z - t + 2 + nz, nz), t - 2)
            if t > 2:
                self._b_relay(mod(self.z + t - 2, nz), t - 2)

    def _along_y(self, ways, t):
        for origin, _, _ in ways:
            two = self._two(origin, self.y)
            self._b_y(origin, two)
            if t > self.RELAYED:
                remote(two, two, self.bo_s.at[0], self.bo_r.at[1],
                       slab=self.z * Y + self.across).start()

    def near_landed(self):
        self._landed(self.gb.at[pl.ds(0, 2 * self.NEAR + 1), 0, pl.ds(0, 2)], self.bo_r.at[0])

    def far_landed(self):
        for t in range(self.RELAYED + 1, self.half + 1):
            for origin in (mod(self.z - t + self.nz, self.nz), mod(self.z + t, self.nz))[: 1 + (t < self.half)]:
                self._landed(self._two(origin, self.left), self.by_r.at[0, origin])
                self._landed(self._two(origin, self.right), self.by_r.at[1, origin])
        self._landed(self.gb.at[pl.ds(0, self.nz - 2 * self.NEAR - 1), 0, pl.ds(0, 2)], self.bo_r.at[1])

    def _late(self, part, j):
        return self.gb.at[self.parts[part], j, 2]

    def late_start(self, turn):
        for way in range(2):
            part = way if turn == 0 else 1 - way
            block = self._late(part, self.y)
            self._go(remote(block, block, self.ly_s.at[way, part], self.ly_r.at[way, part],
                            slab=self.z * Y + self.sides[way]))

    def late_relay(self):
        for way in range(2):
            block = self._late(way, self.sides[1 - way])
            self._landed(block, self.ly_r.at[way, way])
            self._go(remote(block, block, self.lo_s.at[way], self.lo_r.at[way], slab=self.z * Y + self.sides[way]))

    def late_end(self):
        for way in range(2):
            self._landed(self._late(1 - way, self.sides[1 - way]), self.ly_r.at[way, 1 - way])
        for way in range(2):
            self._landed(self._late(way, self.across), self.lo_r.at[way])

    def settle(self):
        nz, one, two = self.nz, pl.ds(0, 1), pl.ds(0, 2)
        for block, sem in (
            (self.ga.at[pl.ds(0, nz - 1)], self.az_s),
            (self.gb.at[pl.ds(0, nz - 1), one], self.bz_s),
            (self.gb.at[:, two, two], self.by_s),
            (self.gb.at[:, one, two], self.bo_s),
        ):
            remote(block, block, sem.at[0], self.own_sem.at[2], slab=self.z * Y + self.right).wait_send()
        for copy in self.sent:
            copy.wait_send()


def row_scale(values):
    return lax.rsqrt(jnp.mean(values * values, axis=-1, keepdims=True) + norm_eps)


OPERANDS = 15
FETCH_ORDER = (2, 3, 4, 5, 0, 1, 6, 7, 8, 9, 10, 11, 12, 13, 14)
QKV_SEMS = 15


def whole_kernel(*refs):
    f32, bf16 = jnp.float32, jnp.bfloat16

    def take(count):
        nonlocal refs
        some, refs = refs[:count], refs[count:]
        return some

    fetched = take(OPERANDS)
    out, text_final = take(2)
    held = take(OPERANDS)
    video, text, wq, wk, wv, wo, twq, twk, twv, qg, kg, tqg, tkg, mask, window = held
    (fetch_sem, wb, ga, gb, normed, tnormed, tweight, text_part, text_rows, acc) = take(10)
    (q, k, v, num, den, num_out, num_in, den_in, attn, live, tsum_part, text_out) = take(12)
    (part, pair, far, near) = take(4)
    qkv = TorusGather(wq, wb, ga, gb, take(QKV_SEMS))
    text_sum = SlabSum(text_part, text_rows, take(5))
    attn_sum = SlabSum(tsum_part, text_out, take(5))
    q_s, q_r, k_s, k_r, v_s, v_r, n_s, n_r, d_s, d_r = take(10)
    pair_s, pair_r, far_s, far_r, near_s, near_r = take(6)

    nz = gb.shape[0]
    nx = part.shape[0]
    slab, head = lax.axis_index("slab"), lax.axis_index("head")
    slab_count = lax.axis_size("slab")
    z, y = slab // Y, mod(slab, Y)
    row, column = slab // COLUMN_TILES, mod(slab, COLUMN_TILES)
    above, below = mod(slab + slab_count - COLUMN_TILES, slab_count), mod(slab + COLUMN_TILES, slab_count)
    has_left, has_right = column > 0, column < COLUMN_TILES - 1
    has_above, has_below = row > 0, row < slab_count // COLUMN_TILES - 1
    jump_left, jump_right = has_left & (y == 0), has_right & (y == Y - 1)
    x, core = head // 2, mod(head, 2)
    x_right, x_left, x_far = mod(x + 1, nx), mod(x + nx - 1, nx), mod(x + 2, nx)
    other, right, left = x * 2 + 1 - core, x_right * 2 + core, x_left * 2 + core
    depth, width = wq.shape
    heads = width // HEAD_SIZE
    tokens, model = video.shape
    txt = text.shape[0]
    score_scale = math.log2(math.e) / math.sqrt(HEAD_SIZE)
    steps = nz // 2
    nt = (((1,), (1,)), ((), ()))

    fetches = [
        pltpu.make_async_copy(src, dst, fetch_sem.at[i]) for i, (src, dst) in enumerate(zip(fetched, held))
    ]
    for i in FETCH_ORDER:
        fetches[i].start()

    barrier, peers = hello_slab(z, y, nz)
    greet((), (other, right, left))

    @pl.when(jump_left)
    def _():
        greet((slab - 1,))

    @pl.when(jump_right)
    def _():
        greet((slab + 1,))

    for i in FETCH_ORDER[:4]:
        fetches[i].wait()
    for i, weight in enumerate((wk, wv, wo)):
        wb[i] = weight[...]
    pl.semaphore_wait(barrier, peers + 3 + jump_left.astype(jnp.int32) + jump_right.astype(jnp.int32))
    def normalize_video(i, carry):
        at = pl.ds(pl.multiple_of(i * 16, 16), 16)
        values = video[at, :].astype(f32)
        center = values - jnp.mean(values, axis=-1, keepdims=True)
        normed[at, :] = (center * row_scale(center)).astype(bf16)
        return carry

    blocks = tokens // 16
    early = blocks // 4

    def first_rows():
        fetches[0].wait()
        lax.fori_loop(0, early, normalize_video, 0)

    qkv.start(first_rows)

    span = tweight.shape[0]
    aligned = jnp.minimum(slab * depth // LANES * LANES, model - span)
    aligned = pl.multiple_of(aligned, LANES)
    offset = pl.multiple_of(slab * depth - aligned, 16)
    share = nz // heads

    def fill_text_weights():
        tweight[...] = jnp.zeros_like(tweight)
        for i, weight in enumerate((twq, twk, twv)):
            tweight[pl.ds(offset, depth), i * width : (i + 1) * width] = weight[...]

    def normalize_text(i, carry):
        at = pl.ds(pl.multiple_of(i * 16, 16), 16)
        values = text[at, :].astype(f32)
        mean = jnp.mean(values, axis=-1, keepdims=True)
        scale = row_scale(values - mean)
        columns = text[at, pl.ds(aligned, span)].astype(f32)
        tnormed[at, :] = ((columns - mean) * scale).astype(bf16)
        return carry

    def multiply_text():
        for i in range(3):
            product = jnp.dot(
                tnormed[...], tweight[:, i * width : (i + 1) * width], preferred_element_type=f32
            ).astype(bf16)
            for h in range(heads):
                block = product[:, h * HEAD_SIZE : (h + 1) * HEAD_SIZE]
                text_part[i, h * share : (h + 1) * share] = block.reshape(share, *text_part.shape[2:])

    def finish_text(total):
        gain = jnp.where(y == 0, tqg[...], tkg[...])
        return jnp.where(y == 2, total, total * row_scale(total) * gain)

    for t in range(1, steps + 1):
        qkv.step(t)
        if t == 1:
            for i in FETCH_ORDER[5:]:
                fetches[i].wait()
            fill_text_weights()
            lax.fori_loop(0, txt // 32, normalize_text, 0)
        if t == 2:
            lax.fori_loop(txt // 32, txt // 16, normalize_text, 0)
            multiply_text()
            text_sum.start()
        if t == 4:
            text_sum.along_z()
        if t == 7:
            text_sum.hand_out_z(finish_text)
        if t > 2:
            rest, steps_left = blocks - early, steps - 2
            lax.fori_loop(
                early + (t - 3) * rest // steps_left, early + (t - 2) * rest // steps_left, normalize_video, 0
            )

    qkv.own_b.wait()
    qkv.late_start(0)

    acc[...] = jnp.zeros_like(acc)
    group = 4 if nz % 4 == 0 else nz
    span = group * Y * depth

    def multiply_query(c, carry):
        rows = normed[:, pl.ds(pl.multiple_of(c * span, span), span)]
        acc[:, :width] += jnp.dot(
            rows, ga[pl.ds(c * group, group)].reshape(span, width), preferred_element_type=f32
        )
        return carry

    lax.fori_loop(0, nz // group, multiply_query, 0)
    rows_out = []
    for h in range(heads):
        values = acc[:, h * HEAD_SIZE : (h + 1) * HEAD_SIZE]
        q[0, h] = (values * row_scale(values) * qg[...]).astype(bf16)
        to_below = remote(q.at[0, h], q.at[1, h], q_s.at[0, h], q_r.at[0, h], slab=below)
        to_above = remote(q.at[0, h], q.at[2, h], q_s.at[1, h], q_r.at[1, h], slab=above)
        to_below.start()
        to_above.start()
        rows_out.append((to_below, to_above))

    pair_depth = 2 * Y * depth

    def multiply_rest(i, j):
        at = mod(z // 2 + i + nz // 2 - 2, nz // 2)
        rows = normed[:, pl.ds(pl.multiple_of(at * pair_depth, pair_depth), pair_depth)]
        acc[:, (j + 1) * width : (j + 2) * width] += jnp.dot(
            rows, gb[pl.ds(at * 2, 2), :, j].reshape(pair_depth, width), preferred_element_type=f32
        )

    def multiply_pairs(first, last, j):
        def body(i, carry):
            multiply_rest(i, j)
            return carry

        lax.fori_loop(first, last, body, 0)

    qkv.near_landed()
    multiply_pairs(0, 5, 0)
    multiply_pairs(0, 5, 1)
    qkv.far_landed()
    multiply_pairs(5, nz // 2, 0)

    to_right, to_left = [], []

    def send_sides(block, send, arrived, h):
        right_now = remote(block.at[0, h], block.at[1, h], send.at[0, h], arrived.at[0, h], slab=slab + 1)
        left_now = remote(block.at[0, h], block.at[2, h], send.at[1, h], arrived.at[1, h], slab=slab - 1)
        pl.when(has_right)(right_now.start)
        pl.when(has_left)(left_now.start)
        to_right.append(right_now)
        to_left.append(left_now)

    for h in range(heads):
        values = acc[:, width + h * HEAD_SIZE : width + (h + 1) * HEAD_SIZE]
        k[0, h] = (values * row_scale(values) * kg[...]).astype(bf16)
        if h == 0:
            send_sides(k, k_s, k_r, h)
    multiply_pairs(5, nz // 2, 1)
    for h in range(heads):
        v[0, h] = acc[:, 2 * width + h * HEAD_SIZE : 2 * width + (h + 1) * HEAD_SIZE].T.astype(bf16)
        if h > 0:
            send_sides(k, k_s, k_r, h)
        send_sides(v, v_s, v_r, h)
    text_sum.hand_out_y()
    qkv.late_start(1)

    @pl.when(jnp.logical_not(has_left))
    def _():
        k[1] = jnp.zeros_like(k[1])
        v[1] = jnp.zeros_like(v[1])

    @pl.when(jnp.logical_not(has_right))
    def _():
        k[2] = jnp.zeros_like(k[2])
        v[2] = jnp.zeros_like(v[2])

    def scores(keys, queries):
        return jnp.exp2(lax.dot_general(keys, queries, nt, preferred_element_type=f32) * score_scale)

    def weigh(values, e):
        return jnp.dot(values, e.astype(bf16), preferred_element_type=f32)

    def column_sum(e):
        return jnp.sum(e, axis=0, keepdims=True)

    tsum_part[heads] = jnp.zeros_like(tsum_part[heads])
    for h in range(heads):
        e = scores(k[0, h], q[0, h])
        num[0, h] = weigh(v[0, h], e)
        den[0, h, 0:1] = column_sum(e)

    for h in range(heads):
        for copy in rows_out[h]:
            copy.wait_recv()

        def neighbour(tile, carry, h=h):
            e = scores(k[0, h], q[tile, h])
            num[tile, h] = weigh(v[0, h], e)
            den[tile, h] = jnp.broadcast_to(column_sum(e), den.shape[2:])
            return carry

        lax.fori_loop(1, 3, neighbour, 0)
    qkv.late_relay()

    def has_side(slot):
        return column != (COLUMN_TILES - 1) * (slot - 1)

    def add_side(slot, tile, h):
        reach = jnp.where(has_side(slot), 1.0, 0.0) * window[1, head * heads + h].astype(f32)
        e = scores(k[slot, h], q[tile, h])
        num[tile, h] += weigh(v[slot, h], e) * reach
        den[tile, h, 0:1] += column_sum(e) * reach

    def text_phase():
        live[...] = jnp.broadcast_to(mask[...].astype(f32), live.shape).T
        is_first = jnp.where(slab == 0, 1.0, 0.0)
        text_sum.end()

        def text_head(i, h):
            return text_rows[i, h * share : (h + 1) * share].reshape(txt, HEAD_SIZE)

        text_values = []
        for h in range(heads):
            tq = text_head(0, h)
            text_values.append(text_head(2, h).astype(f32).T.astype(bf16))
            e = scores(k[0, h], tq)
            own = scores(text_head(1, h), tq) * live[...] * is_first
            total = weigh(v[0, h], e) + weigh(text_values[h], own)
            tsum_part[h] = total.reshape(tsum_part.shape[1:])
            tsum_part[heads, 0, h : h + 1] = column_sum(e) + column_sum(own)
        attn_sum.start()

        live_wide = jnp.concatenate([live[...]] * (tokens // txt), axis=1)
        for h in range(heads):
            e = scores(text_head(1, h), q[0, h]) * live_wide
            num[0, h] += weigh(text_values[h], e)
            den[0, h, 0:1] += column_sum(e)

    back = []
    for h in range(heads):

        for i in range(2):
            slot = 1 + mod(i + jump_left.astype(jnp.int32), 2)

            @pl.when(has_side(slot))
            def _():
                for sem, dst in ((k_r, k), (v_r, v)):
                    block = dst.at[slot, h]
                    arrived = sem.at[slot - 1, h]
                    remote(block, block, arrived, arrived, slab=slab + 2 * slot - 3).wait_recv()

            def side(tile, carry, h=h, slot=slot):
                add_side(slot, tile, h)
                return carry

            lax.fori_loop(1, 3, side, 0)
        for tile in (1, 2):
            num_out[tile - 1, h] = num[tile, h].astype(bf16)
        now = [
            remote(num_out.at[0, h], num_in.at[1, h], n_s.at[1, h], n_r.at[1, h], slab=above),
            remote(num_out.at[1, h], num_in.at[0, h], n_s.at[0, h], n_r.at[0, h], slab=below),
            remote(den.at[1, h], den_in.at[1, h], d_s.at[1, h], d_r.at[1, h], slab=above),
            remote(den.at[2, h], den_in.at[0, h], d_s.at[0, h], d_r.at[0, h], slab=below),
        ]
        for copy in now:
            copy.start()
        back.append(now)

    text_phase()

    def own_side(i, carry):
        add_side(1 + i % 2, 0, i // 2)
        return carry

    lax.fori_loop(0, 2 * heads, own_side, 0)
    text_sum.settle()
    for h in range(heads):
        for copy in back[h]:
            copy.wait_recv()
        total, under = num[0, h], den[0, h, 0:1]
        for side_row, exists in ((0, has_above), (1, has_below)):
            reach = jnp.where(exists, 1.0, 0.0) * window[0, head * heads + h].astype(f32)
            total = total + num_in[side_row, h].astype(f32) * reach
            under = under + den_in[side_row, h, 0:1] * reach
        attn[:, h * HEAD_SIZE : (h + 1) * HEAD_SIZE] = (total / under).T.astype(bf16)

    qkv.late_end()
    rows = tokens // nx
    halves = part.shape[2]
    pairs = []

    def send_pair(xx):
        mine = attn[pl.ds(pl.multiple_of(xx * rows, 16), rows), :]
        for half in range(halves):
            weight = gb[half * nz // halves : (half + 1) * nz // halves, :, 2].reshape(model // halves, width)
            product = lax.dot_general(mine, weight, nt, preferred_element_type=f32).astype(bf16)
            for c in range(2):
                part[xx, c, half] = product[c * rows // 2 : (c + 1) * rows // 2]
            pairs.append(
                remote(part.at[xx, 1 - core, half], pair.at[xx, half], pair_s.at[xx, half], pair_r.at[xx, half],
                       head=other)
            )
            pairs[-1].start()

    def pair_sum(xx, half):
        block = pair.at[xx, half]
        remote(block, block, pair_s.at[xx, half], pair_r.at[xx, half], head=other).wait_recv()
        pair[xx, half] = (pair[xx, half].astype(f32) + part[xx, core, half].astype(f32)).astype(bf16)

    fars = [
        remote(pair.at[x_far, 0], far.at[0], far_s.at[0], far_r.at[0], head=right),
        remote(pair.at[x_far, 1], far.at[1], far_s.at[1], far_r.at[1], head=left),
    ]
    send_pair(x_far)
    send_pair(x_right)
    attn_sum.along_z()
    for half in range(halves):
        pair_sum(x_far, half)
        fars[half].start()
    send_pair(x_left)
    nears = [
        remote(pair.at[x_right, 1], near.at[0, 1], near_s.at[0, 1], near_r.at[0, 1], head=right),
        remote(pair.at[x_left, 0], near.at[1, 0], near_s.at[1, 0], near_r.at[1, 0], head=left),
        remote(pair.at[x_right, 0], near.at[0, 0], near_s.at[0, 0], near_r.at[0, 0], head=right),
        remote(pair.at[x_left, 1], near.at[1, 1], near_s.at[1, 1], near_r.at[1, 1], head=left),
    ]
    pair_sum(x_right, 1)
    nears[0].start()
    pair_sum(x_left, 0)
    nears[1].start()
    pair_sum(x_right, 0)
    pair_sum(x_left, 1)
    attn_sum.hand_out_z(lambda total: total)
    fars[0].wait_recv()
    pair[x_right, 0] = (pair[x_right, 0].astype(f32) + far[0].astype(f32)).astype(bf16)
    nears[2].start()
    fars[1].wait_recv()
    pair[x_left, 1] = (pair[x_left, 1].astype(f32) + far[1].astype(f32)).astype(bf16)
    nears[3].start()
    send_pair(x)
    qkv.settle()
    attn_sum.hand_out_y()
    for copy in (*sum(rows_out, ()), *sum(back, []), *pairs):
        copy.wait_send()

    @pl.when(has_right)
    def _():
        for copy in to_right:
            copy.wait_send()

    @pl.when(has_left)
    def _():
        for copy in to_left:
            copy.wait_send()

    for half in range(halves):
        pair_sum(x, half)
    for copy in nears:
        copy.wait_recv()
    for half in range(halves):
        at = half * model // halves
        out[:, at : at + model // halves] = (
            pair[x, half].astype(f32) + near[0, half].astype(f32) + near[1, half].astype(f32)
        ).astype(bf16)

    attn_sum.end()
    for h in range(heads):
        total = text_out[h].reshape(HEAD_SIZE, txt) / text_out[heads, 0, h : h + 1]
        text_final[:, h * HEAD_SIZE : (h + 1) * HEAD_SIZE] = total.T.astype(bf16)
    attn_sum.settle()
    for copy in (*fars, *nears):
        copy.wait_send()


def run_whole(slab_count, head_count, operands):
    video, text, wq = operands[0], operands[1], operands[2]
    depth, width = wq.shape
    tokens, model = video.shape
    txt = text.shape[0]
    heads = width // HEAD_SIZE
    nz, nx = slab_count // Y, head_count // 2
    rows = tokens // head_count
    bf16, f32 = jnp.bfloat16, jnp.float32
    text_block = jax.ShapeDtypeStruct((3, nz, txt * heads // nz, HEAD_SIZE), bf16)
    sum_block = jax.ShapeDtypeStruct((heads + 1, nz, HEAD_SIZE // nz, txt), f32)
    half = model // 2
    vmem = pl.BlockSpec(memory_space=VMEM)
    return pl.pallas_call(
        whole_kernel,
        out_shape=(
            jax.ShapeDtypeStruct((rows, model), bf16),
            jax.ShapeDtypeStruct((txt, width), bf16),
        ),
        in_specs=[pl.BlockSpec(memory_space=pltpu.HBM)] * OPERANDS,
        out_specs=(vmem, vmem),
        scratch_shapes=[
            *(VMEM(a.shape, a.dtype) for a in operands[:-1]),
            pltpu.SMEM(operands[-1].shape, operands[-1].dtype),
            DMA((OPERANDS,)),
            VMEM((3, depth, width), bf16),
            VMEM((nz, Y, depth, width), bf16),
            VMEM((nz, Y, 3, depth, width), bf16),
            VMEM((tokens, model), bf16),
            VMEM((txt, 2 * LANES), bf16),
            VMEM((2 * LANES, 3 * width), bf16),
            VMEM(text_block.shape, bf16),
            VMEM(text_block.shape, bf16),
            VMEM((tokens, 3 * width), f32),
            VMEM((3, heads, tokens, HEAD_SIZE), bf16),
            VMEM((3, heads, tokens, HEAD_SIZE), bf16),
            VMEM((3, heads, HEAD_SIZE, tokens), bf16),
            VMEM((3, heads, HEAD_SIZE, tokens), f32),
            VMEM((3, heads, 8, tokens), f32),
            VMEM((2, heads, HEAD_SIZE, tokens), bf16),
            VMEM((2, heads, HEAD_SIZE, tokens), bf16),
            VMEM((2, heads, 8, tokens), f32),
            VMEM((tokens, width), bf16),
            VMEM((txt, txt), f32),
            VMEM(sum_block.shape, f32),
            VMEM(sum_block.shape, f32),
            VMEM((nx, 2, 2, rows, half), bf16),
            VMEM((nx, 2, rows, half), bf16),
            VMEM((2, rows, half), bf16),
            VMEM((2, 2, rows, half), bf16),
            *TorusGather.scratch(nz),
            *SlabSum.scratch(text_block),
            *SlabSum.scratch(sum_block),
            *[DMA((2, heads))] * 10,
            DMA((nx, 2)), DMA((nx, 2)), DMA((2,)), DMA((2,)), DMA((2, 2)), DMA((2, 2)),
        ],
        compiler_params=pltpu.CompilerParams(
            collective_id=0, has_side_effects=True, vmem_limit_bytes=32 * MIB
        ),
        name="whole",
    )(*(pltpu.with_memory_space_constraint(a, pltpu.HBM) for a in operands))


def on_device(
    video_token_state,
    text_tokens,
    text_mask,
    head_window,
    video_query_weight,
    video_key_weight,
    video_value_weight,
    wout_video,
    wquery_text,
    wkey_text,
    wvalue_text,
    video_query_gain,
    video_key_gain,
    qgain_text,
    kgain_text,
):
    operands = (
        video_token_state, text_tokens,
        video_query_weight, video_key_weight, video_value_weight, wout_video.T,
        wquery_text, wkey_text, wvalue_text,
        *(row.reshape(1, -1) for row in (video_query_gain, video_key_gain, qgain_text, kgain_text, text_mask)),
        head_window.T,
    )
    return run_whole(lax.axis_size("slab"), lax.axis_size("head"), operands)


def solution(mesh):
    return jax.shard_map(
        on_device,
        mesh=mesh,
        in_specs=(
            P("slab", None),
            P(),
            P(),
            P(),
            P("slab", "head"),
            P("slab", "head"),
            P("slab", "head"),
            P("head", "slab"),
            P("slab", "head"),
            P("slab", "head"),
            P("slab", "head"),
            P(),
            P(),
            P(),
            P(),
        ),
        out_specs=(P(("slab", "head"), None), P(None, "head")),
        check_vma=False,
    )
```
